512 devices in a mesh: sub: 64 (over z, y), own: 8 (over x, core).
Axes of the slice: x: 4, y: 8, z: 8, core: 2. Of those that a mesh axis runs over, the one named last changes fastest.
Arguments:
- deflation: float32 [30, 4096, 2048], P(None, 'sub', 'own'), may hold values from -164 to 164
- permeability_base: float32 [4096, 2048], P('sub', 'own'), may hold values from 0.5 to 2
- design_mask: int32 [4096, 2048], P('sub', 'own'), may hold values 0 or 1
- storage: float32 [4096, 2048], P('sub', 'own'), may hold values from 0.0002 to 0.0008
- right_side: float32 [4096, 2048], P('sub', 'own'), may hold values from -4.1 to 4.9
Outputs:
- coarse_coeffs: float32 [64, 30], P('sub')
- new_residual: float32 [4096, 2048], P('sub', 'own')
The draws below stay inside these ranges and needn't reach their ends.
All inputs are finite; a program needn't handle non-finite values. No bound on the sum of `design_mask` on one device may be relied on, other than what follows from the above.
Results may differ from the reference program's by a relative error of at most 0.00045.
Values sent between devices are 32-bit elements; how exact they have to be, the bound alone decides.
No kernel may reach another device: no remote copies, remote signals or barrier semaphores. Data moves between devices by JAX's collectives and lax.ppermute only.
A program may use at most 128 MiB of HBM per device.

```python
import math
import jax
import jax.numpy as jnp
from jax import lax

NV = 30
CX = 64
SUBS = 64
NX = 4096
NY = 2048


def draw_deflation(key, part):
    key = jax.random.fold_in(key, 11)
    amp_key, mix_key, sign_key, rough_key = jax.random.split(key, 4)
    subdomains = NX // CX
    amplitude = jnp.exp(jax.random.uniform(amp_key, (NV, subdomains), jnp.float32, math.log(30.0), math.log(100.0)))
    mixing = jax.random.uniform(mix_key, (NV, subdomains), jnp.float32, 0.3, 0.6)
    polarity = jnp.where(jax.random.bernoulli(sign_key, 0.5, (NV, subdomains)), 1.0, -1.0).astype(jnp.float32)
    amplitude_rows = jnp.repeat(amplitude * polarity, CX, axis=1)
    mixing_rows = jnp.repeat(mixing, CX, axis=1)
    centres = (jnp.arange(NY, dtype=jnp.float32) + 0.5) * (math.pi / NY)
    orders = jnp.arange(NV, dtype=jnp.float32)
    lower_modes = jnp.cos(orders[:, None] * centres[None, :])
    upper_modes = jnp.cos((orders[:, None] + 1.0) * centres[None, :])
    roughness = 1.0 + 0.004 * jax.random.uniform(rough_key, (NV, NX, NY), jnp.float32, -1.0, 1.0)
    shaped = lower_modes[:, None, :] + mixing_rows[:, :, None] * upper_modes[:, None, :]
    return (amplitude_rows[:, :, None] * shaped * roughness).astype(jnp.float32)


def draw_right_side(key, part):
    key = jax.random.fold_in(key, 23)
    noise = jnp.clip(jax.random.normal(key, (NX, NY), jnp.float32), -4.5, 4.5)
    level = 0.4
    return (noise + level).astype(jnp.float32)


def touch_ends(result, own_key, least, top_value):
    dims = result.shape
    index_at = [jax.random.randint(jax.random.fold_in(own_key, axis), (), 0, dims[axis]) for axis in range(len(dims))]
    result = result.at[tuple(index_at)].set(least)
    longest = dims.index(max(dims))
    index_at[longest] = (index_at[longest] + 1) % dims[longest]
    return result.at[tuple(index_at)].set(top_value)


def levels(key, extent, cuts, least, high):
    def one(position, parts):
        steps = jax.random.uniform(jax.random.fold_in(jax.random.fold_in(key, 6), position), (parts,), jnp.float32, least / len(cuts), high / len(cuts))
        return jnp.repeat(jnp.exp(steps), extent[position] // parts).reshape((-1,) + (1,) * (len(extent) - position - 1))

    factor_of = one(*cuts[0])
    for cut in cuts[1:]:
        factor_of = factor_of * one(*cut)
    return factor_of


def setup_inputs(seed: int = 0) -> dict:
    seeds = jax.random.split(jax.random.key(seed), 6)
    return {
        "deflation": draw_deflation(jax.random.fold_in(seeds[5], 71), 0),
        "permeability_base": jnp.clip(jnp.exp(math.log(2.0) - 1.3862944 * jax.random.uniform(seeds[1], (NX, NY), jnp.float32) ** levels(seeds[1], (NX, NY), ((0, 64), (1, 8)), -0.2, 0.2)), 0.5, 2.0),
        "design_mask": touch_ends((jax.random.randint(seeds[2], (NX, NY), 0, 50) < 49).astype(jnp.int32), jax.random.fold_in(seeds[2], 1), 0, 1),
        "storage": jnp.clip(jnp.exp(math.log(0.0008) - 1.3862944 * jax.random.uniform(seeds[3], (NX, NY), jnp.float32) ** levels(seeds[3], (NX, NY), ((0, 64), (1, 8)), -0.2, 0.2)), 0.0002, 0.0008),
        "right_side": draw_right_side(jax.random.fold_in(seeds[5], 71), 0),
    }


LOG_CONTRAST = math.log(1000.0)
precise = lax.Precision.HIGHEST

def transmit(centre, beside):
    return 2.0 * centre * beside / (centre + beside)

def chain_solve(diag_all, low_all, rhs_all):
    order_n = diag_all.shape[1]
    unit_matrix = jnp.eye(order_n, dtype=diag_all.dtype)

    def forward(state_in, step_in):
        prev_factor, prev_value = state_in
        block, cross, rhs_row = step_in
        link = jax.scipy.linalg.solve_triangular(prev_factor, cross.T, lower=True).T
        schur = block - jnp.dot(link, link.T, precision=precise)
        schur = 0.5 * (schur + schur.T)
        factor = jnp.linalg.cholesky(schur)
        value = jax.scipy.linalg.solve_triangular(factor, rhs_row - jnp.dot(link, prev_value, precision=precise), lower=True)
        return ((factor, value), (factor, link, value))
    start_state = (unit_matrix, jnp.zeros((order_n,), diag_all.dtype))
    _, (factors, links, values) = lax.scan(forward, start_state, (diag_all, low_all, rhs_all))
    next_links = jnp.concatenate([links[1:], jnp.zeros_like(links[:1])], 0)

    def backward(state_in, step_in):
        factor, link_next, value = step_in
        coeff = jax.scipy.linalg.solve_triangular(factor, value - jnp.dot(link_next.T, state_in, precision=precise), lower=True, trans=1)
        return (coeff, coeff)
    _, coeffs = lax.scan(backward, jnp.zeros((order_n,), diag_all.dtype), (factors, next_links, values), reverse=True)
    return coeffs

def reference(deflation, permeability_base, design_mask, storage, right_side):
    permeability = permeability_base * jnp.exp((design_mask.astype(jnp.float32) - 1.0) * LOG_CONTRAST)
    kpadded = jnp.pad(permeability, 1)
    t_east = transmit(permeability, kpadded[2:, 1:-1])
    t_west = transmit(permeability, kpadded[:-2, 1:-1])
    t_north = transmit(permeability, kpadded[1:-1, 2:])
    t_south = transmit(permeability, kpadded[1:-1, :-2])
    indices = jnp.arange(SUBS, dtype=jnp.int32)

    def blocks(slab_index):
        start = slab_index * CX
        zslab = lax.dynamic_slice_in_dim(deflation, start, CX, 1)
        te_slab = lax.dynamic_slice_in_dim(t_east, start, CX, 0)
        tw_slab = lax.dynamic_slice_in_dim(t_west, start, CX, 0)
        tn_slab = lax.dynamic_slice_in_dim(t_north, start, CX, 0)
        ts_slab = lax.dynamic_slice_in_dim(t_south, start, CX, 0)
        st_slab = lax.dynamic_slice_in_dim(storage, start, CX, 0)
        rhs_slab = lax.dynamic_slice_in_dim(right_side, start, CX, 0)
        zpadded = jnp.pad(zslab, ((0, 0), (1, 1), (1, 1)))
        applied = st_slab * zslab + te_slab * (zslab - zpadded[:, 2:, 1:-1]) + tw_slab * (zslab - zpadded[:, :-2, 1:-1])
        applied = applied + tn_slab * (zslab - zpadded[:, 1:-1, 2:]) + ts_slab * (zslab - zpadded[:, 1:-1, :-2])
        flat = zslab.reshape(NV, -1)
        diag_block = jnp.dot(flat, applied.reshape(NV, -1).T, precision=precise)
        prev_row = lax.dynamic_index_in_dim(deflation, jnp.maximum(start - 1, 0), 1, keepdims=False)
        prev_row = prev_row * (slab_index > 0).astype(jnp.float32)
        low_block = -jnp.dot(zslab[:, 0, :] * tw_slab[0], prev_row.T, precision=precise)
        rhs_block = jnp.dot(flat, rhs_slab.reshape(-1), precision=precise)
        return (diag_block, low_block, rhs_block)
    diag_all, low_all, rhs_all = lax.map(blocks, indices)
    coeffs = chain_solve(diag_all, low_all, rhs_all)

    def spread(slab_index):
        zslab = lax.dynamic_slice_in_dim(deflation, slab_index * CX, CX, 1)
        mine = lax.dynamic_index_in_dim(coeffs, slab_index, 0, keepdims=False)
        return jnp.dot(mine, zslab.reshape(NV, -1), precision=precise).reshape(CX, NY)
    field = lax.map(spread, indices).reshape(NX, NY)
    fpadded = jnp.pad(field, 1)
    applied_field = storage * field + t_east * (field - fpadded[2:, 1:-1]) + t_west * (field - fpadded[:-2, 1:-1])
    applied_field = applied_field + t_north * (field - fpadded[1:-1, 2:]) + t_south * (field - fpadded[1:-1, :-2])
    return (coeffs, right_side - applied_field)
```

```python
import functools
import math

import jax
import jax.numpy as jnp
from jax import lax
from jax.experimental import pallas as pl
from jax.experimental.pallas import tpu as pltpu
from jax.sharding import PartitionSpec as P

LOG_CONTRAST = math.log(1000.0)
precise = lax.Precision.HIGHEST


def padded_2(value, sides, width):
    for axis, dim in sides:
        devices, length = (lax.axis_size(axis), value.shape[dim])
        up = [(i, (i + 1) % devices) for i in range(devices - 1)]
        down = [(j, i) for i, j in up]
        last = lax.slice_in_dim(value, length - width, length, axis=dim)
        leading = lax.slice_in_dim(value, 0, width, axis=dim)
        before = lax.ppermute(last, axis, up)
        after = lax.ppermute(leading, axis, down)
        value = jnp.concatenate([before, value, after], axis=dim)
    return value


def transmit(centre, beside):
    return 2.0 * centre * beside / (centre + beside)


def shared_with_all(value, axis):
    copies = jnp.broadcast_to(value[None], (lax.axis_size(axis),) + value.shape)
    return lax.all_to_all(copies, axis, 0, 0)


NV = 30
NT = (((1,), (1,)), ((), ()))


def eliminate(mats):
    rows = lax.broadcasted_iota(jnp.int32, (32, 128), 0)
    for k in range(0, NV, 2):
        first = rows == k
        second = rows == k + 1
        out = []
        for a in mats:
            r1, r2 = a[k : k + 1], a[k + 1 : k + 2]
            c1, c2 = a[:, k : k + 1], a[:, k + 1 : k + 2]
            p, q, s = r1[:, k : k + 1], r1[:, k + 1 : k + 2], r2[:, k + 1 : k + 2]
            inv = 1.0 / (p * s - q * q)
            n1 = (s * inv) * r1 - (q * inv) * r2
            n2 = (p * inv) * r2 - (q * inv) * r1
            new = a - c1 * n1 - c2 * n2
            new = jnp.where(first, n1, jnp.where(second, n2, new))
            out.append(new)
        mats = out
    return mats


def level_rhs(x_left, x_right):
    lanes = lax.broadcasted_iota(jnp.int32, (32, 128), 1)
    low = lanes < NV
    xa = jnp.where(low, pltpu.roll(x_left, 64, 1), jnp.where(lanes < 64, x_left, 0.0))
    blank = jnp.zeros((32, 128), jnp.float32)
    if x_right is None:
        xb = blank
    else:
        keep = (lanes == NV) | (lanes >= 64)
        xb = jnp.where(low, pltpu.roll(x_right, 96, 1), jnp.where(keep, x_right, 0.0))
    return jnp.concatenate([blank, xa, xb, blank], 0)


def solve_kernel(count, group, pos_ref, g_ref, out_ref, aug, xs):
    lanes = lax.broadcasted_iota(jnp.int32, (32, 128), 1)
    def unpack(m):
        t = g_ref[m]
        return jnp.concatenate([t, pltpu.roll(t, 64, 1)], 0)

    nxt = None
    for m in reversed(range(count)):
        q = jnp.where(lanes < 64, unpack(m), 0.0)
        if nxt is None:
            aug[m] = q
        else:
            lt = jnp.transpose(nxt[:, 32:64])
            up = jnp.concatenate([jnp.zeros((32, 64), jnp.float32), lt, jnp.zeros((32, 32), jnp.float32)], 1)
            aug[m] = q + up
        nxt = q
    n = count
    base = 0
    offsets = []
    while n > 1:
        half = n // 2
        offsets.append(base)
        step = min(group, half)

        def eliminate_group(t, _, base=base, step=step):
            mats = [aug[2 * (t * step + i)] for i in range(step)]
            for i, x in enumerate(eliminate(mats)):
                xs[base + t * step + i] = x
            return 0

        if half == step:
            eliminate_group(0, 0)
        else:
            lax.fori_loop(0, half // step, eliminate_group, 0)
        keep = lanes < NV + 1
        for j in range(half):
            a = aug[2 * j + 1]
            rhs = level_rhs(xs[base + j], xs[base + j + 1] if j + 1 < half else None)
            aug[j] = jnp.where(keep, a, 0.0) - jnp.dot(a, rhs, precision=precise, preferred_element_type=jnp.float32)
        base += half
        n = half
    (last,) = eliminate([aug[0]])
    row_id = lax.broadcasted_iota(jnp.int32, (8, 128), 0)
    lane8 = lax.broadcasted_iota(jnp.int32, (8, 128), 1)
    unit = (lane8 == NV).astype(jnp.float32)

    def in_row(v, x):
        return lax.dot_general(v, x, NT, precision=precise, preferred_element_type=jnp.float32)

    pos = pos_ref[0]
    zero = jnp.zeros((8, 128), jnp.float32)
    root = jnp.concatenate([in_row(unit, last), jnp.zeros((8, 96), jnp.float32)], 1)
    window = [zero, root, zero]
    for depth in reversed(range(len(offsets))):
        half = count >> (depth + 1)
        here = pos >> depth
        c = here >> 1
        if half > 1:
            start = jnp.minimum(c, half - 2)
            x2 = xs[pl.ds(offsets[depth] + start, 2)].reshape(64, 128)
            va = unit - pltpu.roll(window[0], 32, 1) - pltpu.roll(window[1], 64, 1)
            vb = unit - pltpu.roll(window[1], 32, 1) - pltpu.roll(window[2], 64, 1)
            v = jnp.where(row_id == 0, va, vb)
            y = in_row(v, x2)
            y = jnp.concatenate([y, jnp.zeros((8, 64), jnp.float32)], 1)
            y = jnp.where(lane8 < 64, y, 0.0)
            lo = jnp.where(lane8 < 32, y, 0.0)
            hi = jnp.where(lane8 < 32, pltpu.roll(y, 64 + 32, 1), 0.0)
            ea = jnp.where(c == start, lo[0:1], hi[0:1])
            eb = jnp.where(c == start, hi[1:2], zero[1:2])
        else:
            va = unit - pltpu.roll(window[1], 64, 1)
            y = jnp.concatenate([in_row(va, xs[offsets[depth]]), jnp.zeros((8, 96), jnp.float32)], 1)
            ea, eb = y[0:1], zero[0:1]
        ea = jnp.broadcast_to(ea, (8, 128))
        eb = jnp.broadcast_to(eb, (8, 128))
        odd = (here & 1) == 1
        window = [
            jnp.where(odd, ea, window[0]),
            jnp.where(odd, window[1], ea),
            jnp.where(odd, eb, window[1]),
        ]
    out_ref[...] = jnp.where(row_id == 0, window[0], jnp.where(row_id == 1, window[1], window[2]))


def solve(g, pos, group=8):
    count = g.shape[0]
    return pl.pallas_call(
        functools.partial(solve_kernel, count, group),
        out_shape=jax.ShapeDtypeStruct((8, 128), jnp.float32),
        in_specs=[pl.BlockSpec(memory_space=pltpu.SMEM), pl.BlockSpec(memory_space=pltpu.VMEM)],
        out_specs=pl.BlockSpec(memory_space=pltpu.VMEM),
        scratch_shapes=[pltpu.VMEM((count, 32, 128), jnp.float32), pltpu.VMEM((count, 32, 128), jnp.float32)],
    )(pos, g)


def per_device(deflation, permeability_base, design_mask, storage, right_side):
    vectors = deflation.shape[0]
    permeability = permeability_base * jnp.exp(
        (design_mask.astype(jnp.float32) - 1.0) * LOG_CONTRAST
    )
    stacked = jnp.concatenate([deflation, permeability[None]], 0)
    padded = padded_2(stacked, (("sub", 1), ("own", 2)), 1)
    zpadded = padded[:vectors]
    kpadded = padded[vectors]
    t_east = transmit(permeability, kpadded[2:, 1:-1])
    t_west = transmit(permeability, kpadded[:-2, 1:-1])
    t_north = transmit(permeability, kpadded[1:-1, 2:])
    t_south = transmit(permeability, kpadded[1:-1, :-2])
    isolated = jnp.pad(zpadded[:, 1:-1, :], ((0, 0), (1, 1), (0, 0)))
    applied = (
        storage * deflation
        + t_east * (deflation - isolated[:, 2:, 1:-1])
        + t_west * (deflation - isolated[:, :-2, 1:-1])
    )
    applied = (
        applied
        + t_north * (deflation - isolated[:, 1:-1, 2:])
        + t_south * (deflation - isolated[:, 1:-1, :-2])
    )
    flat = deflation.reshape(vectors, -1)
    diag_part = jnp.dot(flat, applied.reshape(vectors, -1).T, precision=precise)
    low_part = -jnp.dot(deflation[:, 0, :] * t_west[0], zpadded[:, 0, 1:-1].T, precision=precise)
    rhs_part = jnp.dot(flat, right_side.reshape(-1), precision=precise)
    tile = jnp.zeros((32, 64), jnp.float32)
    tile = tile.at[:vectors, :vectors].set(diag_part)
    tile = tile.at[:vectors, vectors].set(rhs_part)
    tile = tile.at[:vectors, 32 : 32 + vectors].set(low_part)
    part = jnp.concatenate([tile[:16], tile[16:]], 1)
    summed = shared_with_all(part, "own").sum(0)
    gathered = shared_with_all(summed, "sub")
    position = lax.axis_index("sub").astype(jnp.int32)
    window = solve(gathered, position[None])[:3, :vectors]
    mine = window[1]
    middle = jnp.dot(mine, zpadded[:, 1:-1, :].reshape(vectors, -1), precision=precise)
    middle = middle.reshape(zpadded.shape[1] - 2, zpadded.shape[2])
    above = jnp.dot(window[0], zpadded[:, 0, :], precision=precise)
    below = jnp.dot(window[2], zpadded[:, -1, :], precision=precise)
    fpadded = jnp.concatenate([above[None], middle, below[None]], 0)
    field = fpadded[1:-1, 1:-1]
    applied_field = (
        storage * field
        + t_east * (field - fpadded[2:, 1:-1])
        + t_west * (field - fpadded[:-2, 1:-1])
    )
    applied_field = (
        applied_field
        + t_north * (field - fpadded[1:-1, 2:])
        + t_south * (field - fpadded[1:-1, :-2])
    )
    return (mine[None], right_side - applied_field)


def solution(mesh):
    placed = (
        P(None, "sub", "own"),
        P("sub", "own"),
        P("sub", "own"),
        P("sub", "own"),
        P("sub", "own"),
    )
    return jax.shard_map(
        per_device,
        mesh=mesh,
        in_specs=placed,
        out_specs=(P("sub", None), P("sub", "own")),
        check_vma=False,
    )
```

```python
import functools
import math

import jax
import jax.numpy as jnp
from jax import lax
from jax.experimental import pallas as pl
from jax.experimental.pallas import tpu as pltpu
from jax.sharding import PartitionSpec as P

LOG_CONTRAST = math.log(1000.0)
precise = lax.Precision.HIGHEST


def padded_2(value, sides, width):
    for axis, dim in sides:
        devices, length = (lax.axis_size(axis), value.shape[dim])
        up = [(i, (i + 1) % devices) for i in range(devices - 1)]
        down = [(j, i) for i, j in up]
        last = lax.slice_in_dim(value, length - width, length, axis=dim)
        leading = lax.slice_in_dim(value, 0, width, axis=dim)
        before = lax.ppermute(last, axis, up)
        after = lax.ppermute(leading, axis, down)
        value = jnp.concatenate([before, value, after], axis=dim)
    return value


def transmit(centre, beside):
    return 2.0 * centre * beside / (centre + beside)


def shared_with_all(value, axis):
    copies = jnp.broadcast_to(value[None], (lax.axis_size(axis),) + value.shape)
    return lax.all_to_all(copies, axis, 0, 0)


NV = 30
NT = (((1,), (1,)), ((), ()))


def reciprocal(x):
    r = pl.reciprocal(x, approx=True)
    r = r * (2.0 - x * r)
    return r * (2.0 - x * r)


def small_inverse(p):
    a00, a01, a11 = p[0, 0], p[0, 1], p[1, 1]
    b02, b03, b12, b13 = p[0, 2], p[0, 3], p[1, 2], p[1, 3]
    ia = reciprocal(a00 * a11 - a01 * a01)
    h00, h01, h11 = a11 * ia, a01 * ia, a00 * ia
    w02, w03 = h00 * b02 - h01 * b12, h00 * b03 - h01 * b13
    w12, w13 = h11 * b12 - h01 * b02, h11 * b13 - h01 * b03
    s22 = p[2, 2] - (b02 * w02 + b12 * w12)
    s23 = p[2, 3] - (b02 * w03 + b12 * w13)
    s33 = p[3, 3] - (b03 * w03 + b13 * w13)
    iz = reciprocal(s22 * s33 - s23 * s23)
    i22, i23, i33 = s33 * iz, -(s23 * iz), s22 * iz
    i02, i03 = -(w02 * i22 + w03 * i23), -(w02 * i23 + w03 * i33)
    i12, i13 = -(w12 * i22 + w13 * i23), -(w12 * i23 + w13 * i33)
    i00 = h00 - (w02 * i02 + w03 * i03)
    i01 = -h01 - (w02 * i12 + w03 * i13)
    i11 = h11 - (w12 * i12 + w13 * i13)
    return [[i00, i01, i02, i03], [i01, i11, i12, i13], [i02, i12, i22, i23], [i03, i13, i23, i33]]


def take(x, index):
    return jnp.take_along_axis(x, index, axis=1)


def invert_packed(arrays):
    lanes = lax.broadcasted_iota(jnp.int32, (8, 128), 1)
    rows = lax.broadcasted_iota(jnp.int32, (8, 128), 0)
    start, inner = lanes & ~31, lanes & 31
    for k in range(0, 32, 4):
        index = [start + (k + b) for b in range(4)]
        inside = (inner >= k) & (inner < k + 4)
        tile = k // 8
        out = []
        for a in arrays:
            tiles = [a[8 * t : 8 * t + 8] for t in range(4)]
            r = [jnp.broadcast_to(a[k + b : k + b + 1], (8, 128)) for b in range(4)]
            p = {(i, j): take(r[i], index[j]) for i in range(4) for j in range(i, 4)}
            inv = small_inverse(p)
            rhat = [jnp.where(inside, (inner == k + b).astype(jnp.float32), r[b]) for b in range(4)]
            new_rows = [
                (inv[i][0] * rhat[0] + inv[i][1] * rhat[1]) + (inv[i][2] * rhat[2] + inv[i][3] * rhat[3])
                for i in range(4)
            ]
            fresh = []
            for t in range(4):
                c = [take(tiles[t], index[b]) for b in range(4)]
                v = jnp.where(inside, 0.0, tiles[t])
                v = v - ((c[0] * new_rows[0] + c[1] * new_rows[1]) + (c[2] * new_rows[2] + c[3] * new_rows[3]))
                if t == tile:
                    for b in range(4):
                        v = jnp.where(rows == (k + b) % 8, new_rows[b], v)
                fresh.append(v)
            out.append(jnp.concatenate(fresh, 0))
        arrays = out
    return arrays


def solve_kernel(count, group, pos_ref, g_ref, out_ref, aug, xa, xb):
    lanes = lax.broadcasted_iota(jnp.int32, (32, 128), 1)
    rows = lax.broadcasted_iota(jnp.int32, (32, 128), 0)
    low = lanes < NV
    unit_pad = ((lanes == rows) & (rows >= NV)).astype(jnp.float32)
    unit_full = (lanes == rows).astype(jnp.float32)
    blank = jnp.zeros((32, 128), jnp.float32)

    nxt = None
    for m in reversed(range(count)):
        t = g_ref[m]
        q = jnp.where(lanes < 64, jnp.concatenate([t, pltpu.roll(t, 64, 1)], 0), 0.0)
        if nxt is None:
            aug[m] = q
        else:
            lt = jnp.transpose(nxt[:, 32:64])
            up = jnp.concatenate([jnp.zeros((32, 64), jnp.float32), lt, jnp.zeros((32, 32), jnp.float32)], 1)
            aug[m] = q + up
        nxt = q

    def invert_four(blocks):
        total = None
        for g in range(4):
            d = unit_full if blocks[g] is None else jnp.where(low, blocks[g], unit_pad)
            d = d if g == 0 else pltpu.roll(d, 32 * g, 1)
            total = d if total is None else total + d
        return total

    def spread(inverse, g, b):
        zeros = jnp.zeros_like(b)
        rhs = jnp.concatenate([zeros] * g + [b] + [zeros] * (3 - g), 0)
        return jnp.dot(inverse, rhs, precision=precise, preferred_element_type=jnp.float32)

    def arranged(a):
        ba = jnp.where(low, pltpu.roll(a, 64, 1), jnp.where(lanes < 64, a, 0.0))
        bb = jnp.where(low, pltpu.roll(a, 96, 1), jnp.where((lanes == NV) | (lanes >= 64), a, 0.0))
        return jnp.concatenate([ba, bb], 1)

    n = count
    base = 0
    offsets = []
    while n > 1:
        half = n // 2
        offsets.append(base)
        packs = (half + 3) // 4
        step = min(group, packs)

        def eliminate_group(t, _, base=base, step=step, half=half):
            sets = []
            for s in range(step):
                first = (t * step + s) * 4
                sets.append([aug[2 * (first + g)] if g < half else None for g in range(4)])
            inverses = invert_packed([invert_four(b) for b in sets])
            for s in range(step):
                first = (t * step + s) * 4
                for g in range(min(4, half)):
                    x = spread(inverses[s], g, arranged(sets[s][g]))
                    xa[base + first + g] = x[:, :128]
                    xb[base + first + g] = x[:, 128:]
            return 0

        if packs == step:
            eliminate_group(0, 0)
        else:
            lax.fori_loop(0, packs // step, eliminate_group, 0)
        keep = lanes < NV + 1
        for j in range(half):
            a = aug[2 * j + 1]
            right = xb[base + j + 1] if j + 1 < half else blank
            rhs = jnp.concatenate([blank, xa[base + j], right, blank], 0)
            aug[j] = jnp.where(keep, a, 0.0) - jnp.dot(a, rhs, precision=precise, preferred_element_type=jnp.float32)
        base += half
        n = half
    last = aug[0]
    (inverse,) = invert_packed([invert_four([last, None, None, None])])
    last = spread(inverse, 0, jnp.where(lanes == NV, last, 0.0))
    row_id = lax.broadcasted_iota(jnp.int32, (8, 128), 0)
    lane8 = lax.broadcasted_iota(jnp.int32, (8, 128), 1)
    unit = (lane8 == NV).astype(jnp.float32)

    def in_row(v, x):
        return lax.dot_general(v, x, NT, precision=precise, preferred_element_type=jnp.float32)

    pos = pos_ref[0]
    zero = jnp.zeros((8, 128), jnp.float32)
    root = jnp.concatenate([in_row(unit, last), jnp.zeros((8, 96), jnp.float32)], 1)
    window = [zero, root, zero]
    for depth in reversed(range(len(offsets))):
        half = count >> (depth + 1)
        here = pos >> depth
        c = here >> 1
        if half > 1:
            start = jnp.minimum(c, half - 2)
            x2 = xa[pl.ds(offsets[depth] + start, 2)].reshape(64, 128)
            va = unit - pltpu.roll(window[0], 32, 1) - window[1]
            vb = unit - pltpu.roll(window[1], 32, 1) - window[2]
            v = jnp.where(row_id == 0, va, vb)
            y = in_row(v, x2)
            y = jnp.concatenate([y, jnp.zeros((8, 64), jnp.float32)], 1)
            lo = jnp.where(lane8 < 32, y, 0.0)
            hi = jnp.where(lane8 < 32, pltpu.roll(y, 96, 1), 0.0)
            ea = jnp.where(c == start, lo[0:1], hi[0:1])
            eb = jnp.where(c == start, hi[1:2], zero[1:2])
        else:
            va = unit - window[1]
            y = jnp.concatenate([in_row(va, xa[offsets[depth]]), jnp.zeros((8, 96), jnp.float32)], 1)
            ea, eb = y[0:1], zero[0:1]
        ea = jnp.broadcast_to(ea, (8, 128))
        eb = jnp.broadcast_to(eb, (8, 128))
        odd = (here & 1) == 1
        window = [
            jnp.where(odd, ea, window[0]),
            jnp.where(odd, window[1], ea),
            jnp.where(odd, eb, window[1]),
        ]
    out_ref[...] = jnp.where(row_id == 0, window[0], jnp.where(row_id == 1, window[1], window[2]))


def solve(g, pos, group=8):
    count = g.shape[0]
    return pl.pallas_call(
        functools.partial(solve_kernel, count, group),
        out_shape=jax.ShapeDtypeStruct((8, 128), jnp.float32),
        in_specs=[pl.BlockSpec(memory_space=pltpu.SMEM), pl.BlockSpec(memory_space=pltpu.VMEM)],
        out_specs=pl.BlockSpec(memory_space=pltpu.VMEM),
        scratch_shapes=[pltpu.VMEM((count, 32, 128), jnp.float32)] * 3,
        compiler_params=pltpu.CompilerParams(vmem_limit_bytes=32 * 1024 * 1024),
    )(pos, g)


def per_device(deflation, permeability_base, design_mask, storage, right_side):
    vectors = deflation.shape[0]
    permeability = permeability_base * jnp.exp(
        (design_mask.astype(jnp.float32) - 1.0) * LOG_CONTRAST
    )
    stacked = jnp.concatenate([deflation, permeability[None]], 0)
    padded = padded_2(stacked, (("sub", 1), ("own", 2)), 1)
    zpadded = padded[:vectors]
    kpadded = padded[vectors]
    t_east = transmit(permeability, kpadded[2:, 1:-1])
    t_west = transmit(permeability, kpadded[:-2, 1:-1])
    t_north = transmit(permeability, kpadded[1:-1, 2:])
    t_south = transmit(permeability, kpadded[1:-1, :-2])
    isolated = jnp.pad(zpadded[:, 1:-1, :], ((0, 0), (1, 1), (0, 0)))
    applied = (
        storage * deflation
        + t_east * (deflation - isolated[:, 2:, 1:-1])
        + t_west * (deflation - isolated[:, :-2, 1:-1])
    )
    applied = (
        applied
        + t_north * (deflation - isolated[:, 1:-1, 2:])
        + t_south * (deflation - isolated[:, 1:-1, :-2])
    )
    flat = deflation.reshape(vectors, -1)
    diag_part = jnp.dot(flat, applied.reshape(vectors, -1).T, precision=precise)
    low_part = -jnp.dot(deflation[:, 0, :] * t_west[0], zpadded[:, 0, 1:-1].T, precision=precise)
    rhs_part = jnp.dot(flat, right_side.reshape(-1), precision=precise)
    tile = jnp.zeros((32, 64), jnp.float32)
    tile = tile.at[:vectors, :vectors].set(diag_part)
    tile = tile.at[:vectors, vectors].set(rhs_part)
    tile = tile.at[:vectors, 32 : 32 + vectors].set(low_part)
    part = jnp.concatenate([tile[:16], tile[16:]], 1)
    summed = shared_with_all(part, "own").sum(0)
    gathered = shared_with_all(summed, "sub")
    position = lax.axis_index("sub").astype(jnp.int32)
    window = solve(gathered, position[None])[:3, :vectors]
    mine = window[1]
    middle = jnp.dot(mine, zpadded[:, 1:-1, :].reshape(vectors, -1), precision=precise)
    middle = middle.reshape(zpadded.shape[1] - 2, zpadded.shape[2])
    above = jnp.dot(window[0], zpadded[:, 0, :], precision=precise)
    below = jnp.dot(window[2], zpadded[:, -1, :], precision=precise)
    fpadded = jnp.concatenate([above[None], middle, below[None]], 0)
    field = fpadded[1:-1, 1:-1]
    applied_field = (
        storage * field
        + t_east * (field - fpadded[2:, 1:-1])
        + t_west * (field - fpadded[:-2, 1:-1])
    )
    applied_field = (
        applied_field
        + t_north * (field - fpadded[1:-1, 2:])
        + t_south * (field - fpadded[1:-1, :-2])
    )
    return (mine[None], right_side - applied_field)


def solution(mesh):
    placed = (
        P(None, "sub", "own"),
        P("sub", "own"),
        P("sub", "own"),
        P("sub", "own"),
        P("sub", "own"),
    )
    return jax.shard_map(
        per_device,
        mesh=mesh,
        in_specs=placed,
        out_specs=(P("sub", None), P("sub", "own")),
        check_vma=False,
    )
```

```python
import functools
import math

import jax
import jax.numpy as jnp
from jax import lax
from jax.experimental import pallas as pl
from jax.experimental.pallas import tpu as pltpu
from jax.sharding import PartitionSpec as P

LOG_CONTRAST = math.log(1000.0)
precise = lax.Precision.HIGHEST
NV = 30
NT = (((1,), (1,)), ((), ()))
VMEM = pl.BlockSpec(memory_space=pltpu.VMEM)
SMEM = pl.BlockSpec(memory_space=pltpu.SMEM)


def f32(*shape):
    return jax.ShapeDtypeStruct(shape, jnp.float32)


def limit(mib):
    return pltpu.CompilerParams(vmem_limit_bytes=mib * 1024 * 1024)


def iota(shape, dim):
    return lax.broadcasted_iota(jnp.int32, shape, dim)


def transmit(centre, beside):
    return 2.0 * centre * beside / (centre + beside)


def split_parts(x):
    high = x.astype(jnp.bfloat16)
    rest = x - high.astype(jnp.float32)
    middle = rest.astype(jnp.bfloat16)
    low = (rest - middle.astype(jnp.float32)).astype(jnp.bfloat16)
    return high, middle, low


def edges_kernel(z_ref, base_ref, mask_ref, k_ref, first_ref, last_ref, head, tail, sems):
    nx = z_ref.shape[1]
    vectors = z_ref.shape[0]
    copies = [
        pltpu.make_async_copy(z_ref.at[:, pl.ds(0, 8), :], head, sems.at[0]),
        pltpu.make_async_copy(z_ref.at[:, pl.ds(nx - 8, 8), :], tail, sems.at[1]),
    ]
    for c in copies:
        c.start()
    k = base_ref[...] * jnp.exp((mask_ref[...].astype(jnp.float32) - 1.0) * LOG_CONTRAST)
    k_ref[...] = k
    for c in copies:
        c.wait()
    ny = k.shape[1]
    pad = jnp.zeros((31 - vectors, ny), jnp.float32)
    first_ref[...] = jnp.concatenate([head[v, 0:1, :] for v in range(vectors)] + [k[0:1]] + [pad], 0)
    last_ref[...] = jnp.concatenate([tail[v, 7:8, :] for v in range(vectors)] + [k[nx - 1 : nx]] + [pad], 0)


def edges(z, base, mask):
    vectors, nx, ny = z.shape
    return pl.pallas_call(
        edges_kernel,
        out_shape=[f32(nx, ny), f32(32, ny), f32(32, ny)],
        in_specs=[pl.BlockSpec(memory_space=pl.ANY), VMEM, VMEM],
        out_specs=[VMEM, VMEM, VMEM],
        scratch_shapes=[
            pltpu.VMEM((vectors, 8, ny), jnp.float32),
            pltpu.VMEM((vectors, 8, ny), jnp.float32),
            pltpu.SemaphoreType.DMA((2,)),
        ],
        name="edges",
    )(z, base, mask)


def assemble_kernel(z_ref, k_ref, st_ref, rs_ref, p_ref, c_ref, az_ref):
    vectors, nx, ny = z_ref.shape
    k = k_ref[...]
    st = st_ref[...]
    row, lane = iota((nx, ny), 0), iota((nx, ny), 1)
    tn = jnp.where(lane == ny - 1, 0.0, transmit(k, pltpu.roll(k, ny - 1, 1)))
    te = jnp.where(row == nx - 1, 0.0, transmit(k, pltpu.roll(k, nx - 1, 0)))

    def apply(v, _):
        z = z_ref[v]
        fn = tn * (pltpu.roll(z, ny - 1, 1) - z)
        fe = te * (pltpu.roll(z, nx - 1, 0) - z)
        az_ref[v] = st * z - fn + pltpu.roll(fn, 1, 1) - fe + pltpu.roll(fe, 1, 0)
        return 0

    lax.fori_loop(0, vectors, apply, 0, unroll=2)
    az_ref[vectors] = rs_ref[...]
    az_ref[vectors + 1] = jnp.zeros((nx, ny), jnp.float32)

    groups = nx // 8
    pick_n, pick_c = iota((128, ny), 0), iota((128, ny), 1)
    edge_lane = jnp.where(((pick_n >> 3) & 1) == 0, 0, ny - 1)
    gram, columns = None, None
    for g in range(groups):
        rows = pl.ds(8 * g, 8)
        zg = jnp.concatenate(
            [z_ref[:, rows, :].reshape(8 * vectors, ny), k[8 * g : 8 * g + 8], jnp.zeros((8, ny), jnp.float32)], 0
        )
        ag = az_ref[:, rows, :].reshape(8 * (vectors + 2), ny)
        zh, zm, zl = split_parts(zg)
        ah, am, al = split_parts(ag)
        left = jnp.concatenate([zh, zh, zm, zm, zh, zl], 1)
        right = jnp.concatenate([ah, am, ah, am, al, ah], 1)
        part = lax.dot_general(left, right, NT, preferred_element_type=jnp.float32)
        pick = ((pick_n & 7) == g) & (pick_c == edge_lane)
        pick = pick.astype(jnp.float32).astype(jnp.bfloat16)
        col = lax.dot_general(
            jnp.concatenate([zh, zm, zl], 1), jnp.concatenate([pick] * 3, 1), NT, preferred_element_type=jnp.float32
        )
        gram = part if gram is None else gram + part
        columns = col if columns is None else columns + col
    size = 8 * (vectors + 2)
    same = (iota((size, size), 0) & 7) == (iota((size, size), 1) & 7)
    gram = jnp.where(same, gram, 0.0)
    columns = jnp.where((iota((size, 128), 0) & 7) == (iota((size, 128), 1) >> 4), columns, 0.0)
    fold = (iota((32, size), 0) == (iota((32, size), 1) >> 3)).astype(jnp.float32)
    unfold = (iota((size, 128), 1) == (iota((size, 128), 0) >> 3)).astype(jnp.float32)
    folded = jnp.dot(fold, jnp.concatenate([gram, columns], 1), precision=precise, preferred_element_type=jnp.float32)
    p = jnp.dot(folded[:, :size], unfold, precision=precise, preferred_element_type=jnp.float32)
    p_ref[...] = jnp.where(iota((32, 128), 0) < vectors, p, 0.0)
    c_ref[...] = folded[:, size:]


def assemble(z, k, st, rs):
    vectors, nx, ny = z.shape
    return pl.pallas_call(
        assemble_kernel,
        out_shape=[f32(32, 128), f32(32, 128)],
        in_specs=[VMEM] * 4,
        out_specs=[VMEM, VMEM],
        scratch_shapes=[pltpu.VMEM((vectors + 2, nx, ny), jnp.float32)],
        compiler_params=limit(32),
        cost_estimate=pl.CostEstimate(flops=6 * 2 * 256 * 256 * 256 * 8, bytes_accessed=2 * 1024 * 1024, transcendentals=0),
        name="assemble",
    )(z, k, st, rs)


def pack(tile):
    lane = iota((16, 128), 1)
    return jnp.where(lane < 64, tile[:16], pltpu.roll(tile[16:], 64, 1))


def rim_kernel(first_ref, last_ref, up_ref, down_ref, p_ref, c_ref, out_ref):
    ny = first_ref.shape[1]
    body = iota((32, ny), 0) < NV
    tw = transmit(first_ref[NV : NV + 1], up_ref[NV : NV + 1])
    te = transmit(last_ref[NV : NV + 1], down_ref[NV : NV + 1])
    first = jnp.where(body, first_ref[...], 0.0)
    last = jnp.where(body, last_ref[...], 0.0)
    above = jnp.where(body, up_ref[...], 0.0)
    blank = jnp.zeros((32, ny), jnp.float32)
    left = jnp.concatenate([first * tw, last * te], 1)
    right = jnp.concatenate(
        [jnp.concatenate([first, last], 1), jnp.concatenate([-above, blank], 1), jnp.zeros((64, 2 * ny), jnp.float32)], 0
    )
    both = lax.dot_general(left, right, NT, precision=precise, preferred_element_type=jnp.float32)
    share = jnp.concatenate([pack(p_ref[...] + both), c_ref[...]], 0)
    for o in range(out_ref.shape[0]):
        out_ref[o] = share


def rim(first, last, up, down, p, c, copies):
    return pl.pallas_call(
        rim_kernel,
        out_shape=f32(copies, 48, 128),
        in_specs=[VMEM] * 6,
        out_specs=VMEM,
        name="rim",
    )(first, last, up, down, p, c)


def total_kernel(g_ref, out_ref):
    count = g_ref.shape[0]
    tile = g_ref[0, :16, :]
    for o in range(1, count):
        tile = tile + g_ref[o, :16, :]
    lane = iota((32, 128), 1)
    used = (((lane >> 3) & 1) == 0) & (iota((32, 128), 0) < NV)
    steps, flows = [], []
    for o in range(count - 1):
        here = pltpu.roll(g_ref[o, 16:48, :], 120, 1)
        there = g_ref[o + 1, 16:48, :]
        t = transmit(here[NV : NV + 1], there[NV : NV + 1])
        step = jnp.where(used, there - here, 0.0)
        steps.append(step)
        flows.append(jnp.where(used, t * step, 0.0))
    if steps:
        right = jnp.concatenate([jnp.concatenate(steps, 1), jnp.zeros((96, 128 * len(steps)), jnp.float32)], 0)
        faces = lax.dot_general(
            jnp.concatenate(flows, 1), right, NT, precision=precise, preferred_element_type=jnp.float32
        )
        tile = tile + pack(faces)
    for s in range(out_ref.shape[0]):
        out_ref[s] = tile


def total(g, copies):
    return pl.pallas_call(
        total_kernel,
        out_shape=f32(copies, 16, 128),
        in_specs=[VMEM],
        out_specs=VMEM,
        name="total",
    )(g)


def reciprocal(x):
    r = pl.reciprocal(x, approx=True)
    r = r * (2.0 - x * r)
    return r * (2.0 - x * r)


def small_inverse(p):
    a00, a01, a11 = p[0, 0], p[0, 1], p[1, 1]
    b02, b03, b12, b13 = p[0, 2], p[0, 3], p[1, 2], p[1, 3]
    ia = reciprocal(a00 * a11 - a01 * a01)
    h00, h01, h11 = a11 * ia, a01 * ia, a00 * ia
    w02, w03 = h00 * b02 - h01 * b12, h00 * b03 - h01 * b13
    w12, w13 = h11 * b12 - h01 * b02, h11 * b13 - h01 * b03
    s22 = p[2, 2] - (b02 * w02 + b12 * w12)
    s23 = p[2, 3] - (b02 * w03 + b12 * w13)
    s33 = p[3, 3] - (b03 * w03 + b13 * w13)
    iz = reciprocal(s22 * s33 - s23 * s23)
    i22, i23, i33 = s33 * iz, -(s23 * iz), s22 * iz
    i02, i03 = -(w02 * i22 + w03 * i23), -(w02 * i23 + w03 * i33)
    i12, i13 = -(w12 * i22 + w13 * i23), -(w12 * i23 + w13 * i33)
    i00 = h00 - (w02 * i02 + w03 * i03)
    i01 = -h01 - (w02 * i12 + w03 * i13)
    i11 = h11 - (w12 * i12 + w13 * i13)
    return [[i00, i01, i02, i03], [i01, i11, i12, i13], [i02, i12, i22, i23], [i03, i13, i23, i33]]


def take(x, index):
    return jnp.take_along_axis(x, index, axis=1)


def invert_packed(arrays):
    lanes = lax.broadcasted_iota(jnp.int32, (8, 128), 1)
    rows = lax.broadcasted_iota(jnp.int32, (8, 128), 0)
    start, inner = lanes & ~31, lanes & 31
    for k in range(0, 32, 4):
        index = [start + (k + b) for b in range(4)]
        inside = (inner >= k) & (inner < k + 4)
        tile = k // 8
        out = []
        for a in arrays:
            tiles = [a[8 * t : 8 * t + 8] for t in range(4)]
            r = [jnp.broadcast_to(a[k + b : k + b + 1], (8, 128)) for b in range(4)]
            p = {(i, j): take(r[i], index[j]) for i in range(4) for j in range(i, 4)}
            inv = small_inverse(p)
            rhat = [jnp.where(inside, (inner == k + b).astype(jnp.float32), r[b]) for b in range(4)]
            new_rows = [
                (inv[i][0] * rhat[0] + inv[i][1] * rhat[1]) + (inv[i][2] * rhat[2] + inv[i][3] * rhat[3])
                for i in range(4)
            ]
            fresh = []
            for t in range(4):
                c = [take(tiles[t], index[b]) for b in range(4)]
                v = jnp.where(inside, 0.0, tiles[t])
                v = v - ((c[0] * new_rows[0] + c[1] * new_rows[1]) + (c[2] * new_rows[2] + c[3] * new_rows[3]))
                if t == tile:
                    for b in range(4):
                        v = jnp.where(rows == (k + b) % 8, new_rows[b], v)
                fresh.append(v)
            out.append(jnp.concatenate(fresh, 0))
        arrays = out
    return arrays


def solve_kernel(
    count, group, place_ref, all_ref, z_ref, k_ref, st_ref, rs_ref, up_ref, down_ref, g_ref, coeff_ref, out_ref, aug, xa, xb
):
    lanes = lax.broadcasted_iota(jnp.int32, (32, 128), 1)
    rows = lax.broadcasted_iota(jnp.int32, (32, 128), 0)
    low = lanes < NV
    unit_pad = ((lanes == rows) & (rows >= NV)).astype(jnp.float32)
    unit_full = (lanes == rows).astype(jnp.float32)
    blank = jnp.zeros((32, 128), jnp.float32)

    nxt = None
    for m in reversed(range(count)):
        t = all_ref[m]
        q = jnp.where(lanes < 64, jnp.concatenate([t, pltpu.roll(t, 64, 1)], 0), 0.0)
        if nxt is None:
            aug[m] = q
        else:
            lt = jnp.transpose(nxt[:, 32:64])
            up = jnp.concatenate([jnp.zeros((32, 64), jnp.float32), lt, jnp.zeros((32, 32), jnp.float32)], 1)
            aug[m] = q + up
        nxt = q

    def invert_four(blocks):
        total = None
        for g in range(4):
            d = unit_full if blocks[g] is None else jnp.where(low, blocks[g], unit_pad)
            d = d if g == 0 else pltpu.roll(d, 32 * g, 1)
            total = d if total is None else total + d
        return total

    def spread(inverse, g, b):
        zeros = jnp.zeros_like(b)
        rhs = jnp.concatenate([zeros] * g + [b] + [zeros] * (3 - g), 0)
        return jnp.dot(inverse, rhs, precision=precise, preferred_element_type=jnp.float32)

    def arranged(a):
        ba = jnp.where(low, pltpu.roll(a, 64, 1), jnp.where(lanes < 64, a, 0.0))
        bb = jnp.where(low, pltpu.roll(a, 96, 1), jnp.where((lanes == NV) | (lanes >= 64), a, 0.0))
        return jnp.concatenate([ba, bb], 1)

    n = count
    base = 0
    offsets = []
    while n > 1:
        half = n // 2
        offsets.append(base)
        packs = (half + 3) // 4
        step = min(group, packs)

        def eliminate_group(t, _, base=base, step=step, half=half):
            sets = []
            for s in range(step):
                first = (t * step + s) * 4
                sets.append([aug[2 * (first + g)] if g < half else None for g in range(4)])
            inverses = invert_packed([invert_four(b) for b in sets])
            for s in range(step):
                first = (t * step + s) * 4
                for g in range(min(4, half)):
                    x = spread(inverses[s], g, arranged(sets[s][g]))
                    xa[base + first + g] = x[:, :128]
                    xb[base + first + g] = x[:, 128:]
            return 0

        if packs == step:
            eliminate_group(0, 0)
        else:
            lax.fori_loop(0, packs // step, eliminate_group, 0)
        keep = lanes < NV + 1
        for j in range(half):
            a = aug[2 * j + 1]
            right = xb[base + j + 1] if j + 1 < half else blank
            rhs = jnp.concatenate([blank, xa[base + j], right, blank], 0)
            aug[j] = jnp.where(keep, a, 0.0) - jnp.dot(a, rhs, precision=precise, preferred_element_type=jnp.float32)
        base += half
        n = half
    last = aug[0]
    (inverse,) = invert_packed([invert_four([last, None, None, None])])
    last = spread(inverse, 0, jnp.where(lanes == NV, last, 0.0))
    row_id = lax.broadcasted_iota(jnp.int32, (8, 128), 0)
    lane8 = lax.broadcasted_iota(jnp.int32, (8, 128), 1)
    unit = (lane8 == NV).astype(jnp.float32)

    def in_row(v, x):
        return lax.dot_general(v, x, NT, precision=precise, preferred_element_type=jnp.float32)

    pos = place_ref[0]
    zero = jnp.zeros((8, 128), jnp.float32)
    root = jnp.concatenate([in_row(unit, last), jnp.zeros((8, 96), jnp.float32)], 1)
    window = [zero, root, zero]
    for depth in reversed(range(len(offsets))):
        half = count >> (depth + 1)
        here = pos >> depth
        c = here >> 1
        if half > 1:
            start = jnp.minimum(c, half - 2)
            x2 = xa[pl.ds(offsets[depth] + start, 2)].reshape(64, 128)
            va = unit - pltpu.roll(window[0], 32, 1) - window[1]
            vb = unit - pltpu.roll(window[1], 32, 1) - window[2]
            v = jnp.where(row_id == 0, va, vb)
            y = in_row(v, x2)
            y = jnp.concatenate([y, jnp.zeros((8, 64), jnp.float32)], 1)
            lo = jnp.where(lane8 < 32, y, 0.0)
            hi = jnp.where(lane8 < 32, pltpu.roll(y, 96, 1), 0.0)
            ea = jnp.where(c == start, lo[0:1], hi[0:1])
            eb = jnp.where(c == start, hi[1:2], zero[1:2])
        else:
            va = unit - window[1]
            y = jnp.concatenate([in_row(va, xa[offsets[depth]]), jnp.zeros((8, 96), jnp.float32)], 1)
            ea, eb = y[0:1], zero[0:1]
        ea = jnp.broadcast_to(ea, (8, 128))
        eb = jnp.broadcast_to(eb, (8, 128))
        odd = (here & 1) == 1
        window = [
            jnp.where(odd, ea, window[0]),
            jnp.where(odd, window[1], ea),
            jnp.where(odd, eb, window[1]),
        ]
    coeff_ref[...] = window[1][0:1, :NV]
    finish(place_ref, window, z_ref, k_ref, st_ref, rs_ref, up_ref, down_ref, g_ref, out_ref)


def finish(place_ref, window, z_ref, k_ref, st_ref, rs_ref, up_ref, down_ref, g_ref, out_ref):
    vectors, nx, ny = z_ref.shape
    own, owners = place_ref[1], g_ref.shape[0]
    lane8 = iota((8, 128), 1)
    mine = window[1]
    weights = [take(mine, jnp.full((8, 128), v, jnp.int32)) for v in range(vectors)]
    field = None
    for v in range(vectors):
        w = weights[v]
        w = jnp.concatenate([jnp.concatenate([w] * (ny // 128), 1)] * (nx // 8), 0)
        term = w * z_ref[v]
        field = term if field is None else field + term
    k = k_ref[...]

    def in_row(row, block):
        return jnp.dot(row[:, :32], block, precision=precise, preferred_element_type=jnp.float32)

    body = iota((32, ny), 0) < NV
    f_up = in_row(window[0], jnp.where(body, up_ref[...], 0.0))[0:1]
    f_down = in_row(window[2], jnp.where(body, down_ref[...], 0.0))[0:1]
    k_up, k_down = up_ref[NV : NV + 1], down_ref[NV : NV + 1]

    def beside(o, side, there):
        block = g_ref[o, 16:48, :]
        f_row = in_row(mine, jnp.where(iota((32, 128), 0) < NV, block, 0.0))
        f_row = jnp.where(there, jnp.broadcast_to(f_row[0:1], (8, 128)), 0.0)
        k_row = jnp.where(there, jnp.broadcast_to(block[NV : NV + 1], (8, 128)), 0.0)
        f_col, k_col = [], []
        for g in range(nx // 8):
            at = lane8 == 16 * iota((8, 128), 0) + 8 * side + g
            f_col.append(jnp.sum(jnp.where(at, f_row, 0.0), 1, keepdims=True))
            k_col.append(jnp.sum(jnp.where(at, k_row, 0.0), 1, keepdims=True))
        return jnp.concatenate(f_col, 0), jnp.concatenate(k_col, 0)

    f_left, k_left = beside(jnp.maximum(own - 1, 0), 1, own > 0)
    f_right, k_right = beside(jnp.minimum(own + 1, owners - 1), 0, own < owners - 1)
    row, lane = iota((nx, ny), 0), iota((nx, ny), 1)
    east, west, north, south = row == nx - 1, row == 0, lane == ny - 1, lane == 0

    def flow(shift, axis, edge, f_edge, k_edge):
        f_near = jnp.where(edge, f_edge, pltpu.roll(field, shift, axis))
        k_near = jnp.where(edge, k_edge, pltpu.roll(k, shift, axis))
        return transmit(k, k_near) * (field - f_near)

    applied = st_ref[...] * field
    applied = applied + flow(nx - 1, 0, east, f_down, k_down)
    applied = applied + flow(1, 0, west, f_up, k_up)
    applied = applied + flow(ny - 1, 1, north, f_right, k_right)
    applied = applied + flow(1, 1, south, f_left, k_left)
    out_ref[...] = rs_ref[...] - applied


def solve(place, gathered, z, k, st, rs, up, down, g, group=8):
    count = gathered.shape[0]
    nx, ny = k.shape
    return pl.pallas_call(
        functools.partial(solve_kernel, count, group),
        out_shape=[f32(1, NV), f32(nx, ny)],
        in_specs=[SMEM] + [VMEM] * 8,
        out_specs=[VMEM, VMEM],
        scratch_shapes=[pltpu.VMEM((count, 32, 128), jnp.float32)] * 3,
        compiler_params=limit(32),
        name="solve",
    )(place, gathered, z, k, st, rs, up, down, g)


def per_device(deflation, permeability_base, design_mask, storage, right_side):
    subs, owners = lax.axis_size("sub"), lax.axis_size("own")
    k, first, last = edges(deflation, permeability_base, design_mask)
    ahead = [(i, i + 1) for i in range(subs - 1)]
    up = lax.ppermute(last, "sub", ahead)
    down = lax.ppermute(first, "sub", [(j, i) for i, j in ahead])
    p, c = assemble(deflation, k, storage, right_side)
    share = rim(first, last, up, down, p, c, owners)
    g = lax.all_to_all(share, "own", 0, 0)
    gathered = lax.all_to_all(total(g, subs), "sub", 0, 0)
    place = jnp.stack([lax.axis_index("sub"), lax.axis_index("own")]).astype(jnp.int32)
    return tuple(solve(place, gathered, deflation, k, storage, right_side, up, down, g))


def solution(mesh):
    fields = P("sub", "own")
    return jax.shard_map(
        per_device,
        mesh=mesh,
        in_specs=(P(None, "sub", "own"), fields, fields, fields, fields),
        out_specs=(P("sub", None), fields),
        check_vma=False,
    )
```

```python
import functools
import math

import jax
import jax.numpy as jnp
from jax import lax
from jax.experimental import pallas as pl
from jax.experimental.pallas import tpu as pltpu
from jax.sharding import PartitionSpec as P

LOG_CONTRAST = math.log(1000.0)
precise = lax.Precision.HIGHEST
NV = 30
NT = (((1,), (1,)), ((), ()))
VMEM = pl.BlockSpec(memory_space=pltpu.VMEM)
SMEM = pl.BlockSpec(memory_space=pltpu.SMEM)


def f32(*shape):
    return jax.ShapeDtypeStruct(shape, jnp.float32)


def limit(mib):
    return pltpu.CompilerParams(vmem_limit_bytes=mib * 1024 * 1024)


def iota(shape, dim):
    return lax.broadcasted_iota(jnp.int32, shape, dim)


def transmit(centre, beside):
    return 2.0 * centre * beside / (centre + beside)


def split_parts(x):
    high = x.astype(jnp.bfloat16)
    rest = x - high.astype(jnp.float32)
    middle = rest.astype(jnp.bfloat16)
    low = (rest - middle.astype(jnp.float32)).astype(jnp.bfloat16)
    return high, middle, low


def edges_kernel(z_ref, base_ref, mask_ref, k_ref, first_ref, last_ref, head, tail, sems):
    nx = z_ref.shape[1]
    vectors = z_ref.shape[0]
    copies = [
        pltpu.make_async_copy(z_ref.at[:, pl.ds(0, 8), :], head, sems.at[0]),
        pltpu.make_async_copy(z_ref.at[:, pl.ds(nx - 8, 8), :], tail, sems.at[1]),
    ]
    for c in copies:
        c.start()
    k = base_ref[...] * jnp.exp((mask_ref[...].astype(jnp.float32) - 1.0) * LOG_CONTRAST)
    k_ref[...] = k
    for c in copies:
        c.wait()
    ny = k.shape[1]
    pad = jnp.zeros((31 - vectors, ny), jnp.float32)
    first_ref[...] = jnp.concatenate([head[v, 0:1, :] for v in range(vectors)] + [k[0:1]] + [pad], 0)
    last_ref[...] = jnp.concatenate([tail[v, 7:8, :] for v in range(vectors)] + [k[nx - 1 : nx]] + [pad], 0)


def edges(z, base, mask):
    vectors, nx, ny = z.shape
    return pl.pallas_call(
        edges_kernel,
        out_shape=[f32(nx, ny), f32(32, ny), f32(32, ny)],
        in_specs=[pl.BlockSpec(memory_space=pl.ANY), VMEM, VMEM],
        out_specs=[VMEM, VMEM, VMEM],
        scratch_shapes=[
            pltpu.VMEM((vectors, 8, ny), jnp.float32),
            pltpu.VMEM((vectors, 8, ny), jnp.float32),
            pltpu.SemaphoreType.DMA((2,)),
        ],
        compiler_params=limit(4),
        name="edges",
    )(z, base, mask)


def assemble_kernel(z_ref, k_ref, st_ref, rs_ref, p_ref, c_ref, az_ref):
    vectors, nx, ny = z_ref.shape
    k = k_ref[...]
    st = st_ref[...]
    row, lane = iota((nx, ny), 0), iota((nx, ny), 1)
    tn = jnp.where(lane == ny - 1, 0.0, transmit(k, pltpu.roll(k, ny - 1, 1)))
    te = jnp.where(row == nx - 1, 0.0, transmit(k, pltpu.roll(k, nx - 1, 0)))

    def apply(v, _):
        z = z_ref[v]
        fn = tn * (pltpu.roll(z, ny - 1, 1) - z)
        fe = te * (pltpu.roll(z, nx - 1, 0) - z)
        az_ref[v] = st * z - fn + pltpu.roll(fn, 1, 1) - fe + pltpu.roll(fe, 1, 0)
        return 0

    lax.fori_loop(0, vectors, apply, 0, unroll=2)
    az_ref[vectors] = rs_ref[...]
    az_ref[vectors + 1] = jnp.zeros((nx, ny), jnp.float32)

    groups = nx // 8
    pick_n, pick_c = iota((128, ny), 0), iota((128, ny), 1)
    edge_lane = jnp.where(((pick_n >> 3) & 1) == 0, 0, ny - 1)
    gram, columns = None, None
    for g in range(groups):
        rows = pl.ds(8 * g, 8)
        zg = jnp.concatenate(
            [z_ref[:, rows, :].reshape(8 * vectors, ny), k[8 * g : 8 * g + 8], jnp.zeros((8, ny), jnp.float32)], 0
        )
        ag = az_ref[:, rows, :].reshape(8 * (vectors + 2), ny)
        zh, zm, zl = split_parts(zg)
        ah, am, al = split_parts(ag)
        left = jnp.concatenate([zh, zh, zm, zm, zh, zl], 1)
        right = jnp.concatenate([ah, am, ah, am, al, ah], 1)
        part = lax.dot_general(left, right, NT, preferred_element_type=jnp.float32)
        pick = ((pick_n & 7) == g) & (pick_c == edge_lane)
        pick = pick.astype(jnp.float32).astype(jnp.bfloat16)
        col = lax.dot_general(
            jnp.concatenate([zh, zm, zl], 1), jnp.concatenate([pick] * 3, 1), NT, preferred_element_type=jnp.float32
        )
        gram = part if gram is None else gram + part
        columns = col if columns is None else columns + col
    size = 8 * (vectors + 2)
    same = (iota((size, size), 0) & 7) == (iota((size, size), 1) & 7)
    gram = jnp.where(same, gram, 0.0)
    columns = jnp.where((iota((size, 128), 0) & 7) == (iota((size, 128), 1) >> 4), columns, 0.0)
    fold = (iota((32, size), 0) == (iota((32, size), 1) >> 3)).astype(jnp.float32)
    unfold = (iota((size, 128), 1) == (iota((size, 128), 0) >> 3)).astype(jnp.float32)
    folded = jnp.dot(fold, jnp.concatenate([gram, columns], 1), precision=precise, preferred_element_type=jnp.float32)
    p = jnp.dot(folded[:, :size], unfold, precision=precise, preferred_element_type=jnp.float32)
    p_ref[...] = jnp.where(iota((32, 128), 0) < vectors, p, 0.0)
    c_ref[...] = folded[:, size:]


def assemble(z, k, st, rs):
    vectors, nx, ny = z.shape
    return pl.pallas_call(
        assemble_kernel,
        out_shape=[f32(32, 128), f32(32, 128)],
        in_specs=[VMEM] * 4,
        out_specs=[VMEM, VMEM],
        scratch_shapes=[pltpu.VMEM((vectors + 2, nx, ny), jnp.float32)],
        compiler_params=limit(16),
        cost_estimate=pl.CostEstimate(flops=6 * 2 * 256 * 256 * 256 * 8, bytes_accessed=2 * 1024 * 1024, transcendentals=0),
        name="assemble",
    )(z, k, st, rs)


def pack(tile):
    lane = iota((16, 128), 1)
    return jnp.where(lane < 64, tile[:16], pltpu.roll(tile[16:], 64, 1))


def rim_kernel(first_ref, last_ref, up_ref, down_ref, p_ref, c_ref, out_ref):
    ny = first_ref.shape[1]
    body = iota((32, ny), 0) < NV
    tw = transmit(first_ref[NV : NV + 1], up_ref[NV : NV + 1])
    te = transmit(last_ref[NV : NV + 1], down_ref[NV : NV + 1])
    first = jnp.where(body, first_ref[...], 0.0)
    last = jnp.where(body, last_ref[...], 0.0)
    above = jnp.where(body, up_ref[...], 0.0)
    blank = jnp.zeros((32, ny), jnp.float32)
    left = jnp.concatenate([first * tw, last * te], 1)
    right = jnp.concatenate(
        [jnp.concatenate([first, last], 1), jnp.concatenate([-above, blank], 1), jnp.zeros((64, 2 * ny), jnp.float32)], 0
    )
    both = lax.dot_general(left, right, NT, precision=precise, preferred_element_type=jnp.float32)
    share = jnp.concatenate([pack(p_ref[...] + both), c_ref[...]], 0)
    for o in range(out_ref.shape[0]):
        out_ref[o] = share


def rim(first, last, up, down, p, c, copies):
    return pl.pallas_call(
        rim_kernel,
        out_shape=f32(copies, 48, 128),
        in_specs=[VMEM] * 6,
        out_specs=VMEM,
        compiler_params=limit(4),
        name="rim",
    )(first, last, up, down, p, c)


def total_kernel(place_ref, g_ref, out_ref):
    count = g_ref.shape[0]
    tile = g_ref[0, :16, :]
    for o in range(1, count):
        tile = tile + g_ref[o, :16, :]
    lane, row = iota((32, 128), 1), iota((32, 128), 0)
    used = (((lane >> 3) & 1) == 0) & (row < NV)
    steps, flows = [], []
    for o in range(count - 1):
        here = pltpu.roll(g_ref[o, 16:48, :], 120, 1)
        there = g_ref[o + 1, 16:48, :]
        t = transmit(here[NV : NV + 1], there[NV : NV + 1])
        step = jnp.where(used, there - here, 0.0)
        steps.append(step)
        flows.append(jnp.where(used, t * step, 0.0))
    tile = jnp.concatenate([tile, pltpu.roll(tile, 64, 1)], 0)
    if steps:
        right = jnp.concatenate([jnp.concatenate(steps, 1), jnp.zeros((96, 128 * len(steps)), jnp.float32)], 0)
        faces = lax.dot_general(
            jnp.concatenate(flows, 1), right, NT, precision=precise, preferred_element_type=jnp.float32
        )
        tile = tile + faces
    diag, inner = lane < NV, lane & 31
    (inverse,) = invert_packed([jnp.where(diag, tile, 0.0) + jnp.where((lane >= NV) & (inner == row), 1.0, 0.0)])
    right_side = jnp.sum(jnp.where(lane == NV, tile, 0.0), 1, keepdims=True)
    right_row = jnp.sum(jnp.where(lane == row, jnp.broadcast_to(right_side, (32, 128)), 0.0), 0, keepdims=True)
    even_diag = jnp.where(row < NV, inverse, jnp.where(row == NV, jnp.broadcast_to(right_row, (32, 128)), 0.0))
    before = pltpu.roll(tile, 96, 1)[:, :32]
    back = jnp.concatenate([jnp.transpose(before), jnp.zeros((32, 96), jnp.float32)], 1)
    even = jnp.where(lane < 32, back, jnp.where(lane < 32 + NV, pltpu.roll(even_diag, 32, 1), 0.0))
    odd = jnp.where(lane < 32, pltpu.roll(tile, 96, 1), jnp.where(lane < 64, pltpu.roll(tile, 32, 1), 0.0))
    both = jnp.where((place_ref[0] & 1) == 0, even, odd)
    top, bottom = both[:16], both[16:]
    half = iota((16, 128), 1)
    packed = jnp.where(
        half < 32,
        top,
        jnp.where(half < 64, pltpu.roll(bottom, 32, 1), jnp.where(half < 96, pltpu.roll(top, 32, 1), pltpu.roll(bottom, 64, 1))),
    )
    for s in range(out_ref.shape[0]):
        out_ref[s] = packed


def total(place, g, copies):
    return pl.pallas_call(
        total_kernel,
        out_shape=f32(copies, 16, 128),
        in_specs=[SMEM, VMEM],
        out_specs=VMEM,
        compiler_params=limit(4),
        name="total",
    )(place, g)


def small_inverse(p):
    a00, a01, a11 = p[0, 0], p[0, 1], p[1, 1]
    b02, b03, b12, b13 = p[0, 2], p[0, 3], p[1, 2], p[1, 3]
    ia = 1.0 / (a00 * a11 - a01 * a01)
    h00, h01, h11 = a11 * ia, a01 * ia, a00 * ia
    w02, w03 = h00 * b02 - h01 * b12, h00 * b03 - h01 * b13
    w12, w13 = h11 * b12 - h01 * b02, h11 * b13 - h01 * b03
    s22 = p[2, 2] - (b02 * w02 + b12 * w12)
    s23 = p[2, 3] - (b02 * w03 + b12 * w13)
    s33 = p[3, 3] - (b03 * w03 + b13 * w13)
    iz = 1.0 / (s22 * s33 - s23 * s23)
    i22, i23, i33 = s33 * iz, -(s23 * iz), s22 * iz
    i02, i03 = -(w02 * i22 + w03 * i23), -(w02 * i23 + w03 * i33)
    i12, i13 = -(w12 * i22 + w13 * i23), -(w12 * i23 + w13 * i33)
    i00 = h00 - (w02 * i02 + w03 * i03)
    i01 = -h01 - (w02 * i12 + w03 * i13)
    i11 = h11 - (w12 * i12 + w13 * i13)
    return [[i00, i01, i02, i03], [i01, i11, i12, i13], [i02, i12, i22, i23], [i03, i13, i23, i33]]


def take(x, index):
    return jnp.take_along_axis(x, index, axis=1)


def invert_packed(arrays):
    lanes = lax.broadcasted_iota(jnp.int32, (8, 128), 1)
    rows = lax.broadcasted_iota(jnp.int32, (8, 128), 0)
    start, inner = lanes & ~31, lanes & 31
    for k in range(0, 32, 4):
        index = [start + (k + b) for b in range(4)]
        inside = (inner >= k) & (inner < k + 4)
        tile = k // 8
        out = []
        for a in arrays:
            tiles = [a[8 * t : 8 * t + 8] for t in range(4)]
            r = [jnp.broadcast_to(a[k + b : k + b + 1], (8, 128)) for b in range(4)]
            p = {(i, j): take(r[i], index[j]) for i in range(4) for j in range(i, 4)}
            inv = small_inverse(p)
            rhat = [jnp.where(inside, (inner == k + b).astype(jnp.float32), r[b]) for b in range(4)]
            new_rows = [
                (inv[i][0] * rhat[0] + inv[i][1] * rhat[1]) + (inv[i][2] * rhat[2] + inv[i][3] * rhat[3])
                for i in range(4)
            ]
            fresh = []
            for t in range(4):
                c = [take(tiles[t], index[b]) for b in range(4)]
                v = jnp.where(inside, 0.0, tiles[t])
                v = v - ((c[0] * new_rows[0] + c[1] * new_rows[1]) + (c[2] * new_rows[2] + c[3] * new_rows[3]))
                if t == tile:
                    for b in range(4):
                        v = jnp.where(rows == (k + b) % 8, new_rows[b], v)
                fresh.append(v)
            out.append(jnp.concatenate(fresh, 0))
        arrays = out
    return arrays


def three(x):
    high = x.astype(jnp.bfloat16).astype(jnp.float32)
    rest = x - high
    middle = rest.astype(jnp.bfloat16).astype(jnp.float32)
    return high, middle, rest - middle


def narrow(*parts):
    return jnp.concatenate([p.astype(jnp.bfloat16) for p in parts], 1)


def six_left(x, lanes):
    h, m, l = three(x)
    return narrow(jnp.where(lanes < 96, h, m), jnp.where(lanes < 32, m, l)[:, :64])


def six_right(x, lanes):
    h, m, l = three(x)
    one = jnp.where(lanes < 32, h, jnp.where(lanes < 64, m, jnp.where(lanes < 96, l, h)))
    return narrow(one, jnp.where(lanes < 32, m, h)[:, :64])


def six_rows(x):
    h, m, l = (p.astype(jnp.bfloat16) for p in three(x))
    return jnp.concatenate([h, m, l, h, m, h], 0)


def six_left_64(x, lanes):
    h, m, l = three(x)
    return narrow(h, jnp.where(lanes < 64, h, m), jnp.where(lanes < 64, m, l))


def six_rows_64(x):
    h, m, l = (p.astype(jnp.bfloat16) for p in three(x))
    return jnp.concatenate([h, m, l, h, m, h], 0)


def solve_kernel(
    count,
    place_ref,
    all_ref,
    z_ref,
    k_ref,
    st_ref,
    rs_ref,
    up_ref,
    down_ref,
    g_ref,
    coeff_ref,
    out_ref,
    aug,
    xa,
    xb,
    coupling,
):
    lanes = iota((32, 128), 1)
    rows = iota((32, 128), 0)
    inner = lanes & 31
    blank = jnp.zeros((32, 128), jnp.float32)
    body = rows < NV
    diag_lanes = (lanes >= 64) & (lanes < 64 + NV)
    rhs_lane = lanes == 64 + NV
    kept = diag_lanes | rhs_lane
    below_32, below_64 = lanes < 32, lanes < 64
    flat = (((1,), (0,)), ((), ()))

    def dot(a, b, dims=flat):
        return lax.dot_general(a, b, dims, preferred_element_type=jnp.float32)

    def unpack(m):
        t = all_ref[m]
        return jnp.where((lanes & 32) == 0, jnp.concatenate([t, pltpu.roll(t, 96, 1)], 0), 0.0)

    def for_all(total, body_fn, width=16):
        if total <= width:
            for i in range(total):
                body_fn(i)
        else:

            def step(t, _):
                for i in range(width):
                    body_fn(t * width + i)
                return 0

            lax.fori_loop(0, total // width, step, 0)

    half = count // 2
    index32 = inner
    index_d = 64 + inner

    def first_spread(j):
        even, odd = unpack(2 * j), unpack(2 * j + 1)
        inverse = take(even, index_d)
        back = take(even, index32)
        ahead = take(odd, index32)
        right_row = jnp.broadcast_to(inverse[NV : NV + 1], (32, 128))
        left = six_left(jnp.where(body, inverse, 0.0), lanes)
        tb, ta, tr = six_right(back, lanes), six_right(ahead, lanes), six_right(right_row, lanes)
        is_r = iota((32, 192), 0) == NV
        zero = jnp.zeros((32, 192), jnp.bfloat16)

        def with_r(t):
            return jnp.where(is_r, tr.astype(jnp.float32), t.astype(jnp.float32)).astype(jnp.bfloat16)

        right = jnp.concatenate([tb, zero, with_r(ta), zero, zero, ta, with_r(tb), zero], 0)
        x = dot(left, right, NT)
        xa[j] = x[:, :128]
        xb[j] = x[:, 128:]
        aug[j] = odd
        coupling[j] = jnp.where((lanes & 63) < 32, ahead, 0.0)
        coupling[count + j] = jnp.where((lanes & 63) < 32, 0.0, back)

    for_all(half, first_spread)
    xb[half] = blank
    coupling[count + half] = blank

    def first_update(j):
        pair = coupling[j] + coupling[count + j + 1]
        x = jnp.concatenate([xa[j], xb[j + 1]], 0)
        aug[j] = jnp.where(kept, aug[j], 0.0) - dot(six_left_64(pair, lanes), six_rows_64(x))

    for_all(half, first_update)

    offsets = [0]
    base = half
    n = half
    unit_pad = ((lanes == rows) & (rows >= NV)).astype(jnp.float32)
    unit_full = (lanes == rows).astype(jnp.float32)

    def packed(blocks):
        total = None
        for g in range(4):
            if blocks[g] is None:
                d = unit_full if g == 0 else pltpu.roll(unit_full, 32 * g, 1)
            else:
                d = jnp.where(diag_lanes, blocks[g], 0.0)
                d = d if g == 2 else pltpu.roll(d, (32 * g + 64) % 128, 1)
                d = d + (unit_pad if g == 0 else pltpu.roll(unit_pad, 32 * g, 1))
            total = d if total is None else total + d
        return total

    def arranged(a):
        r32, r64 = pltpu.roll(a, 32, 1), pltpu.roll(a, 64, 1)
        right = jnp.where(rhs_lane, a, 0.0)
        ba = jnp.where(below_32, a, jnp.where(diag_lanes, r32, right))
        bb = jnp.where(below_64 & ~below_32, a, jnp.where(diag_lanes, r64, right))
        return jnp.concatenate([ba, bb], 1)

    while n > 1:
        half = n // 2
        offsets.append(base)
        packs = (half + 3) // 4
        sets = [[aug[2 * (4 * s + g)] if 4 * s + g < half else None for g in range(4)] for s in range(packs)]
        inverses = invert_packed([packed(b) for b in sets])
        for s in range(packs):
            for g in range(min(4, half)):
                left = six_left(take(inverses[s], 32 * g + inner), lanes)
                x = dot(left, six_rows(arranged(sets[s][g])))
                xa[base + 4 * s + g] = x[:, :128]
                xb[base + 4 * s + g] = x[:, 128:]
        xb[base + half] = blank
        for j in range(half):
            a = aug[2 * j + 1]
            pair = jnp.where(below_64, a, pltpu.roll(a, 64, 1))
            x = jnp.concatenate([xa[base + j], xb[base + j + 1]], 0)
            aug[j] = jnp.where(kept, a, 0.0) - dot(six_left_64(pair, lanes), six_rows_64(x))
        base += half
        n = half

    row_id = iota((8, 128), 0)
    lane8 = iota((8, 128), 1)
    unit = (lane8 == 64 + NV).astype(jnp.float32)
    last = aug[0]
    (inverse,) = invert_packed([packed([last, None, None, None])])
    root = jnp.sum(take(last, jnp.full((32, 128), 64 + NV, jnp.int32)) * inverse, 0, keepdims=True)
    root = jnp.where(lane8 < 32, jnp.broadcast_to(root, (8, 128)), 0.0)
    pos = place_ref[0]
    zero = jnp.zeros((8, 128), jnp.float32)
    window = [zero, root, zero]
    for depth in reversed(range(len(offsets))):
        half = count >> (depth + 1)
        here = pos >> depth
        c = here >> 1
        if half > 1:
            start = jnp.minimum(c, half - 2)
            x2 = xa[pl.ds(offsets[depth] + start, 2)].reshape(64, 128)
            va = unit - window[0] - pltpu.roll(window[1], 64, 1)
            vb = unit - window[1] - pltpu.roll(window[2], 64, 1)
            v = jnp.where(row_id == 0, va, vb)
            y = lax.dot_general(v, x2, NT, precision=precise, preferred_element_type=jnp.float32)
            y = jnp.concatenate([y, jnp.zeros((8, 64), jnp.float32)], 1)
            lo = jnp.where(lane8 < 32, y, 0.0)
            hi = jnp.where(lane8 < 32, pltpu.roll(y, 96, 1), 0.0)
            ea = jnp.where(c == start, lo[0:1], hi[0:1])
            eb = jnp.where(c == start, hi[1:2], zero[1:2])
        else:
            va = unit - pltpu.roll(window[1], 64, 1)
            y = lax.dot_general(va, xa[offsets[depth]], NT, precision=precise, preferred_element_type=jnp.float32)
            y = jnp.concatenate([y, jnp.zeros((8, 96), jnp.float32)], 1)
            ea, eb = y[0:1], zero[0:1]
        ea = jnp.broadcast_to(ea, (8, 128))
        eb = jnp.broadcast_to(eb, (8, 128))
        odd = (here & 1) == 1
        window = [
            jnp.where(odd, ea, window[0]),
            jnp.where(odd, window[1], ea),
            jnp.where(odd, eb, window[1]),
        ]
    coeff_ref[...] = window[1][0:1, :NV]
    finish(place_ref, window, z_ref, k_ref, st_ref, rs_ref, up_ref, down_ref, g_ref, out_ref)


def finish(place_ref, window, z_ref, k_ref, st_ref, rs_ref, up_ref, down_ref, g_ref, out_ref):
    vectors, nx, ny = z_ref.shape
    own, owners = place_ref[1], g_ref.shape[0]
    lane8 = iota((8, 128), 1)
    mine = window[1]
    weights = [take(mine, jnp.full((8, 128), v, jnp.int32)) for v in range(vectors)]
    field = None
    for v in range(vectors):
        w = weights[v]
        w = jnp.concatenate([jnp.concatenate([w] * (ny // 128), 1)] * (nx // 8), 0)
        term = w * z_ref[v]
        field = term if field is None else field + term
    k = k_ref[...]

    def in_row(row, block):
        return jnp.dot(row[:, :32], block, precision=precise, preferred_element_type=jnp.float32)

    body = iota((32, ny), 0) < NV
    f_up = in_row(window[0], jnp.where(body, up_ref[...], 0.0))[0:1]
    f_down = in_row(window[2], jnp.where(body, down_ref[...], 0.0))[0:1]
    k_up, k_down = up_ref[NV : NV + 1], down_ref[NV : NV + 1]

    def beside(o, side, there):
        block = g_ref[o, 16:48, :]
        f_row = in_row(mine, jnp.where(iota((32, 128), 0) < NV, block, 0.0))
        f_row = jnp.where(there, jnp.broadcast_to(f_row[0:1], (8, 128)), 0.0)
        k_row = jnp.where(there, jnp.broadcast_to(block[NV : NV + 1], (8, 128)), 0.0)
        f_col, k_col = [], []
        for g in range(nx // 8):
            at = lane8 == 16 * iota((8, 128), 0) + 8 * side + g
            f_col.append(jnp.sum(jnp.where(at, f_row, 0.0), 1, keepdims=True))
            k_col.append(jnp.sum(jnp.where(at, k_row, 0.0), 1, keepdims=True))
        return jnp.concatenate(f_col, 0), jnp.concatenate(k_col, 0)

    f_left, k_left = beside(jnp.maximum(own - 1, 0), 1, own > 0)
    f_right, k_right = beside(jnp.minimum(own + 1, owners - 1), 0, own < owners - 1)
    row, lane = iota((nx, ny), 0), iota((nx, ny), 1)
    east, west, north, south = row == nx - 1, row == 0, lane == ny - 1, lane == 0

    def flow(shift, axis, edge, f_edge, k_edge):
        f_near = jnp.where(edge, f_edge, pltpu.roll(field, shift, axis))
        k_near = jnp.where(edge, k_edge, pltpu.roll(k, shift, axis))
        return transmit(k, k_near) * (field - f_near)

    applied = st_ref[...] * field
    applied = applied + flow(nx - 1, 0, east, f_down, k_down)
    applied = applied + flow(1, 0, west, f_up, k_up)
    applied = applied + flow(ny - 1, 1, north, f_right, k_right)
    applied = applied + flow(1, 1, south, f_left, k_left)
    out_ref[...] = rs_ref[...] - applied


def solve(place, gathered, z, k, st, rs, up, down, g):
    count = gathered.shape[0]
    nx, ny = k.shape
    return pl.pallas_call(
        functools.partial(solve_kernel, count),
        out_shape=[f32(1, NV), f32(nx, ny)],
        in_specs=[SMEM] + [VMEM] * 8,
        out_specs=[VMEM, VMEM],
        scratch_shapes=[pltpu.VMEM((n, 32, 128), jnp.float32) for n in (count // 2, count, count + 1, 2 * count)],
        compiler_params=limit(16),
        name="solve",
    )(place, gathered, z, k, st, rs, up, down, g)


def per_device(deflation, permeability_base, design_mask, storage, right_side):
    subs, owners = lax.axis_size("sub"), lax.axis_size("own")
    place = jnp.stack([lax.axis_index("sub"), lax.axis_index("own")]).astype(jnp.int32)
    k, first, last = edges(deflation, permeability_base, design_mask)
    ahead = [(i, i + 1) for i in range(subs - 1)]
    up = lax.ppermute(last, "sub", ahead)
    down = lax.ppermute(first, "sub", [(j, i) for i, j in ahead])
    p, c = assemble(deflation, k, storage, right_side)
    share = rim(first, last, up, down, p, c, owners)
    g = lax.all_to_all(share, "own", 0, 0)
    gathered = lax.all_to_all(total(place, g, subs), "sub", 0, 0)
    return tuple(solve(place, gathered, deflation, k, storage, right_side, up, down, g))


def solution(mesh):
    fields = P("sub", "own")
    return jax.shard_map(
        per_device,
        mesh=mesh,
        in_specs=(P(None, "sub", "own"), fields, fields, fields, fields),
        out_specs=(P("sub", None), fields),
        check_vma=False,
    )
```

```python
import functools
import math

import jax
import jax.numpy as jnp
from jax import lax
from jax.experimental import pallas as pl
from jax.experimental.pallas import tpu as pltpu
from jax.sharding import PartitionSpec as P

LOG_CONTRAST = math.log(1000.0)
precise = lax.Precision.HIGHEST
NV = 30
NT = (((1,), (1,)), ((), ()))
VMEM = pl.BlockSpec(memory_space=pltpu.VMEM)
SMEM = pl.BlockSpec(memory_space=pltpu.SMEM)


def f32(*shape):
    return jax.ShapeDtypeStruct(shape, jnp.float32)


def limit(mib):
    return pltpu.CompilerParams(vmem_limit_bytes=mib * 1024 * 1024)


def iota(shape, dim):
    return lax.broadcasted_iota(jnp.int32, shape, dim)


def permeability(base, mask):
    return base * jnp.exp((mask.astype(jnp.float32) - 1.0) * LOG_CONTRAST)


def transmit(centre, beside):
    return 2.0 * centre * beside / (centre + beside)


def split_parts(x):
    high = x.astype(jnp.bfloat16)
    rest = x - high.astype(jnp.float32)
    middle = rest.astype(jnp.bfloat16)
    low = (rest - middle.astype(jnp.float32)).astype(jnp.bfloat16)
    return high, middle, low


def edges_kernel(z_ref, k_ref, first_ref, last_ref):
    vectors, nx, ny = z_ref.shape
    pad = jnp.zeros((31 - vectors, ny), jnp.float32)
    for row, out in ((0, first_ref), (nx - 1, last_ref)):
        rows = [z_ref[v, row : row + 1, :] for v in range(vectors)]
        out[...] = jnp.concatenate(rows + [k_ref[row : row + 1, :], pad], 0)


def edges(z, k):
    ny = k.shape[1]
    return pl.pallas_call(
        edges_kernel,
        out_shape=[f32(32, ny), f32(32, ny)],
        in_specs=[VMEM, VMEM],
        out_specs=[VMEM, VMEM],
        compiler_params=limit(4),
        name="edges",
    )(z, k)


def assemble_kernel(z_ref, k_ref, st_ref, rs_ref, p_ref, c_ref, az_ref):
    vectors, nx, ny = z_ref.shape
    k = k_ref[...]
    st = st_ref[...]
    row, lane = iota((nx, ny), 0), iota((nx, ny), 1)
    tn = jnp.where(lane == ny - 1, 0.0, transmit(k, pltpu.roll(k, ny - 1, 1)))
    te = jnp.where(row == nx - 1, 0.0, transmit(k, pltpu.roll(k, nx - 1, 0)))

    def apply(v, _):
        z = z_ref[v]
        fn = tn * (pltpu.roll(z, ny - 1, 1) - z)
        fe = te * (pltpu.roll(z, nx - 1, 0) - z)
        az_ref[v] = st * z - fn + pltpu.roll(fn, 1, 1) - fe + pltpu.roll(fe, 1, 0)
        return 0

    lax.fori_loop(0, vectors, apply, 0, unroll=6)
    az_ref[vectors] = rs_ref[...]
    az_ref[vectors + 1] = jnp.zeros((nx, ny), jnp.float32)

    groups = nx // 8
    pick_n, pick_c = iota((128, ny), 0), iota((128, ny), 1)
    edge_lane = jnp.where(((pick_n >> 3) & 1) == 0, 0, ny - 1)
    gram, columns = None, None
    for g in range(groups):
        rows = pl.ds(8 * g, 8)
        zg = jnp.concatenate(
            [z_ref[:, rows, :].reshape(8 * vectors, ny), k[8 * g : 8 * g + 8], jnp.zeros((8, ny), jnp.float32)], 0
        )
        ag = az_ref[:, rows, :].reshape(8 * (vectors + 2), ny)
        zh, zm, zl = split_parts(zg)
        ah, am, al = split_parts(ag)
        left = jnp.concatenate([zh, zh, zm, zm, zh, zl], 1)
        right = jnp.concatenate([ah, am, ah, am, al, ah], 1)
        part = lax.dot_general(left, right, NT, preferred_element_type=jnp.float32)
        pick = ((pick_n & 7) == g) & (pick_c == edge_lane)
        pick = pick.astype(jnp.float32).astype(jnp.bfloat16)
        col = lax.dot_general(
            jnp.concatenate([zh, zm, zl], 1), jnp.concatenate([pick] * 3, 1), NT, preferred_element_type=jnp.float32
        )
        gram = part if gram is None else gram + part
        columns = col if columns is None else columns + col
    size = 8 * (vectors + 2)
    same = (iota((size, size), 0) & 7) == (iota((size, size), 1) & 7)
    gram = jnp.where(same, gram, 0.0)
    columns = jnp.where((iota((size, 128), 0) & 7) == (iota((size, 128), 1) >> 4), columns, 0.0)
    fold = (iota((32, size), 0) == (iota((32, size), 1) >> 3)).astype(jnp.float32)
    unfold = (iota((size, 128), 1) == (iota((size, 128), 0) >> 3)).astype(jnp.float32)
    folded = jnp.dot(fold, jnp.concatenate([gram, columns], 1), precision=precise, preferred_element_type=jnp.float32)
    p = jnp.dot(folded[:, :size], unfold, precision=precise, preferred_element_type=jnp.float32)
    p_ref[...] = jnp.where(iota((32, 128), 0) < vectors, p, 0.0)
    c_ref[...] = folded[:, size:]


def assemble(z, k, st, rs):
    vectors, nx, ny = z.shape
    return pl.pallas_call(
        assemble_kernel,
        out_shape=[f32(32, 128), f32(32, 128)],
        in_specs=[VMEM] * 4,
        out_specs=[VMEM, VMEM],
        scratch_shapes=[pltpu.VMEM((vectors + 2, nx, ny), jnp.float32)],
        compiler_params=limit(16),
        cost_estimate=pl.CostEstimate(flops=6 * 2 * 256 * 256 * 256 * 8, bytes_accessed=2 * 1024 * 1024, transcendentals=0),
        name="assemble",
    )(z, k, st, rs)


def pack(tile):
    lane = iota((16, 128), 1)
    return jnp.where(lane < 64, tile[:16], pltpu.roll(tile[16:], 64, 1))


def rim_kernel(first_ref, last_ref, up_ref, down_ref, p_ref, c_ref, out_ref):
    ny = first_ref.shape[1]
    body = iota((32, ny), 0) < NV
    tw = transmit(first_ref[NV : NV + 1], up_ref[NV : NV + 1])
    te = transmit(last_ref[NV : NV + 1], down_ref[NV : NV + 1])
    first = jnp.where(body, first_ref[...], 0.0)
    last = jnp.where(body, last_ref[...], 0.0)
    above = jnp.where(body, up_ref[...], 0.0)
    blank = jnp.zeros((32, ny), jnp.float32)
    left = jnp.concatenate([first * tw, last * te], 1)
    right = jnp.concatenate(
        [jnp.concatenate([first, last], 1), jnp.concatenate([-above, blank], 1), jnp.zeros((64, 2 * ny), jnp.float32)], 0
    )
    both = lax.dot_general(left, right, NT, precision=precise, preferred_element_type=jnp.float32)
    share = jnp.concatenate([pack(p_ref[...] + both), c_ref[...]], 0)
    for o in range(out_ref.shape[0]):
        out_ref[o] = share


def rim(first, last, up, down, p, c, copies):
    return pl.pallas_call(
        rim_kernel,
        out_shape=f32(copies, 48, 128),
        in_specs=[VMEM] * 6,
        out_specs=VMEM,
        compiler_params=limit(4),
        name="rim",
    )(first, last, up, down, p, c)


def total_kernel(place_ref, g_ref, out_ref):
    count = g_ref.shape[0]
    tile = g_ref[0, :16, :]
    for o in range(1, count):
        tile = tile + g_ref[o, :16, :]
    lane, row = iota((32, 128), 1), iota((32, 128), 0)
    used = (((lane >> 3) & 1) == 0) & (row < NV)
    steps, flows = [], []
    for o in range(count - 1):
        here = pltpu.roll(g_ref[o, 16:48, :], 120, 1)
        there = g_ref[o + 1, 16:48, :]
        t = transmit(here[NV : NV + 1], there[NV : NV + 1])
        step = jnp.where(used, there - here, 0.0)
        steps.append(step)
        flows.append(jnp.where(used, t * step, 0.0))
    tile = jnp.concatenate([tile, pltpu.roll(tile, 64, 1)], 0)
    if steps:
        right = jnp.concatenate([jnp.concatenate(steps, 1), jnp.zeros((96, 128 * len(steps)), jnp.float32)], 0)
        faces = lax.dot_general(
            jnp.concatenate(flows, 1), right, NT, precision=precise, preferred_element_type=jnp.float32
        )
        tile = tile + faces
    diag, inner = lane < NV, lane & 31
    (inverse,) = invert_packed([jnp.where(diag, tile, 0.0) + jnp.where((lane >= NV) & (inner == row), 1.0, 0.0)])
    right_side = jnp.sum(jnp.where(lane == NV, tile, 0.0), 1, keepdims=True)
    right_row = jnp.sum(jnp.where(lane == row, jnp.broadcast_to(right_side, (32, 128)), 0.0), 0, keepdims=True)
    even_diag = jnp.where(row < NV, inverse, jnp.where(row == NV, jnp.broadcast_to(right_row, (32, 128)), 0.0))
    before = pltpu.roll(tile, 96, 1)[:, :32]
    back = jnp.concatenate([jnp.transpose(before), jnp.zeros((32, 96), jnp.float32)], 1)
    even = jnp.where(lane < 32, back, jnp.where(lane < 32 + NV, pltpu.roll(even_diag, 32, 1), 0.0))
    odd = jnp.where(lane < 32, pltpu.roll(tile, 96, 1), jnp.where(lane < 64, pltpu.roll(tile, 32, 1), 0.0))
    both = jnp.where((place_ref[0] & 1) == 0, even, odd)
    top, bottom = both[:16], both[16:]
    half = iota((16, 128), 1)
    packed = jnp.where(
        half < 32,
        top,
        jnp.where(half < 64, pltpu.roll(bottom, 32, 1), jnp.where(half < 96, pltpu.roll(top, 32, 1), pltpu.roll(bottom, 64, 1))),
    )
    for s in range(out_ref.shape[0]):
        out_ref[s] = packed


def total(place, g, copies):
    return pl.pallas_call(
        total_kernel,
        out_shape=f32(copies, 16, 128),
        in_specs=[SMEM, VMEM],
        out_specs=VMEM,
        compiler_params=limit(4),
        name="total",
    )(place, g)


def small_inverse(p):
    a00, a01, a11 = p[0, 0], p[0, 1], p[1, 1]
    b02, b03, b12, b13 = p[0, 2], p[0, 3], p[1, 2], p[1, 3]
    ia = 1.0 / (a00 * a11 - a01 * a01)
    h00, h01, h11 = a11 * ia, a01 * ia, a00 * ia
    w02, w03 = h00 * b02 - h01 * b12, h00 * b03 - h01 * b13
    w12, w13 = h11 * b12 - h01 * b02, h11 * b13 - h01 * b03
    s22 = p[2, 2] - (b02 * w02 + b12 * w12)
    s23 = p[2, 3] - (b02 * w03 + b12 * w13)
    s33 = p[3, 3] - (b03 * w03 + b13 * w13)
    iz = 1.0 / (s22 * s33 - s23 * s23)
    i22, i23, i33 = s33 * iz, -(s23 * iz), s22 * iz
    i02, i03 = -(w02 * i22 + w03 * i23), -(w02 * i23 + w03 * i33)
    i12, i13 = -(w12 * i22 + w13 * i23), -(w12 * i23 + w13 * i33)
    i00 = h00 - (w02 * i02 + w03 * i03)
    i01 = -h01 - (w02 * i12 + w03 * i13)
    i11 = h11 - (w12 * i12 + w13 * i13)
    return [[i00, i01, i02, i03], [i01, i11, i12, i13], [i02, i12, i22, i23], [i03, i13, i23, i33]]


def take(x, index):
    return jnp.take_along_axis(x, index, axis=1)


def spread_row(x, row):
    return jnp.broadcast_to(x[row : row + 1], (8, 128))


def invert_packed(arrays):
    lanes = iota((8, 128), 1)
    rows = iota((8, 128), 0)
    start, inner = lanes & ~31, lanes & 31
    states = []
    for a in arrays:
        tiles = [a[8 * t : 8 * t + 8] for t in range(4)]
        c = [take(tiles[0], start + b) for b in range(4)]
        states.append((tiles, {(i, j): spread_row(c[j], i) for i in range(4) for j in range(i, 4)}))
    for k in range(0, 32, 4):
        index = [start + (k + b) for b in range(4)]
        inside = (inner >= k) & (inner < k + 4)
        tile, q = k // 8, k % 8
        out = []
        for tiles, p in states:
            inv = small_inverse(p)
            cols = [[take(tiles[t], index[b]) for b in range(4)] for t in range(4)]
            pivot = None
            if k < 28:
                t2, q2 = (k + 4) // 8, (k + 4) % 8
                own = [take(tiles[t2], start + (k + 4 + b)) for b in range(4)]
                cross = [[spread_row(cols[t2][b], q2 + i) for b in range(4)] for i in range(4)]
                scaled = [
                    [
                        (inv[b][0] * cross[i][0] + inv[b][1] * cross[i][1])
                        + (inv[b][2] * cross[i][2] + inv[b][3] * cross[i][3])
                        for b in range(4)
                    ]
                    for i in range(4)
                ]
                pivot = {}
                for i in range(4):
                    for j in range(i, 4):
                        change = (cross[i][0] * scaled[j][0] + cross[i][1] * scaled[j][1]) + (
                            cross[i][2] * scaled[j][2] + cross[i][3] * scaled[j][3]
                        )
                        pivot[i, j] = spread_row(own[j], q2 + i) - change
            rhat = [jnp.where(inside, (inner == k + b).astype(jnp.float32), spread_row(tiles[tile], q + b)) for b in range(4)]
            new_rows = [
                (inv[i][0] * rhat[0] + inv[i][1] * rhat[1]) + (inv[i][2] * rhat[2] + inv[i][3] * rhat[3])
                for i in range(4)
            ]
            fresh = []
            for t in range(4):
                c = cols[t]
                v = jnp.where(inside, 0.0, tiles[t])
                v = v - ((c[0] * new_rows[0] + c[1] * new_rows[1]) + (c[2] * new_rows[2] + c[3] * new_rows[3]))
                if t == tile:
                    for b in range(4):
                        v = jnp.where(rows == q + b, new_rows[b], v)
                fresh.append(v)
            out.append((fresh, pivot))
        states = out
    return [jnp.concatenate(tiles, 0) for tiles, _ in states]


def invert_many(arrays):
    lanes = iota((8, 128), 1)
    rows = iota((8, 128), 0)
    start, inner = lanes & ~31, lanes & 31
    for k in range(0, 32, 4):
        index = [start + (k + b) for b in range(4)]
        inside = (inner >= k) & (inner < k + 4)
        tile = k // 8
        out = []
        for a in arrays:
            tiles = [a[8 * t : 8 * t + 8] for t in range(4)]
            r = [jnp.broadcast_to(a[k + b : k + b + 1], (8, 128)) for b in range(4)]
            cols = [[take(tiles[t], index[b]) for b in range(4)] for t in range(4)]
            q = k % 8
            p = {
                (i, j): spread_row(cols[tile][j], q + i) for i in range(4) for j in range(i, 4)
            }
            inv = small_inverse(p)
            rhat = [jnp.where(inside, (inner == k + b).astype(jnp.float32), r[b]) for b in range(4)]
            new_rows = [
                (inv[i][0] * rhat[0] + inv[i][1] * rhat[1]) + (inv[i][2] * rhat[2] + inv[i][3] * rhat[3])
                for i in range(4)
            ]
            fresh = []
            for t in range(4):
                c = cols[t]
                v = jnp.where(inside, 0.0, tiles[t])
                v = v - ((c[0] * new_rows[0] + c[1] * new_rows[1]) + (c[2] * new_rows[2] + c[3] * new_rows[3]))
                if t == tile:
                    for b in range(4):
                        v = jnp.where(rows == (k + b) % 8, new_rows[b], v)
                fresh.append(v)
            out.append(jnp.concatenate(fresh, 0))
        arrays = out
    return arrays


def three(x):
    high = x.astype(jnp.bfloat16).astype(jnp.float32)
    rest = x - high
    middle = rest.astype(jnp.bfloat16).astype(jnp.float32)
    return high, middle, rest - middle


def narrow(*parts):
    return jnp.concatenate([p.astype(jnp.bfloat16) for p in parts], 1)


def six_left(x, lanes):
    h, m, l = three(x)
    return narrow(jnp.where(lanes < 96, h, m), jnp.where(lanes < 32, m, l)[:, :64])


def six_right(x, lanes):
    h, m, l = three(x)
    one = jnp.where(lanes < 32, h, jnp.where(lanes < 64, m, jnp.where(lanes < 96, l, h)))
    return narrow(one, jnp.where(lanes < 32, m, h)[:, :64])


def six_rows(x):
    h, m, l = (p.astype(jnp.bfloat16) for p in three(x))
    return jnp.concatenate([h, m, l, h, m, h], 0)


def six_left_64(x, lanes):
    h, m, l = three(x)
    return narrow(h, jnp.where(lanes < 64, h, m), jnp.where(lanes < 64, m, l))


def six_rows_64(x):
    h, m, l = (p.astype(jnp.bfloat16) for p in three(x))
    return jnp.concatenate([h, m, l, h, m, h], 0)


def solve_kernel(
    count,
    place_ref,
    all_ref,
    z_ref,
    k_ref,
    st_ref,
    rs_ref,
    up_ref,
    down_ref,
    g_ref,
    coeff_ref,
    out_ref,
    aug,
    xa,
    xb,
    coupling,
):
    lanes = iota((32, 128), 1)
    rows = iota((32, 128), 0)
    inner = lanes & 31
    blank = jnp.zeros((32, 128), jnp.float32)
    body = rows < NV
    diag_lanes = (lanes >= 64) & (lanes < 64 + NV)
    rhs_lane = lanes == 64 + NV
    kept = diag_lanes | rhs_lane
    below_32, below_64 = lanes < 32, lanes < 64
    flat = (((1,), (0,)), ((), ()))

    def dot(a, b, dims=flat):
        return lax.dot_general(a, b, dims, preferred_element_type=jnp.float32)

    def unpack(m):
        t = all_ref[m]
        return jnp.where((lanes & 32) == 0, jnp.concatenate([t, pltpu.roll(t, 96, 1)], 0), 0.0)

    def for_all(total, body_fn, width=16):
        if total <= width:
            for i in range(total):
                body_fn(i)
        else:

            def step(t, _):
                for i in range(width):
                    body_fn(t * width + i)
                return 0

            lax.fori_loop(0, total // width, step, 0)

    half = count // 2
    index32 = inner
    index_d = 64 + inner

    def first_spread(j):
        even, odd = unpack(2 * j), unpack(2 * j + 1)
        inverse = take(even, index_d)
        back = take(even, index32)
        ahead = take(odd, index32)
        right_row = jnp.broadcast_to(inverse[NV : NV + 1], (32, 128))
        left = six_left(jnp.where(body, inverse, 0.0), lanes)
        tb, ta, tr = six_right(back, lanes), six_right(ahead, lanes), six_right(right_row, lanes)
        is_r = iota((32, 192), 0) == NV
        zero = jnp.zeros((32, 192), jnp.bfloat16)

        def with_r(t):
            return jnp.where(is_r, tr.astype(jnp.float32), t.astype(jnp.float32)).astype(jnp.bfloat16)

        right = jnp.concatenate([tb, zero, with_r(ta), zero, zero, ta, with_r(tb), zero], 0)
        x = dot(left, right, NT)
        xa[j] = x[:, :128]
        xb[j] = x[:, 128:]
        aug[j] = odd
        coupling[j] = jnp.where((lanes & 63) < 32, ahead, 0.0)
        coupling[count + j] = jnp.where((lanes & 63) < 32, 0.0, back)

    for_all(half, first_spread)
    xb[half] = blank
    coupling[count + half] = blank

    def first_update(j):
        pair = coupling[j] + coupling[count + j + 1]
        x = jnp.concatenate([xa[j], xb[j + 1]], 0)
        aug[j] = jnp.where(kept, aug[j], 0.0) - dot(six_left_64(pair, lanes), six_rows_64(x))

    for_all(half, first_update)

    offsets = [0]
    base = half
    n = half
    unit_pad = ((lanes == rows) & (rows >= NV)).astype(jnp.float32)
    unit_full = (lanes == rows).astype(jnp.float32)

    def packed(blocks):
        total = None
        for g in range(4):
            if blocks[g] is None:
                d = unit_full if g == 0 else pltpu.roll(unit_full, 32 * g, 1)
            else:
                d = jnp.where(diag_lanes, blocks[g], 0.0)
                d = d if g == 2 else pltpu.roll(d, (32 * g + 64) % 128, 1)
                d = d + (unit_pad if g == 0 else pltpu.roll(unit_pad, 32 * g, 1))
            total = d if total is None else total + d
        return total

    def arranged(a):
        r32, r64 = pltpu.roll(a, 32, 1), pltpu.roll(a, 64, 1)
        right = jnp.where(rhs_lane, a, 0.0)
        ba = jnp.where(below_32, a, jnp.where(diag_lanes, r32, right))
        bb = jnp.where(below_64 & ~below_32, a, jnp.where(diag_lanes, r64, right))
        return jnp.concatenate([ba, bb], 1)

    while n > 1:
        half = n // 2
        offsets.append(base)
        packs = (half + 3) // 4
        sets = [[aug[2 * (4 * s + g)] if 4 * s + g < half else None for g in range(4)] for s in range(packs)]
        inverses = (invert_packed if packs < 4 else invert_many)([packed(b) for b in sets])
        for s in range(packs):
            for g in range(min(4, half)):
                left = six_left(take(inverses[s], 32 * g + inner), lanes)
                x = dot(left, six_rows(arranged(sets[s][g])))
                xa[base + 4 * s + g] = x[:, :128]
                xb[base + 4 * s + g] = x[:, 128:]
        xb[base + half] = blank
        for j in range(half):
            a = aug[2 * j + 1]
            pair = jnp.where(below_64, a, pltpu.roll(a, 64, 1))
            x = jnp.concatenate([xa[base + j], xb[base + j + 1]], 0)
            aug[j] = jnp.where(kept, a, 0.0) - dot(six_left_64(pair, lanes), six_rows_64(x))
        base += half
        n = half

    row_id = iota((8, 128), 0)
    lane8 = iota((8, 128), 1)
    unit = (lane8 == 64 + NV).astype(jnp.float32)
    last = aug[0]
    (inverse,) = invert_packed([packed([last, None, None, None])])
    root = jnp.sum(take(last, jnp.full((32, 128), 64 + NV, jnp.int32)) * inverse, 0, keepdims=True)
    root = jnp.where(lane8 < 32, jnp.broadcast_to(root, (8, 128)), 0.0)
    pos = place_ref[0]
    zero = jnp.zeros((8, 128), jnp.float32)
    window = [zero, root, zero]
    for depth in reversed(range(len(offsets))):
        half = count >> (depth + 1)
        here = pos >> depth
        c = here >> 1
        if half > 1:
            start = jnp.minimum(c, half - 2)
            x2 = xa[pl.ds(offsets[depth] + start, 2)].reshape(64, 128)
            va = unit - window[0] - pltpu.roll(window[1], 64, 1)
            vb = unit - window[1] - pltpu.roll(window[2], 64, 1)
            v = jnp.where(row_id == 0, va, vb)
            y = lax.dot_general(v, x2, NT, precision=precise, preferred_element_type=jnp.float32)
            y = jnp.concatenate([y, jnp.zeros((8, 64), jnp.float32)], 1)
            lo = jnp.where(lane8 < 32, y, 0.0)
            hi = jnp.where(lane8 < 32, pltpu.roll(y, 96, 1), 0.0)
            ea = jnp.where(c == start, lo[0:1], hi[0:1])
            eb = jnp.where(c == start, hi[1:2], zero[1:2])
        else:
            va = unit - pltpu.roll(window[1], 64, 1)
            y = lax.dot_general(va, xa[offsets[depth]], NT, precision=precise, preferred_element_type=jnp.float32)
            y = jnp.concatenate([y, jnp.zeros((8, 96), jnp.float32)], 1)
            ea, eb = y[0:1], zero[0:1]
        ea = jnp.broadcast_to(ea, (8, 128))
        eb = jnp.broadcast_to(eb, (8, 128))
        odd = (here & 1) == 1
        window = [
            jnp.where(odd, ea, window[0]),
            jnp.where(odd, window[1], ea),
            jnp.where(odd, eb, window[1]),
        ]
    coeff_ref[...] = window[1][0:1, :NV]
    finish(place_ref, window, z_ref, k_ref, st_ref, rs_ref, up_ref, down_ref, g_ref, out_ref)


def finish(place_ref, window, z_ref, k_ref, st_ref, rs_ref, up_ref, down_ref, g_ref, out_ref):
    vectors, nx, ny = z_ref.shape
    own, owners = place_ref[1], g_ref.shape[0]
    lane8 = iota((8, 128), 1)
    mine = window[1]
    weights = [take(mine, jnp.full((8, 128), v, jnp.int32)) for v in range(vectors)]
    field = None
    for v in range(vectors):
        w = weights[v]
        w = jnp.concatenate([jnp.concatenate([w] * (ny // 128), 1)] * (nx // 8), 0)
        term = w * z_ref[v]
        field = term if field is None else field + term
    k = k_ref[...]

    def in_row(row, block):
        return jnp.dot(row[:, :32], block, precision=precise, preferred_element_type=jnp.float32)

    body = iota((32, ny), 0) < NV
    f_up = in_row(window[0], jnp.where(body, up_ref[...], 0.0))[0:1]
    f_down = in_row(window[2], jnp.where(body, down_ref[...], 0.0))[0:1]
    k_up, k_down = up_ref[NV : NV + 1], down_ref[NV : NV + 1]

    def beside(o, side, there):
        block = g_ref[o, 16:48, :]
        f_row = in_row(mine, jnp.where(iota((32, 128), 0) < NV, block, 0.0))
        f_row = jnp.where(there, jnp.broadcast_to(f_row[0:1], (8, 128)), 0.0)
        k_row = jnp.where(there, jnp.broadcast_to(block[NV : NV + 1], (8, 128)), 0.0)
        f_col, k_col = [], []
        for g in range(nx // 8):
            at = lane8 == 16 * iota((8, 128), 0) + 8 * side + g
            f_col.append(jnp.sum(jnp.where(at, f_row, 0.0), 1, keepdims=True))
            k_col.append(jnp.sum(jnp.where(at, k_row, 0.0), 1, keepdims=True))
        return jnp.concatenate(f_col, 0), jnp.concatenate(k_col, 0)

    f_left, k_left = beside(jnp.maximum(own - 1, 0), 1, own > 0)
    f_right, k_right = beside(jnp.minimum(own + 1, owners - 1), 0, own < owners - 1)
    row, lane = iota((nx, ny), 0), iota((nx, ny), 1)
    east, west, north, south = row == nx - 1, row == 0, lane == ny - 1, lane == 0

    def flow(shift, axis, edge, f_edge, k_edge):
        f_near = jnp.where(edge, f_edge, pltpu.roll(field, shift, axis))
        k_near = jnp.where(edge, k_edge, pltpu.roll(k, shift, axis))
        return transmit(k, k_near) * (field - f_near)

    applied = st_ref[...] * field
    applied = applied + flow(nx - 1, 0, east, f_down, k_down)
    applied = applied + flow(1, 0, west, f_up, k_up)
    applied = applied + flow(ny - 1, 1, north, f_right, k_right)
    applied = applied + flow(1, 1, south, f_left, k_left)
    out_ref[...] = rs_ref[...] - applied


def solve(place, gathered, z, k, st, rs, up, down, g):
    count = gathered.shape[0]
    nx, ny = k.shape
    return pl.pallas_call(
        functools.partial(solve_kernel, count),
        out_shape=[f32(1, NV), f32(nx, ny)],
        in_specs=[SMEM] + [VMEM] * 8,
        out_specs=[VMEM, VMEM],
        scratch_shapes=[pltpu.VMEM((n, 32, 128), jnp.float32) for n in (count // 2, count, count + 1, 2 * count)],
        compiler_params=limit(16),
        name="solve",
    )(place, gathered, z, k, st, rs, up, down, g)


def per_device(deflation, permeability_base, design_mask, storage, right_side):
    subs, owners = lax.axis_size("sub"), lax.axis_size("own")
    place = jnp.stack([lax.axis_index("sub"), lax.axis_index("own")]).astype(jnp.int32)
    k = permeability(permeability_base, design_mask)
    first, last = edges(deflation, k)
    ahead = [(i, i + 1) for i in range(subs - 1)]
    up = lax.ppermute(last, "sub", ahead)
    down = lax.ppermute(first, "sub", [(j, i) for i, j in ahead])
    p, c = assemble(deflation, k, storage, right_side)
    share = rim(first, last, up, down, p, c, owners)
    g = lax.all_to_all(share, "own", 0, 0)
    gathered = lax.all_to_all(total(place, g, subs), "sub", 0, 0)
    return tuple(solve(place, gathered, deflation, k, storage, right_side, up, down, g))


def solution(mesh):
    fields = P("sub", "own")
    return jax.shard_map(
        per_device,
        mesh=mesh,
        in_specs=(P(None, "sub", "own"), fields, fields, fields, fields),
        out_specs=(P("sub", None), fields),
        check_vma=False,
    )
```

```python
import functools
import math

import jax
import jax.numpy as jnp
from jax import lax
from jax.experimental import pallas as pl
from jax.experimental.pallas import tpu as pltpu
from jax.sharding import PartitionSpec as P

LOG_CONTRAST = math.log(1000.0)
precise = lax.Precision.HIGHEST
NV = 30
NT = (((1,), (1,)), ((), ()))
VMEM = pl.BlockSpec(memory_space=pltpu.VMEM)
SMEM = pl.BlockSpec(memory_space=pltpu.SMEM)


def f32(*shape):
    return jax.ShapeDtypeStruct(shape, jnp.float32)


def limit(mib):
    return pltpu.CompilerParams(vmem_limit_bytes=mib * 1024 * 1024)


def iota(shape, dim):
    return lax.broadcasted_iota(jnp.int32, shape, dim)


def permeability(base, mask):
    return base * jnp.exp((mask.astype(jnp.float32) - 1.0) * LOG_CONTRAST)


def transmit(centre, beside):
    return 2.0 * centre * beside / (centre + beside)


def split_parts(x):
    high = x.astype(jnp.bfloat16)
    rest = x - high.astype(jnp.float32)
    middle = rest.astype(jnp.bfloat16)
    low = (rest - middle.astype(jnp.float32)).astype(jnp.bfloat16)
    return high, middle, low


def edges_kernel(z_ref, k_ref, first_ref, last_ref):
    vectors, nx, ny = z_ref.shape
    pad = jnp.zeros((31 - vectors, ny), jnp.float32)
    for row, out in ((0, first_ref), (nx - 1, last_ref)):
        rows = [z_ref[v, row : row + 1, :] for v in range(vectors)]
        out[...] = jnp.concatenate(rows + [k_ref[row : row + 1, :], pad], 0)


def edges(z, k):
    ny = k.shape[1]
    return pl.pallas_call(
        edges_kernel,
        out_shape=[f32(32, ny), f32(32, ny)],
        in_specs=[VMEM, VMEM],
        out_specs=[VMEM, VMEM],
        compiler_params=limit(4),
        name="edges",
    )(z, k)


def assemble_kernel(z_ref, k_ref, st_ref, rs_ref, p_ref, c_ref, az_ref):
    vectors, nx, ny = z_ref.shape
    k = k_ref[...]
    st = st_ref[...]
    row, lane = iota((nx, ny), 0), iota((nx, ny), 1)
    tn = jnp.where(lane == ny - 1, 0.0, transmit(k, pltpu.roll(k, ny - 1, 1)))
    te = jnp.where(row == nx - 1, 0.0, transmit(k, pltpu.roll(k, nx - 1, 0)))

    groups = nx // 8
    pick_n, pick_c = iota((128, ny), 0), iota((128, ny), 1)
    edge_lane = jnp.where(((pick_n >> 3) & 1) == 0, 0, ny - 1)
    ts = pltpu.roll(tn, 1, 1)
    tw = pltpu.roll(te, 1, 0)
    last_row, first_row = iota((8, ny), 0) == 7, iota((8, ny), 0) == 0
    gram, columns = None, None
    for g in range(groups):
        at = slice(8 * g, 8 * g + 8)
        tn_g, ts_g, te_g, tw_g, st_g = tn[at], ts[at], te[at], tw[at], st[at]
        for v in range(vectors):
            z = z_ref[v, at, :]
            east = pltpu.roll(z, 7, 0)
            if g + 1 < groups:
                east = jnp.where(last_row, z_ref[v, 8 * g + 8 : 8 * g + 9, :], east)
            west = pltpu.roll(z, 1, 0)
            if g > 0:
                west = jnp.where(first_row, z_ref[v, 8 * g - 1 : 8 * g, :], west)
            near = tn_g * (z - pltpu.roll(z, ny - 1, 1)) + ts_g * (z - pltpu.roll(z, 1, 1))
            az_ref[g % 2, v] = (st_g * z + te_g * (z - east)) + (tw_g * (z - west) + near)
        az_ref[g % 2, vectors] = rs_ref[at, :]
        az_ref[g % 2, vectors + 1] = jnp.zeros((8, ny), jnp.float32)
        zg = jnp.concatenate([z_ref[:, at, :].reshape(8 * vectors, ny), k[at], jnp.zeros((8, ny), jnp.float32)], 0)
        ag = az_ref[g % 2].reshape(8 * (vectors + 2), ny)
        zh, zm, zl = split_parts(zg)
        ah, am, al = split_parts(ag)
        left = jnp.concatenate([zh, zh, zm, zm, zh, zl], 1)
        right = jnp.concatenate([ah, am, ah, am, al, ah], 1)
        part = lax.dot_general(left, right, NT, preferred_element_type=jnp.float32)
        pick = ((pick_n & 7) == g) & (pick_c == edge_lane)
        pick = pick.astype(jnp.float32).astype(jnp.bfloat16)
        col = lax.dot_general(
            jnp.concatenate([zh, zm, zl], 1), jnp.concatenate([pick] * 3, 1), NT, preferred_element_type=jnp.float32
        )
        gram = part if gram is None else gram + part
        columns = col if columns is None else columns + col
    size = 8 * (vectors + 2)
    same = (iota((size, size), 0) & 7) == (iota((size, size), 1) & 7)
    gram = jnp.where(same, gram, 0.0)
    columns = jnp.where((iota((size, 128), 0) & 7) == (iota((size, 128), 1) >> 4), columns, 0.0)
    fold = (iota((32, size), 0) == (iota((32, size), 1) >> 3)).astype(jnp.float32)
    unfold = (iota((size, 128), 1) == (iota((size, 128), 0) >> 3)).astype(jnp.float32)
    folded = jnp.dot(fold, jnp.concatenate([gram, columns], 1), precision=precise, preferred_element_type=jnp.float32)
    p = jnp.dot(folded[:, :size], unfold, precision=precise, preferred_element_type=jnp.float32)
    p_ref[...] = jnp.where(iota((32, 128), 0) < vectors, p, 0.0)
    c_ref[...] = folded[:, size:]


def assemble(z, k, st, rs):
    vectors, nx, ny = z.shape
    return pl.pallas_call(
        assemble_kernel,
        out_shape=[f32(32, 128), f32(32, 128)],
        in_specs=[VMEM] * 4,
        out_specs=[VMEM, VMEM],
        scratch_shapes=[pltpu.VMEM((2, vectors + 2, 8, ny), jnp.float32)],
        compiler_params=limit(16),
        cost_estimate=pl.CostEstimate(flops=6 * 2 * 256 * 256 * 256 * 8, bytes_accessed=2 * 1024 * 1024, transcendentals=0),
        name="assemble",
    )(z, k, st, rs)


def pack(tile):
    lane = iota((16, 128), 1)
    return jnp.where(lane < 64, tile[:16], pltpu.roll(tile[16:], 64, 1))


def rim_kernel(first_ref, last_ref, up_ref, down_ref, p_ref, c_ref, out_ref):
    ny = first_ref.shape[1]
    body = iota((32, ny), 0) < NV
    tw = transmit(first_ref[NV : NV + 1], up_ref[NV : NV + 1])
    te = transmit(last_ref[NV : NV + 1], down_ref[NV : NV + 1])
    first = jnp.where(body, first_ref[...], 0.0)
    last = jnp.where(body, last_ref[...], 0.0)
    above = jnp.where(body, up_ref[...], 0.0)
    blank = jnp.zeros((32, ny), jnp.float32)
    left = jnp.concatenate([first * tw, last * te], 1)
    right = jnp.concatenate(
        [jnp.concatenate([first, last], 1), jnp.concatenate([-above, blank], 1), jnp.zeros((64, 2 * ny), jnp.float32)], 0
    )
    both = lax.dot_general(left, right, NT, precision=precise, preferred_element_type=jnp.float32)
    share = jnp.concatenate([pack(p_ref[...] + both), c_ref[...]], 0)
    for o in range(out_ref.shape[0]):
        out_ref[o] = share


def rim(first, last, up, down, p, c, copies):
    return pl.pallas_call(
        rim_kernel,
        out_shape=f32(copies, 48, 128),
        in_specs=[VMEM] * 6,
        out_specs=VMEM,
        compiler_params=limit(4),
        name="rim",
    )(first, last, up, down, p, c)


def total_kernel(place_ref, g_ref, out_ref):
    count = g_ref.shape[0]
    tile = g_ref[0, :16, :]
    for o in range(1, count):
        tile = tile + g_ref[o, :16, :]
    lane, row = iota((32, 128), 1), iota((32, 128), 0)
    used = (((lane >> 3) & 1) == 0) & (row < NV)
    steps, flows = [], []
    for o in range(count - 1):
        here = pltpu.roll(g_ref[o, 16:48, :], 120, 1)
        there = g_ref[o + 1, 16:48, :]
        t = transmit(here[NV : NV + 1], there[NV : NV + 1])
        step = jnp.where(used, there - here, 0.0)
        steps.append(step)
        flows.append(jnp.where(used, t * step, 0.0))
    tile = jnp.concatenate([tile, pltpu.roll(tile, 64, 1)], 0)
    if steps:
        right = jnp.concatenate([jnp.concatenate(steps, 1), jnp.zeros((96, 128 * len(steps)), jnp.float32)], 0)
        faces = lax.dot_general(
            jnp.concatenate(flows, 1), right, NT, precision=precise, preferred_element_type=jnp.float32
        )
        tile = tile + faces
    diag, inner = lane < NV, lane & 31
    (inverse,) = invert_packed([jnp.where(diag, tile, 0.0) + jnp.where((lane >= NV) & (inner == row), 1.0, 0.0)])
    right_side = jnp.sum(jnp.where(lane == NV, tile, 0.0), 1, keepdims=True)
    right_row = jnp.sum(jnp.where(lane == row, jnp.broadcast_to(right_side, (32, 128)), 0.0), 0, keepdims=True)
    even_diag = jnp.where(row < NV, inverse, 0.0)
    before = pltpu.roll(tile, 96, 1)[:, :32]
    back = jnp.concatenate([jnp.transpose(before), jnp.zeros((32, 96), jnp.float32)], 1)
    back = jnp.where(row == NV, jnp.broadcast_to(right_row, (32, 128)), back)
    even = jnp.where(lane < 32, back, jnp.where(lane < 32 + NV, pltpu.roll(even_diag, 32, 1), 0.0))
    odd = jnp.where(lane < 32, pltpu.roll(tile, 96, 1), jnp.where(lane < 64, pltpu.roll(tile, 32, 1), 0.0))
    both = jnp.where((place_ref[0] & 1) == 0, even, odd)
    top, bottom = both[:16], both[16:]
    half = iota((16, 128), 1)
    packed = jnp.where(
        half < 32,
        top,
        jnp.where(half < 64, pltpu.roll(bottom, 32, 1), jnp.where(half < 96, pltpu.roll(top, 32, 1), pltpu.roll(bottom, 64, 1))),
    )
    for s in range(out_ref.shape[0]):
        out_ref[s] = packed


def total(place, g, copies):
    return pl.pallas_call(
        total_kernel,
        out_shape=f32(copies, 16, 128),
        in_specs=[SMEM, VMEM],
        out_specs=VMEM,
        compiler_params=limit(4),
        name="total",
    )(place, g)


def small_inverse(p):
    a00, a01, a11 = p[0, 0], p[0, 1], p[1, 1]
    b02, b03, b12, b13 = p[0, 2], p[0, 3], p[1, 2], p[1, 3]
    ia = 1.0 / (a00 * a11 - a01 * a01)
    h00, h01, h11 = a11 * ia, a01 * ia, a00 * ia
    w02, w03 = h00 * b02 - h01 * b12, h00 * b03 - h01 * b13
    w12, w13 = h11 * b12 - h01 * b02, h11 * b13 - h01 * b03
    s22 = p[2, 2] - (b02 * w02 + b12 * w12)
    s23 = p[2, 3] - (b02 * w03 + b12 * w13)
    s33 = p[3, 3] - (b03 * w03 + b13 * w13)
    iz = 1.0 / (s22 * s33 - s23 * s23)
    i22, i23, i33 = s33 * iz, -(s23 * iz), s22 * iz
    i02, i03 = -(w02 * i22 + w03 * i23), -(w02 * i23 + w03 * i33)
    i12, i13 = -(w12 * i22 + w13 * i23), -(w12 * i23 + w13 * i33)
    i00 = h00 - (w02 * i02 + w03 * i03)
    i01 = -h01 - (w02 * i12 + w03 * i13)
    i11 = h11 - (w12 * i12 + w13 * i13)
    return [[i00, i01, i02, i03], [i01, i11, i12, i13], [i02, i12, i22, i23], [i03, i13, i23, i33]]


def take(x, index):
    return jnp.take_along_axis(x, index, axis=1)


def spread_row(x, row):
    return jnp.broadcast_to(x[row : row + 1], (8, 128))


def invert_packed(arrays):
    lanes = iota((8, 128), 1)
    rows = iota((8, 128), 0)
    start, inner = lanes & ~31, lanes & 31
    states = []
    for a in arrays:
        tiles = [a[8 * t : 8 * t + 8] for t in range(4)]
        c = [take(tiles[0], start + b) for b in range(4)]
        states.append((tiles, {(i, j): spread_row(c[j], i) for i in range(4) for j in range(i, 4)}))
    for k in range(0, 32, 4):
        index = [start + (k + b) for b in range(4)]
        inside = (inner >= k) & (inner < k + 4)
        tile, q = k // 8, k % 8
        out = []
        for tiles, p in states:
            inv = small_inverse(p)
            cols = [[take(tiles[t], index[b]) for b in range(4)] for t in range(4)]
            pivot = None
            if k < 28:
                t2, q2 = (k + 4) // 8, (k + 4) % 8
                own = [take(tiles[t2], start + (k + 4 + b)) for b in range(4)]
                cross = [[spread_row(cols[t2][b], q2 + i) for b in range(4)] for i in range(4)]
                scaled = [
                    [
                        (inv[b][0] * cross[i][0] + inv[b][1] * cross[i][1])
                        + (inv[b][2] * cross[i][2] + inv[b][3] * cross[i][3])
                        for b in range(4)
                    ]
                    for i in range(4)
                ]
                pivot = {}
                for i in range(4):
                    for j in range(i, 4):
                        change = (cross[i][0] * scaled[j][0] + cross[i][1] * scaled[j][1]) + (
                            cross[i][2] * scaled[j][2] + cross[i][3] * scaled[j][3]
                        )
                        pivot[i, j] = spread_row(own[j], q2 + i) - change
            rhat = [jnp.where(inside, (inner == k + b).astype(jnp.float32), spread_row(tiles[tile], q + b)) for b in range(4)]
            new_rows = [
                (inv[i][0] * rhat[0] + inv[i][1] * rhat[1]) + (inv[i][2] * rhat[2] + inv[i][3] * rhat[3])
                for i in range(4)
            ]
            fresh = []
            for t in range(4):
                c = cols[t]
                v = jnp.where(inside, 0.0, tiles[t])
                v = v - ((c[0] * new_rows[0] + c[1] * new_rows[1]) + (c[2] * new_rows[2] + c[3] * new_rows[3]))
                if t == tile:
                    for b in range(4):
                        v = jnp.where(rows == q + b, new_rows[b], v)
                fresh.append(v)
            out.append((fresh, pivot))
        states = out
    return [jnp.concatenate(tiles, 0) for tiles, _ in states]


def invert_many(arrays):
    lanes = iota((8, 128), 1)
    rows = iota((8, 128), 0)
    start, inner = lanes & ~31, lanes & 31
    for k in range(0, 32, 4):
        index = [start + (k + b) for b in range(4)]
        inside = (inner >= k) & (inner < k + 4)
        tile = k // 8
        out = []
        for a in arrays:
            tiles = [a[8 * t : 8 * t + 8] for t in range(4)]
            r = [jnp.broadcast_to(a[k + b : k + b + 1], (8, 128)) for b in range(4)]
            cols = [[take(tiles[t], index[b]) for b in range(4)] for t in range(4)]
            q = k % 8
            p = {
                (i, j): spread_row(cols[tile][j], q + i) for i in range(4) for j in range(i, 4)
            }
            inv = small_inverse(p)
            rhat = [jnp.where(inside, (inner == k + b).astype(jnp.float32), r[b]) for b in range(4)]
            new_rows = [
                (inv[i][0] * rhat[0] + inv[i][1] * rhat[1]) + (inv[i][2] * rhat[2] + inv[i][3] * rhat[3])
                for i in range(4)
            ]
            fresh = []
            for t in range(4):
                c = cols[t]
                v = jnp.where(inside, 0.0, tiles[t])
                v = v - ((c[0] * new_rows[0] + c[1] * new_rows[1]) + (c[2] * new_rows[2] + c[3] * new_rows[3]))
                if t == tile:
                    for b in range(4):
                        v = jnp.where(rows == (k + b) % 8, new_rows[b], v)
                fresh.append(v)
            out.append(jnp.concatenate(fresh, 0))
        arrays = out
    return arrays


def three(x):
    high = x.astype(jnp.bfloat16).astype(jnp.float32)
    rest = x - high
    middle = rest.astype(jnp.bfloat16).astype(jnp.float32)
    return high, middle, rest - middle


def narrow(*parts):
    return jnp.concatenate([p.astype(jnp.bfloat16) for p in parts], 1)


def six_left(x, lanes):
    h, m, l = three(x)
    return narrow(jnp.where(lanes < 96, h, m), jnp.where(lanes < 32, m, l)[:, :64])


def six_right(x, lanes):
    h, m, l = three(x)
    one = jnp.where(lanes < 32, h, jnp.where(lanes < 64, m, jnp.where(lanes < 96, l, h)))
    return narrow(one, jnp.where(lanes < 32, m, h)[:, :64])


def six_rows(x):
    h, m, l = (p.astype(jnp.bfloat16) for p in three(x))
    return jnp.concatenate([h, m, l, h, m, h], 0)


def six_left_64(x, lanes):
    h, m, l = three(x)
    return narrow(h, jnp.where(lanes < 64, h, m), jnp.where(lanes < 64, m, l))


def six_rows_64(x):
    h, m, l = (p.astype(jnp.bfloat16) for p in three(x))
    return jnp.concatenate([h, m, l, h, m, h], 0)


def solve_kernel(
    count,
    place_ref,
    all_ref,
    z_ref,
    k_ref,
    st_ref,
    rs_ref,
    up_ref,
    down_ref,
    g_ref,
    coeff_ref,
    out_ref,
    aug,
    xa,
    xb,
    coupling,
):
    lanes = iota((32, 128), 1)
    rows = iota((32, 128), 0)
    inner = lanes & 31
    blank = jnp.zeros((32, 128), jnp.float32)
    body = rows < NV
    diag_lanes = (lanes >= 64) & (lanes < 64 + NV)
    rhs_lane = lanes == 64 + NV
    kept = diag_lanes | rhs_lane
    below_32, below_64 = lanes < 32, lanes < 64
    flat = (((1,), (0,)), ((), ()))

    def dot(a, b, dims=flat):
        return lax.dot_general(a, b, dims, preferred_element_type=jnp.float32)

    def for_all(total, body_fn, width=32):
        if total <= width:
            for i in range(total):
                body_fn(i)
        else:

            def step(t, _):
                for i in range(width):
                    body_fn(t * width + i)
                return 0

            lax.fori_loop(0, total // width, step, 0)

    half = count // 2
    inner16 = iota((16, 128), 1) & 31

    def pick(t, top, bottom):
        return jnp.concatenate([take(t, top + inner16), take(t, bottom + inner16)], 0)

    second_64 = (lanes & 32) != 0
    back_rows = second_64 & body

    def first_spread(j):
        even, odd = all_ref[2 * j], all_ref[2 * j + 1]
        inverse = pick(even, 64, 96)
        back = pick(even, 0, 32)
        ahead = pick(odd, 0, 32)
        left = six_left(inverse, lanes)
        tb = six_right(back, lanes)
        ta = six_right(jnp.where(rows == NV, jnp.broadcast_to(back[NV : NV + 1], (32, 128)), ahead), lanes)
        zero = jnp.zeros((32, 192), jnp.bfloat16)
        x = dot(left, jnp.concatenate([tb, zero, ta, zero, zero, ta, tb, zero], 0), NT)
        xa[j] = x[:, :128]
        xb[j] = x[:, 128:]
        aug[j] = jnp.concatenate([odd, pltpu.roll(odd, 96, 1)], 0)
        coupling[j] = jnp.where(second_64, 0.0, ahead)
        coupling[count + j] = jnp.where(back_rows, back, 0.0)

    for_all(half, first_spread)
    xb[half] = blank
    coupling[count + half] = blank

    def first_update(j):
        pair = coupling[j] + coupling[count + j + 1]
        x = jnp.concatenate([xa[j], xb[j + 1]], 0)
        aug[j] = jnp.where(kept, aug[j], 0.0) - dot(six_left_64(pair, lanes), six_rows_64(x))

    for_all(half, first_update)

    offsets = [0]
    base = half
    n = half
    unit_pad = ((lanes == rows) & (rows >= NV)).astype(jnp.float32)
    unit_full = (lanes == rows).astype(jnp.float32)

    def packed(blocks):
        total = None
        for g in range(4):
            if blocks[g] is None:
                d = unit_full if g == 0 else pltpu.roll(unit_full, 32 * g, 1)
            else:
                d = jnp.where(diag_lanes, blocks[g], 0.0)
                d = d if g == 2 else pltpu.roll(d, (32 * g + 64) % 128, 1)
                d = d + (unit_pad if g == 0 else pltpu.roll(unit_pad, 32 * g, 1))
            total = d if total is None else total + d
        return total

    def arranged(a):
        r32, r64 = pltpu.roll(a, 32, 1), pltpu.roll(a, 64, 1)
        right = jnp.where(rhs_lane, a, 0.0)
        ba = jnp.where(below_32, a, jnp.where(diag_lanes, r32, right))
        bb = jnp.where(below_64 & ~below_32, a, jnp.where(diag_lanes, r64, right))
        return jnp.concatenate([ba, bb], 1)

    while n > 1:
        half = n // 2
        offsets.append(base)
        packs = (half + 3) // 4
        sets = [[aug[2 * (4 * s + g)] if 4 * s + g < half else None for g in range(4)] for s in range(packs)]
        inverses = (invert_packed if packs < 4 else invert_many)([packed(b) for b in sets])
        for s in range(packs):
            for g in range(min(4, half)):
                left = six_left(take(inverses[s], 32 * g + inner), lanes)
                x = dot(left, six_rows(arranged(sets[s][g])))
                xa[base + 4 * s + g] = x[:, :128]
                xb[base + 4 * s + g] = x[:, 128:]
        xb[base + half] = blank
        for j in range(half):
            a = aug[2 * j + 1]
            pair = jnp.where(below_64, a, pltpu.roll(a, 64, 1))
            x = jnp.concatenate([xa[base + j], xb[base + j + 1]], 0)
            aug[j] = jnp.where(kept, a, 0.0) - dot(six_left_64(pair, lanes), six_rows_64(x))
        base += half
        n = half

    row_id = iota((8, 128), 0)
    lane8 = iota((8, 128), 1)
    unit = (lane8 == 64 + NV).astype(jnp.float32)
    last = aug[0]
    (inverse,) = invert_packed([packed([last, None, None, None])])
    root = jnp.sum(take(last, jnp.full((32, 128), 64 + NV, jnp.int32)) * inverse, 0, keepdims=True)
    root = jnp.where(lane8 < 32, jnp.broadcast_to(root, (8, 128)), 0.0)
    pos = place_ref[0]
    zero = jnp.zeros((8, 128), jnp.float32)
    window = [zero, root, zero]
    for depth in reversed(range(len(offsets))):
        half = count >> (depth + 1)
        here = pos >> depth
        c = here >> 1
        if half > 1:
            start = jnp.minimum(c, half - 2)
            x2 = xa[pl.ds(offsets[depth] + start, 2)].reshape(64, 128)
            va = unit - window[0] - pltpu.roll(window[1], 64, 1)
            vb = unit - window[1] - pltpu.roll(window[2], 64, 1)
            v = jnp.where(row_id == 0, va, vb)
            y = lax.dot_general(v, x2, NT, precision=precise, preferred_element_type=jnp.float32)
            y = jnp.concatenate([y, jnp.zeros((8, 64), jnp.float32)], 1)
            lo = jnp.where(lane8 < 32, y, 0.0)
            hi = jnp.where(lane8 < 32, pltpu.roll(y, 96, 1), 0.0)
            ea = jnp.where(c == start, lo[0:1], hi[0:1])
            eb = jnp.where(c == start, hi[1:2], zero[1:2])
        else:
            va = unit - pltpu.roll(window[1], 64, 1)
            y = lax.dot_general(va, xa[offsets[depth]], NT, precision=precise, preferred_element_type=jnp.float32)
            y = jnp.concatenate([y, jnp.zeros((8, 96), jnp.float32)], 1)
            ea, eb = y[0:1], zero[0:1]
        ea = jnp.broadcast_to(ea, (8, 128))
        eb = jnp.broadcast_to(eb, (8, 128))
        odd = (here & 1) == 1
        window = [
            jnp.where(odd, ea, window[0]),
            jnp.where(odd, window[1], ea),
            jnp.where(odd, eb, window[1]),
        ]
    coeff_ref[...] = window[1][0:1, :NV]
    finish(place_ref, window, z_ref, k_ref, st_ref, rs_ref, up_ref, down_ref, g_ref, out_ref)


def finish(place_ref, window, z_ref, k_ref, st_ref, rs_ref, up_ref, down_ref, g_ref, out_ref):
    vectors, nx, ny = z_ref.shape
    own, owners = place_ref[1], g_ref.shape[0]
    lane8 = iota((8, 128), 1)
    mine = window[1]
    weights = [take(mine, jnp.full((8, 128), v, jnp.int32)) for v in range(vectors)]
    field = None
    for v in range(vectors):
        w = weights[v]
        w = jnp.concatenate([jnp.concatenate([w] * (ny // 128), 1)] * (nx // 8), 0)
        term = w * z_ref[v]
        field = term if field is None else field + term
    k = k_ref[...]

    def in_row(row, block):
        return jnp.dot(row[:, :32], block, precision=precise, preferred_element_type=jnp.float32)

    body = iota((32, ny), 0) < NV
    f_up = in_row(window[0], jnp.where(body, up_ref[...], 0.0))[0:1]
    f_down = in_row(window[2], jnp.where(body, down_ref[...], 0.0))[0:1]
    k_up, k_down = up_ref[NV : NV + 1], down_ref[NV : NV + 1]

    def beside(o, side, there):
        block = g_ref[o, 16:48, :]
        f_row = in_row(mine, jnp.where(iota((32, 128), 0) < NV, block, 0.0))
        f_row = jnp.where(there, jnp.broadcast_to(f_row[0:1], (8, 128)), 0.0)
        k_row = jnp.where(there, jnp.broadcast_to(block[NV : NV + 1], (8, 128)), 0.0)
        f_col, k_col = [], []
        for g in range(nx // 8):
            at = lane8 == 16 * iota((8, 128), 0) + 8 * side + g
            f_col.append(jnp.sum(jnp.where(at, f_row, 0.0), 1, keepdims=True))
            k_col.append(jnp.sum(jnp.where(at, k_row, 0.0), 1, keepdims=True))
        return jnp.concatenate(f_col, 0), jnp.concatenate(k_col, 0)

    f_left, k_left = beside(jnp.maximum(own - 1, 0), 1, own > 0)
    f_right, k_right = beside(jnp.minimum(own + 1, owners - 1), 0, own < owners - 1)
    row, lane = iota((nx, ny), 0), iota((nx, ny), 1)
    east, west, north, south = row == nx - 1, row == 0, lane == ny - 1, lane == 0

    def flow(shift, axis, edge, f_edge, k_edge):
        f_near = jnp.where(edge, f_edge, pltpu.roll(field, shift, axis))
        k_near = jnp.where(edge, k_edge, pltpu.roll(k, shift, axis))
        return transmit(k, k_near) * (field - f_near)

    applied = st_ref[...] * field
    applied = applied + flow(nx - 1, 0, east, f_down, k_down)
    applied = applied + flow(1, 0, west, f_up, k_up)
    applied = applied + flow(ny - 1, 1, north, f_right, k_right)
    applied = applied + flow(1, 1, south, f_left, k_left)
    out_ref[...] = rs_ref[...] - applied


def solve(place, gathered, z, k, st, rs, up, down, g):
    count = gathered.shape[0]
    nx, ny = k.shape
    return pl.pallas_call(
        functools.partial(solve_kernel, count),
        out_shape=[f32(1, NV), f32(nx, ny)],
        in_specs=[SMEM] + [VMEM] * 8,
        out_specs=[VMEM, VMEM],
        scratch_shapes=[pltpu.VMEM((n, 32, 128), jnp.float32) for n in (count // 2, count, count + 1, 2 * count)],
        compiler_params=limit(16),
        name="solve",
    )(place, gathered, z, k, st, rs, up, down, g)


def per_device(deflation, permeability_base, design_mask, storage, right_side):
    subs, owners = lax.axis_size("sub"), lax.axis_size("own")
    place = jnp.stack([lax.axis_index("sub"), lax.axis_index("own")]).astype(jnp.int32)
    k = permeability(permeability_base, design_mask)
    first, last = edges(deflation, k)
    ahead = [(i, i + 1) for i in range(subs - 1)]
    up = lax.ppermute(last, "sub", ahead)
    down = lax.ppermute(first, "sub", [(j, i) for i, j in ahead])
    p, c = assemble(deflation, k, storage, right_side)
    share = rim(first, last, up, down, p, c, owners)
    g = lax.all_to_all(share, "own", 0, 0)
    gathered = lax.all_to_all(total(place, g, subs), "sub", 0, 0)
    return tuple(solve(place, gathered, deflation, k, storage, right_side, up, down, g))


def solution(mesh):
    fields = P("sub", "own")
    return jax.shard_map(
        per_device,
        mesh=mesh,
        in_specs=(P(None, "sub", "own"), fields, fields, fields, fields),
        out_specs=(P("sub", None), fields),
        check_vma=False,
    )
```

```python
import functools
import math

import jax
import jax.numpy as jnp
from jax import lax
from jax.experimental import pallas as pl
from jax.experimental.pallas import tpu as pltpu
from jax.sharding import PartitionSpec as P

LOG_CONTRAST = math.log(1000.0)
precise = lax.Precision.HIGHEST
NV = 30
NT = (((1,), (1,)), ((), ()))
VMEM = pl.BlockSpec(memory_space=pltpu.VMEM)
SMEM = pl.BlockSpec(memory_space=pltpu.SMEM)


def f32(*shape):
    return jax.ShapeDtypeStruct(shape, jnp.float32)


def limit(mib):
    return pltpu.CompilerParams(vmem_limit_bytes=mib * 1024 * 1024)


def iota(shape, dim):
    return lax.broadcasted_iota(jnp.int32, shape, dim)


def permeability(base, mask):
    return base * jnp.exp((mask.astype(jnp.float32) - 1.0) * LOG_CONTRAST)


def transmit(centre, beside):
    return 2.0 * centre * beside / (centre + beside)


def split_parts(x):
    high = x.astype(jnp.bfloat16)
    rest = x - high.astype(jnp.float32)
    middle = rest.astype(jnp.bfloat16)
    low = (rest - middle.astype(jnp.float32)).astype(jnp.bfloat16)
    return high, middle, low


def edges_kernel(z_ref, k_ref, out_ref):
    vectors, nx, ny = z_ref.shape
    pad = jnp.zeros((31 - vectors, ny), jnp.float32)
    for row, at in ((0, 0), (nx - 1, 32)):
        rows = [z_ref[v, row : row + 1, :] for v in range(vectors)]
        out_ref[at : at + 32, :] = jnp.concatenate(rows + [k_ref[row : row + 1, :], pad], 0)


def edges(z, k):
    return pl.pallas_call(
        edges_kernel,
        out_shape=f32(64, k.shape[1]),
        in_specs=[VMEM, VMEM],
        out_specs=VMEM,
        compiler_params=limit(4),
        name="edges",
    )(z, k)


def neighbours(place_ref, a_ref, b_ref):
    odd = (place_ref[0] & 1) == 1
    up = jnp.where(odd, a_ref[32:, :], b_ref[32:, :])
    down = jnp.where(odd, b_ref[:32, :], a_ref[:32, :])
    return up, down


def assemble_kernel(z_ref, k_ref, st_ref, rs_ref, p_ref, c_ref, az_ref):
    vectors, nx, ny = z_ref.shape
    k = k_ref[...]
    st = st_ref[...]
    row, lane = iota((nx, ny), 0), iota((nx, ny), 1)
    tn = jnp.where(lane == ny - 1, 0.0, transmit(k, pltpu.roll(k, ny - 1, 1)))
    te = jnp.where(row == nx - 1, 0.0, transmit(k, pltpu.roll(k, nx - 1, 0)))

    groups = nx // 8
    pick_n, pick_c = iota((128, ny), 0), iota((128, ny), 1)
    edge_lane = jnp.where(((pick_n >> 3) & 1) == 0, 0, ny - 1)
    ts = pltpu.roll(tn, 1, 1)
    tw = pltpu.roll(te, 1, 0)
    last_row, first_row = iota((8, ny), 0) == 7, iota((8, ny), 0) == 0
    gram, columns = None, None
    for g in range(groups):
        at = slice(8 * g, 8 * g + 8)
        tn_g, ts_g, te_g, tw_g, st_g = tn[at], ts[at], te[at], tw[at], st[at]
        for v in range(vectors):
            z = z_ref[v, at, :]
            east = pltpu.roll(z, 7, 0)
            if g + 1 < groups:
                east = jnp.where(last_row, z_ref[v, 8 * g + 8 : 8 * g + 9, :], east)
            west = pltpu.roll(z, 1, 0)
            if g > 0:
                west = jnp.where(first_row, z_ref[v, 8 * g - 1 : 8 * g, :], west)
            near = tn_g * (z - pltpu.roll(z, ny - 1, 1)) + ts_g * (z - pltpu.roll(z, 1, 1))
            az_ref[g % 2, v] = (st_g * z + te_g * (z - east)) + (tw_g * (z - west) + near)
        az_ref[g % 2, vectors] = rs_ref[at, :]
        az_ref[g % 2, vectors + 1] = jnp.zeros((8, ny), jnp.float32)
        zg = jnp.concatenate([z_ref[:, at, :].reshape(8 * vectors, ny), k[at], jnp.zeros((8, ny), jnp.float32)], 0)
        ag = az_ref[g % 2].reshape(8 * (vectors + 2), ny)
        zh, zm, zl = split_parts(zg)
        ah, am, al = split_parts(ag)
        left = jnp.concatenate([zh, zh, zm, zm, zh, zl], 1)
        right = jnp.concatenate([ah, am, ah, am, al, ah], 1)
        part = lax.dot_general(left, right, NT, preferred_element_type=jnp.float32)
        pick = ((pick_n & 7) == g) & (pick_c == edge_lane)
        pick = pick.astype(jnp.float32).astype(jnp.bfloat16)
        col = lax.dot_general(
            jnp.concatenate([zh, zm, zl], 1), jnp.concatenate([pick] * 3, 1), NT, preferred_element_type=jnp.float32
        )
        gram = part if gram is None else gram + part
        columns = col if columns is None else columns + col
    size = 8 * (vectors + 2)
    same = (iota((size, size), 0) & 7) == (iota((size, size), 1) & 7)
    gram = jnp.where(same, gram, 0.0)
    columns = jnp.where((iota((size, 128), 0) & 7) == (iota((size, 128), 1) >> 4), columns, 0.0)
    fold = (iota((32, size), 0) == (iota((32, size), 1) >> 3)).astype(jnp.float32)
    unfold = (iota((size, 128), 1) == (iota((size, 128), 0) >> 3)).astype(jnp.float32)
    folded = jnp.dot(fold, jnp.concatenate([gram, columns], 1), precision=precise, preferred_element_type=jnp.float32)
    p = jnp.dot(folded[:, :size], unfold, precision=precise, preferred_element_type=jnp.float32)
    p_ref[...] = jnp.where(iota((32, 128), 0) < vectors, p, 0.0)
    c_ref[...] = folded[:, size:]


def assemble(z, k, st, rs):
    vectors, nx, ny = z.shape
    return pl.pallas_call(
        assemble_kernel,
        out_shape=[f32(32, 128), f32(32, 128)],
        in_specs=[VMEM] * 4,
        out_specs=[VMEM, VMEM],
        scratch_shapes=[pltpu.VMEM((2, vectors + 2, 8, ny), jnp.float32)],
        compiler_params=limit(16),
        cost_estimate=pl.CostEstimate(flops=6 * 2 * 256 * 256 * 256 * 8, bytes_accessed=2 * 1024 * 1024, transcendentals=0),
        name="assemble",
    )(z, k, st, rs)


def pack(tile):
    lane = iota((16, 128), 1)
    return jnp.where(lane < 64, tile[:16], pltpu.roll(tile[16:], 64, 1))


def rim_kernel(place_ref, edge_ref, a_ref, b_ref, p_ref, c_ref, out_ref):
    ny = edge_ref.shape[1]
    body = iota((32, ny), 0) < NV
    up, down = neighbours(place_ref, a_ref, b_ref)
    tw = transmit(edge_ref[NV : NV + 1, :], up[NV : NV + 1])
    te = transmit(edge_ref[32 + NV : 33 + NV, :], down[NV : NV + 1])
    first = jnp.where(body, edge_ref[:32, :], 0.0)
    last = jnp.where(body, edge_ref[32:, :], 0.0)
    above = jnp.where(body, up, 0.0)
    blank = jnp.zeros((32, ny), jnp.float32)
    left = jnp.concatenate([first * tw, last * te], 1)
    right = jnp.concatenate(
        [jnp.concatenate([first, last], 1), jnp.concatenate([-above, blank], 1), jnp.zeros((64, 2 * ny), jnp.float32)], 0
    )
    both = lax.dot_general(left, right, NT, precision=precise, preferred_element_type=jnp.float32)
    share = jnp.concatenate([pack(p_ref[...] + both), c_ref[...]], 0)
    for o in range(out_ref.shape[0]):
        out_ref[o] = share


def rim(place, edge, a, b, p, c, copies):
    return pl.pallas_call(
        rim_kernel,
        out_shape=f32(copies, 48, 128),
        in_specs=[SMEM] + [VMEM] * 5,
        out_specs=VMEM,
        compiler_params=limit(4),
        name="rim",
    )(place, edge, a, b, p, c)


def total_kernel(place_ref, g_ref, out_ref):
    count = g_ref.shape[0]
    tile = g_ref[0, :16, :]
    for o in range(1, count):
        tile = tile + g_ref[o, :16, :]
    lane, row = iota((32, 128), 1), iota((32, 128), 0)
    used = (((lane >> 3) & 1) == 0) & (row < NV)
    steps, flows = [], []
    for o in range(count - 1):
        here = pltpu.roll(g_ref[o, 16:48, :], 120, 1)
        there = g_ref[o + 1, 16:48, :]
        t = transmit(here[NV : NV + 1], there[NV : NV + 1])
        step = jnp.where(used, there - here, 0.0)
        steps.append(step)
        flows.append(jnp.where(used, t * step, 0.0))
    tile = jnp.concatenate([tile, pltpu.roll(tile, 64, 1)], 0)
    if steps:
        right = jnp.concatenate([jnp.concatenate(steps, 1), jnp.zeros((96, 128 * len(steps)), jnp.float32)], 0)
        faces = lax.dot_general(
            jnp.concatenate(flows, 1), right, NT, precision=precise, preferred_element_type=jnp.float32
        )
        tile = tile + faces
    diag, inner = lane < NV, lane & 31
    (inverse,) = invert_packed([jnp.where(diag, tile, 0.0) + jnp.where((lane >= NV) & (inner == row), 1.0, 0.0)])
    right_side = jnp.sum(jnp.where(lane == NV, tile, 0.0), 1, keepdims=True)
    right_row = jnp.sum(jnp.where(lane == row, jnp.broadcast_to(right_side, (32, 128)), 0.0), 0, keepdims=True)
    even_diag = jnp.where(row < NV, inverse, 0.0)
    before = pltpu.roll(tile, 96, 1)[:, :32]
    back = jnp.concatenate([jnp.transpose(before), jnp.zeros((32, 96), jnp.float32)], 1)
    back = jnp.where(row == NV, jnp.broadcast_to(right_row, (32, 128)), back)
    even = jnp.where(lane < 32, back, jnp.where(lane < 32 + NV, pltpu.roll(even_diag, 32, 1), 0.0))
    odd = jnp.where(lane < 32, pltpu.roll(tile, 96, 1), jnp.where(lane < 64, pltpu.roll(tile, 32, 1), 0.0))
    both = jnp.where((place_ref[0] & 1) == 0, even, odd)
    top, bottom = both[:16], both[16:]
    half = iota((16, 128), 1)
    packed = jnp.where(
        half < 32,
        top,
        jnp.where(half < 64, pltpu.roll(bottom, 32, 1), jnp.where(half < 96, pltpu.roll(top, 32, 1), pltpu.roll(bottom, 64, 1))),
    )
    for s in range(out_ref.shape[0]):
        out_ref[s] = packed


def total(place, g, copies):
    return pl.pallas_call(
        total_kernel,
        out_shape=f32(copies, 16, 128),
        in_specs=[SMEM, VMEM],
        out_specs=VMEM,
        compiler_params=limit(4),
        name="total",
    )(place, g)


def small_inverse(p):
    a00, a01, a11 = p[0, 0], p[0, 1], p[1, 1]
    b02, b03, b12, b13 = p[0, 2], p[0, 3], p[1, 2], p[1, 3]
    ia = 1.0 / (a00 * a11 - a01 * a01)
    h00, h01, h11 = a11 * ia, a01 * ia, a00 * ia
    w02, w03 = h00 * b02 - h01 * b12, h00 * b03 - h01 * b13
    w12, w13 = h11 * b12 - h01 * b02, h11 * b13 - h01 * b03
    s22 = p[2, 2] - (b02 * w02 + b12 * w12)
    s23 = p[2, 3] - (b02 * w03 + b12 * w13)
    s33 = p[3, 3] - (b03 * w03 + b13 * w13)
    iz = 1.0 / (s22 * s33 - s23 * s23)
    i22, i23, i33 = s33 * iz, -(s23 * iz), s22 * iz
    i02, i03 = -(w02 * i22 + w03 * i23), -(w02 * i23 + w03 * i33)
    i12, i13 = -(w12 * i22 + w13 * i23), -(w12 * i23 + w13 * i33)
    i00 = h00 - (w02 * i02 + w03 * i03)
    i01 = -h01 - (w02 * i12 + w03 * i13)
    i11 = h11 - (w12 * i12 + w13 * i13)
    return [[i00, i01, i02, i03], [i01, i11, i12, i13], [i02, i12, i22, i23], [i03, i13, i23, i33]]


def take(x, index):
    return jnp.take_along_axis(x, index, axis=1)


def spread_row(x, row):
    return jnp.broadcast_to(x[row : row + 1], (8, 128))


def invert_packed(arrays):
    lanes = iota((8, 128), 1)
    rows = iota((8, 128), 0)
    start, inner = lanes & ~31, lanes & 31
    states = []
    for a in arrays:
        tiles = [a[8 * t : 8 * t + 8] for t in range(4)]
        c = [take(tiles[0], start + b) for b in range(4)]
        states.append((tiles, {(i, j): spread_row(c[j], i) for i in range(4) for j in range(i, 4)}))
    for k in range(0, 32, 4):
        index = [start + (k + b) for b in range(4)]
        inside = (inner >= k) & (inner < k + 4)
        tile, q = k // 8, k % 8
        out = []
        for tiles, p in states:
            inv = small_inverse(p)
            cols = [[take(tiles[t], index[b]) for b in range(4)] for t in range(4)]
            pivot = None
            if k < 28:
                t2, q2 = (k + 4) // 8, (k + 4) % 8
                own = [take(tiles[t2], start + (k + 4 + b)) for b in range(4)]
                cross = [[spread_row(cols[t2][b], q2 + i) for b in range(4)] for i in range(4)]
                scaled = [
                    [
                        (inv[b][0] * cross[i][0] + inv[b][1] * cross[i][1])
                        + (inv[b][2] * cross[i][2] + inv[b][3] * cross[i][3])
                        for b in range(4)
                    ]
                    for i in range(4)
                ]
                pivot = {}
                for i in range(4):
                    for j in range(i, 4):
                        change = (cross[i][0] * scaled[j][0] + cross[i][1] * scaled[j][1]) + (
                            cross[i][2] * scaled[j][2] + cross[i][3] * scaled[j][3]
                        )
                        pivot[i, j] = spread_row(own[j], q2 + i) - change
            rhat = [jnp.where(inside, (inner == k + b).astype(jnp.float32), spread_row(tiles[tile], q + b)) for b in range(4)]
            new_rows = [
                (inv[i][0] * rhat[0] + inv[i][1] * rhat[1]) + (inv[i][2] * rhat[2] + inv[i][3] * rhat[3])
                for i in range(4)
            ]
            fresh = []
            for t in range(4):
                c = cols[t]
                v = jnp.where(inside, 0.0, tiles[t])
                v = v - ((c[0] * new_rows[0] + c[1] * new_rows[1]) + (c[2] * new_rows[2] + c[3] * new_rows[3]))
                if t == tile:
                    for b in range(4):
                        v = jnp.where(rows == q + b, new_rows[b], v)
                fresh.append(v)
            out.append((fresh, pivot))
        states = out
    return [jnp.concatenate(tiles, 0) for tiles, _ in states]


def invert_many(arrays):
    lanes = iota((8, 128), 1)
    rows = iota((8, 128), 0)
    start, inner = lanes & ~31, lanes & 31
    for k in range(0, 32, 4):
        index = [start + (k + b) for b in range(4)]
        inside = (inner >= k) & (inner < k + 4)
        tile = k // 8
        out = []
        for a in arrays:
            tiles = [a[8 * t : 8 * t + 8] for t in range(4)]
            r = [jnp.broadcast_to(a[k + b : k + b + 1], (8, 128)) for b in range(4)]
            cols = [[take(tiles[t], index[b]) for b in range(4)] for t in range(4)]
            q = k % 8
            p = {
                (i, j): spread_row(cols[tile][j], q + i) for i in range(4) for j in range(i, 4)
            }
            inv = small_inverse(p)
            rhat = [jnp.where(inside, (inner == k + b).astype(jnp.float32), r[b]) for b in range(4)]
            new_rows = [
                (inv[i][0] * rhat[0] + inv[i][1] * rhat[1]) + (inv[i][2] * rhat[2] + inv[i][3] * rhat[3])
                for i in range(4)
            ]
            fresh = []
            for t in range(4):
                c = cols[t]
                v = jnp.where(inside, 0.0, tiles[t])
                v = v - ((c[0] * new_rows[0] + c[1] * new_rows[1]) + (c[2] * new_rows[2] + c[3] * new_rows[3]))
                if t == tile:
                    for b in range(4):
                        v = jnp.where(rows == (k + b) % 8, new_rows[b], v)
                fresh.append(v)
            out.append(jnp.concatenate(fresh, 0))
        arrays = out
    return arrays


def three(x):
    high = x.astype(jnp.bfloat16).astype(jnp.float32)
    rest = x - high
    middle = rest.astype(jnp.bfloat16).astype(jnp.float32)
    return high, middle, rest - middle


def narrow(*parts):
    return jnp.concatenate([p.astype(jnp.bfloat16) for p in parts], 1)


def six_left(x, lanes):
    h, m, l = three(x)
    return narrow(jnp.where(lanes < 96, h, m), jnp.where(lanes < 32, m, l)[:, :64])


def six_right(x, lanes):
    h, m, l = three(x)
    one = jnp.where(lanes < 32, h, jnp.where(lanes < 64, m, jnp.where(lanes < 96, l, h)))
    return narrow(one, jnp.where(lanes < 32, m, h)[:, :64])


def six_rows(x):
    h, m, l = (p.astype(jnp.bfloat16) for p in three(x))
    return jnp.concatenate([h, m, l, h, m, h], 0)


def six_left_64(x, lanes):
    h, m, l = three(x)
    return narrow(h, jnp.where(lanes < 64, h, m), jnp.where(lanes < 64, m, l))


def six_rows_64(x):
    h, m, l = (p.astype(jnp.bfloat16) for p in three(x))
    return jnp.concatenate([h, m, l, h, m, h], 0)


def solve_kernel(
    count,
    place_ref,
    all_ref,
    z_ref,
    k_ref,
    st_ref,
    rs_ref,
    a_ref,
    b_ref,
    g_ref,
    coeff_ref,
    out_ref,
    aug,
    xa,
    xb,
    coupling,
):
    lanes = iota((32, 128), 1)
    rows = iota((32, 128), 0)
    inner = lanes & 31
    blank = jnp.zeros((32, 128), jnp.float32)
    body = rows < NV
    diag_lanes = (lanes >= 64) & (lanes < 64 + NV)
    rhs_lane = lanes == 64 + NV
    kept = diag_lanes | rhs_lane
    below_32, below_64 = lanes < 32, lanes < 64
    flat = (((1,), (0,)), ((), ()))

    def dot(a, b, dims=flat):
        return lax.dot_general(a, b, dims, preferred_element_type=jnp.float32)

    def for_all(total, body_fn, width=32):
        if total <= width:
            for i in range(total):
                body_fn(i)
        else:

            def step(t, _):
                for i in range(width):
                    body_fn(t * width + i)
                return 0

            lax.fori_loop(0, total // width, step, 0)

    half = count // 2
    inner16 = iota((16, 128), 1) & 31

    def pick(t, top, bottom):
        return jnp.concatenate([take(t, top + inner16), take(t, bottom + inner16)], 0)

    second_64 = (lanes & 32) != 0
    back_rows = second_64 & body

    def first_spread(j):
        even, odd = all_ref[2 * j], all_ref[2 * j + 1]
        inverse = pick(even, 64, 96)
        back = pick(even, 0, 32)
        ahead = pick(odd, 0, 32)
        left = six_left(inverse, lanes)
        tb = six_right(back, lanes)
        ta = six_right(jnp.where(rows == NV, jnp.broadcast_to(back[NV : NV + 1], (32, 128)), ahead), lanes)
        zero = jnp.zeros((32, 192), jnp.bfloat16)
        x = dot(left, jnp.concatenate([tb, zero, ta, zero, zero, ta, tb, zero], 0), NT)
        xa[j] = x[:, :128]
        xb[j] = x[:, 128:]
        aug[j] = jnp.concatenate([odd, pltpu.roll(odd, 96, 1)], 0)
        coupling[j] = jnp.where(second_64, 0.0, ahead)
        coupling[count + j] = jnp.where(back_rows, back, 0.0)

    for_all(half, first_spread)
    xb[half] = blank
    coupling[count + half] = blank

    def first_update(j):
        pair = coupling[j] + coupling[count + j + 1]
        x = jnp.concatenate([xa[j], xb[j + 1]], 0)
        aug[j] = jnp.where(kept, aug[j], 0.0) - dot(six_left_64(pair, lanes), six_rows_64(x))

    for_all(half, first_update)

    offsets = [0]
    base = half
    n = half
    unit_pad = ((lanes == rows) & (rows >= NV)).astype(jnp.float32)
    unit_full = (lanes == rows).astype(jnp.float32)

    def packed(blocks):
        total = None
        for g in range(4):
            if blocks[g] is None:
                d = unit_full if g == 0 else pltpu.roll(unit_full, 32 * g, 1)
            else:
                d = jnp.where(diag_lanes, blocks[g], 0.0)
                d = d if g == 2 else pltpu.roll(d, (32 * g + 64) % 128, 1)
                d = d + (unit_pad if g == 0 else pltpu.roll(unit_pad, 32 * g, 1))
            total = d if total is None else total + d
        return total

    def arranged(a):
        r32, r64 = pltpu.roll(a, 32, 1), pltpu.roll(a, 64, 1)
        right = jnp.where(rhs_lane, a, 0.0)
        ba = jnp.where(below_32, a, jnp.where(diag_lanes, r32, right))
        bb = jnp.where(below_64 & ~below_32, a, jnp.where(diag_lanes, r64, right))
        return jnp.concatenate([ba, bb], 1)

    while n > 1:
        half = n // 2
        offsets.append(base)
        packs = (half + 3) // 4
        sets = [[aug[2 * (4 * s + g)] if 4 * s + g < half else None for g in range(4)] for s in range(packs)]
        inverses = (invert_packed if packs < 4 else invert_many)([packed(b) for b in sets])
        for s in range(packs):
            for g in range(min(4, half)):
                left = six_left(take(inverses[s], 32 * g + inner), lanes)
                x = dot(left, six_rows(arranged(sets[s][g])))
                xa[base + 4 * s + g] = x[:, :128]
                xb[base + 4 * s + g] = x[:, 128:]
        xb[base + half] = blank
        for j in range(half):
            a = aug[2 * j + 1]
            pair = jnp.where(below_64, a, pltpu.roll(a, 64, 1))
            x = jnp.concatenate([xa[base + j], xb[base + j + 1]], 0)
            aug[j] = jnp.where(kept, a, 0.0) - dot(six_left_64(pair, lanes), six_rows_64(x))
        base += half
        n = half

    row_id = iota((8, 128), 0)
    lane8 = iota((8, 128), 1)
    unit = (lane8 == 64 + NV).astype(jnp.float32)
    last = aug[0]
    (inverse,) = invert_packed([packed([last, None, None, None])])
    root = jnp.sum(take(last, jnp.full((32, 128), 64 + NV, jnp.int32)) * inverse, 0, keepdims=True)
    root = jnp.where(lane8 < 32, jnp.broadcast_to(root, (8, 128)), 0.0)
    pos = place_ref[0]
    zero = jnp.zeros((8, 128), jnp.float32)
    window = [zero, root, zero]
    for depth in reversed(range(len(offsets))):
        half = count >> (depth + 1)
        here = pos >> depth
        c = here >> 1
        if half > 1:
            start = jnp.minimum(c, half - 2)
            x2 = xa[pl.ds(offsets[depth] + start, 2)].reshape(64, 128)
            va = unit - window[0] - pltpu.roll(window[1], 64, 1)
            vb = unit - window[1] - pltpu.roll(window[2], 64, 1)
            v = jnp.where(row_id == 0, va, vb)
            y = lax.dot_general(v, x2, NT, precision=precise, preferred_element_type=jnp.float32)
            y = jnp.concatenate([y, jnp.zeros((8, 64), jnp.float32)], 1)
            lo = jnp.where(lane8 < 32, y, 0.0)
            hi = jnp.where(lane8 < 32, pltpu.roll(y, 96, 1), 0.0)
            ea = jnp.where(c == start, lo[0:1], hi[0:1])
            eb = jnp.where(c == start, hi[1:2], zero[1:2])
        else:
            va = unit - pltpu.roll(window[1], 64, 1)
            y = lax.dot_general(va, xa[offsets[depth]], NT, precision=precise, preferred_element_type=jnp.float32)
            y = jnp.concatenate([y, jnp.zeros((8, 96), jnp.float32)], 1)
            ea, eb = y[0:1], zero[0:1]
        ea = jnp.broadcast_to(ea, (8, 128))
        eb = jnp.broadcast_to(eb, (8, 128))
        odd = (here & 1) == 1
        window = [
            jnp.where(odd, ea, window[0]),
            jnp.where(odd, window[1], ea),
            jnp.where(odd, eb, window[1]),
        ]
    coeff_ref[...] = window[1][0:1, :NV]
    finish(place_ref, window, z_ref, k_ref, st_ref, rs_ref, a_ref, b_ref, g_ref, out_ref)


def finish(place_ref, window, z_ref, k_ref, st_ref, rs_ref, a_ref, b_ref, g_ref, out_ref):
    vectors, nx, ny = z_ref.shape
    own, owners = place_ref[1], g_ref.shape[0]
    lane8 = iota((8, 128), 1)
    mine = window[1]
    weights = [take(mine, jnp.full((8, 128), v, jnp.int32)) for v in range(vectors)]
    field = None
    for v in range(vectors):
        w = weights[v]
        w = jnp.concatenate([jnp.concatenate([w] * (ny // 128), 1)] * (nx // 8), 0)
        term = w * z_ref[v]
        field = term if field is None else field + term
    k = k_ref[...]

    def in_row(row, block):
        return jnp.dot(row[:, :32], block, precision=precise, preferred_element_type=jnp.float32)

    body = iota((32, ny), 0) < NV
    up, down = neighbours(place_ref, a_ref, b_ref)
    f_up = in_row(window[0], jnp.where(body, up, 0.0))[0:1]
    f_down = in_row(window[2], jnp.where(body, down, 0.0))[0:1]
    k_up, k_down = up[NV : NV + 1], down[NV : NV + 1]

    def beside(o, side, there):
        block = g_ref[o, 16:48, :]
        f_row = in_row(mine, jnp.where(iota((32, 128), 0) < NV, block, 0.0))
        f_row = jnp.where(there, jnp.broadcast_to(f_row[0:1], (8, 128)), 0.0)
        k_row = jnp.where(there, jnp.broadcast_to(block[NV : NV + 1], (8, 128)), 0.0)
        f_col, k_col = [], []
        for g in range(nx // 8):
            at = lane8 == 16 * iota((8, 128), 0) + 8 * side + g
            f_col.append(jnp.sum(jnp.where(at, f_row, 0.0), 1, keepdims=True))
            k_col.append(jnp.sum(jnp.where(at, k_row, 0.0), 1, keepdims=True))
        return jnp.concatenate(f_col, 0), jnp.concatenate(k_col, 0)

    f_left, k_left = beside(jnp.maximum(own - 1, 0), 1, own > 0)
    f_right, k_right = beside(jnp.minimum(own + 1, owners - 1), 0, own < owners - 1)
    row, lane = iota((nx, ny), 0), iota((nx, ny), 1)
    east, west, north, south = row == nx - 1, row == 0, lane == ny - 1, lane == 0

    def flow(shift, axis, edge, f_edge, k_edge):
        f_near = jnp.where(edge, f_edge, pltpu.roll(field, shift, axis))
        k_near = jnp.where(edge, k_edge, pltpu.roll(k, shift, axis))
        return transmit(k, k_near) * (field - f_near)

    applied = st_ref[...] * field
    applied = applied + flow(nx - 1, 0, east, f_down, k_down)
    applied = applied + flow(1, 0, west, f_up, k_up)
    applied = applied + flow(ny - 1, 1, north, f_right, k_right)
    applied = applied + flow(1, 1, south, f_left, k_left)
    out_ref[...] = rs_ref[...] - applied


def solve(place, gathered, z, k, st, rs, a, b, g):
    count = gathered.shape[0]
    nx, ny = k.shape
    return pl.pallas_call(
        functools.partial(solve_kernel, count),
        out_shape=[f32(1, NV), f32(nx, ny)],
        in_specs=[SMEM] + [VMEM] * 8,
        out_specs=[VMEM, VMEM],
        scratch_shapes=[pltpu.VMEM((n, 32, 128), jnp.float32) for n in (count // 2, count, count + 1, 2 * count)],
        compiler_params=limit(16),
        name="solve",
    )(place, gathered, z, k, st, rs, a, b, g)


def per_device(deflation, permeability_base, design_mask, storage, right_side):
    subs, owners = lax.axis_size("sub"), lax.axis_size("own")
    place = jnp.stack([lax.axis_index("sub"), lax.axis_index("own")]).astype(jnp.int32)
    k = permeability(permeability_base, design_mask)
    edge = edges(deflation, k)
    swaps = [(i, i ^ 1) for i in range(subs) if i ^ 1 < subs]
    others = [(i, i + 1 if i % 2 else i - 1) for i in range(1, subs) if i % 2 == 0 or i + 1 < subs]
    a = lax.ppermute(edge, "sub", swaps)
    b = lax.ppermute(edge, "sub", others)
    p, c = assemble(deflation, k, storage, right_side)
    share = rim(place, edge, a, b, p, c, owners)
    g = lax.all_to_all(share, "own", 0, 0)
    gathered = lax.all_to_all(total(place, g, subs), "sub", 0, 0)
    return tuple(solve(place, gathered, deflation, k, storage, right_side, a, b, g))


def solution(mesh):
    fields = P("sub", "own")
    return jax.shard_map(
        per_device,
        mesh=mesh,
        in_specs=(P(None, "sub", "own"), fields, fields, fields, fields),
        out_specs=(P("sub", None), fields),
        check_vma=False,
    )
```

```python
import functools
import math

import jax
import jax.numpy as jnp
from jax import lax
from jax.experimental import pallas as pl
from jax.experimental.pallas import tpu as pltpu
from jax.sharding import PartitionSpec as P

LOG_CONTRAST = math.log(1000.0)
precise = lax.Precision.HIGHEST
NV = 30
NT = (((1,), (1,)), ((), ()))
VMEM = pl.BlockSpec(memory_space=pltpu.VMEM)
SMEM = pl.BlockSpec(memory_space=pltpu.SMEM)


def f32(*shape):
    return jax.ShapeDtypeStruct(shape, jnp.float32)


def limit(mib):
    return pltpu.CompilerParams(vmem_limit_bytes=mib * 1024 * 1024)


def iota(shape, dim):
    return lax.broadcasted_iota(jnp.int32, shape, dim)


def permeability(base, mask):
    return base * jnp.exp((mask.astype(jnp.float32) - 1.0) * LOG_CONTRAST)


def transmit(centre, beside):
    return 2.0 * centre * beside / (centre + beside)


def split_parts(x):
    high = x.astype(jnp.bfloat16)
    rest = x - high.astype(jnp.float32)
    middle = rest.astype(jnp.bfloat16)
    low = (rest - middle.astype(jnp.float32)).astype(jnp.bfloat16)
    return high, middle, low


def edges_kernel(z_ref, k_ref, out_ref):
    vectors, nx, ny = z_ref.shape
    pad = jnp.zeros((31 - vectors, ny), jnp.float32)
    for row, at in ((0, 0), (nx - 1, 32)):
        rows = [z_ref[v, row : row + 1, :] for v in range(vectors)]
        out_ref[at : at + 32, :] = jnp.concatenate(rows + [k_ref[row : row + 1, :], pad], 0)


def edges(z, k):
    return pl.pallas_call(
        edges_kernel,
        out_shape=f32(64, k.shape[1]),
        in_specs=[VMEM, VMEM],
        out_specs=VMEM,
        compiler_params=limit(4),
        name="edges",
    )(z, k)


def neighbours(place_ref, a_ref, b_ref):
    odd = (place_ref[0] & 1) == 1
    up = jnp.where(odd, a_ref[32:, :], b_ref[32:, :])
    down = jnp.where(odd, b_ref[:32, :], a_ref[:32, :])
    return up, down


def assemble_kernel(z_ref, k_ref, st_ref, rs_ref, p_ref, c_ref, az_ref):
    vectors, nx, ny = z_ref.shape
    k = k_ref[...]
    st = st_ref[...]
    row, lane = iota((nx, ny), 0), iota((nx, ny), 1)
    tn = jnp.where(lane == ny - 1, 0.0, transmit(k, pltpu.roll(k, ny - 1, 1)))
    te = jnp.where(row == nx - 1, 0.0, transmit(k, pltpu.roll(k, nx - 1, 0)))

    groups = nx // 8
    pick_n, pick_c = iota((128, ny), 0), iota((128, ny), 1)
    edge_lane = jnp.where(((pick_n >> 3) & 1) == 0, 0, ny - 1)
    ts = pltpu.roll(tn, 1, 1)
    tw = pltpu.roll(te, 1, 0)
    last_row, first_row = iota((8, ny), 0) == 7, iota((8, ny), 0) == 0
    gram, columns = None, None
    for g in range(groups):
        at = slice(8 * g, 8 * g + 8)
        tn_g, ts_g, te_g, tw_g, st_g = tn[at], ts[at], te[at], tw[at], st[at]
        for v in range(vectors):
            z = z_ref[v, at, :]
            east = pltpu.roll(z, 7, 0)
            if g + 1 < groups:
                east = jnp.where(last_row, z_ref[v, 8 * g + 8 : 8 * g + 9, :], east)
            west = pltpu.roll(z, 1, 0)
            if g > 0:
                west = jnp.where(first_row, z_ref[v, 8 * g - 1 : 8 * g, :], west)
            near = tn_g * (z - pltpu.roll(z, ny - 1, 1)) + ts_g * (z - pltpu.roll(z, 1, 1))
            az_ref[g % 2, v] = (st_g * z + te_g * (z - east)) + (tw_g * (z - west) + near)
        az_ref[g % 2, vectors] = rs_ref[at, :]
        az_ref[g % 2, vectors + 1] = jnp.zeros((8, ny), jnp.float32)
        zg = jnp.concatenate([z_ref[:, at, :].reshape(8 * vectors, ny), k[at], jnp.zeros((8, ny), jnp.float32)], 0)
        ag = az_ref[g % 2].reshape(8 * (vectors + 2), ny)
        zh, zm, zl = split_parts(zg)
        ah, am, al = split_parts(ag)
        left = jnp.concatenate([zh, zh, zm, zm, zh, zl], 1)
        right = jnp.concatenate([ah, am, ah, am, al, ah], 1)
        part = lax.dot_general(left, right, NT, preferred_element_type=jnp.float32)
        pick = ((pick_n & 7) == g) & (pick_c == edge_lane)
        pick = pick.astype(jnp.float32).astype(jnp.bfloat16)
        col = lax.dot_general(
            jnp.concatenate([zh, zm, zl], 1), jnp.concatenate([pick] * 3, 1), NT, preferred_element_type=jnp.float32
        )
        gram = part if gram is None else gram + part
        columns = col if columns is None else columns + col
    size = 8 * (vectors + 2)
    same = (iota((size, size), 0) & 7) == (iota((size, size), 1) & 7)
    gram = jnp.where(same, gram, 0.0)
    columns = jnp.where((iota((size, 128), 0) & 7) == (iota((size, 128), 1) >> 4), columns, 0.0)
    fold = (iota((32, size), 0) == (iota((32, size), 1) >> 3)).astype(jnp.float32)
    unfold = (iota((size, 128), 1) == (iota((size, 128), 0) >> 3)).astype(jnp.float32)
    folded = jnp.dot(fold, jnp.concatenate([gram, columns], 1), precision=precise, preferred_element_type=jnp.float32)
    p = jnp.dot(folded[:, :size], unfold, precision=precise, preferred_element_type=jnp.float32)
    p_ref[...] = jnp.where(iota((32, 128), 0) < vectors, p, 0.0)
    c_ref[...] = folded[:, size:]


def assemble(z, k, st, rs):
    vectors, nx, ny = z.shape
    return pl.pallas_call(
        assemble_kernel,
        out_shape=[f32(32, 128), f32(32, 128)],
        in_specs=[VMEM] * 4,
        out_specs=[VMEM, VMEM],
        scratch_shapes=[pltpu.VMEM((2, vectors + 2, 8, ny), jnp.float32)],
        compiler_params=limit(16),
        cost_estimate=pl.CostEstimate(flops=6 * 2 * 256 * 256 * 256 * 8, bytes_accessed=2 * 1024 * 1024, transcendentals=0),
        name="assemble",
    )(z, k, st, rs)


def pack(tile):
    lane = iota((16, 128), 1)
    return jnp.where(lane < 64, tile[:16], pltpu.roll(tile[16:], 64, 1))


def rim_kernel(place_ref, edge_ref, a_ref, b_ref, p_ref, c_ref, out_ref):
    ny = edge_ref.shape[1]
    body = iota((32, ny), 0) < NV
    up, down = neighbours(place_ref, a_ref, b_ref)
    tw = transmit(edge_ref[NV : NV + 1, :], up[NV : NV + 1])
    te = transmit(edge_ref[32 + NV : 33 + NV, :], down[NV : NV + 1])
    first = jnp.where(body, edge_ref[:32, :], 0.0)
    last = jnp.where(body, edge_ref[32:, :], 0.0)
    above = jnp.where(body, up, 0.0)
    blank = jnp.zeros((32, ny), jnp.float32)
    left = jnp.concatenate([first * tw, last * te], 1)
    right = jnp.concatenate(
        [jnp.concatenate([first, last], 1), jnp.concatenate([-above, blank], 1), jnp.zeros((64, 2 * ny), jnp.float32)], 0
    )
    both = lax.dot_general(left, right, NT, precision=precise, preferred_element_type=jnp.float32)
    share = jnp.concatenate([pack(p_ref[...] + both), c_ref[...]], 0)
    for o in range(out_ref.shape[0]):
        out_ref[o] = share


def rim(place, edge, a, b, p, c, copies):
    return pl.pallas_call(
        rim_kernel,
        out_shape=f32(copies, 48, 128),
        in_specs=[SMEM] + [VMEM] * 5,
        out_specs=VMEM,
        compiler_params=limit(4),
        name="rim",
    )(place, edge, a, b, p, c)


def total_kernel(place_ref, g_ref, out_ref):
    count = g_ref.shape[0]
    tile = g_ref[0, :16, :]
    for o in range(1, count):
        tile = tile + g_ref[o, :16, :]
    lane, row = iota((32, 128), 1), iota((32, 128), 0)
    used = (((lane >> 3) & 1) == 0) & (row < NV)
    steps, flows = [], []
    for o in range(count - 1):
        here = pltpu.roll(g_ref[o, 16:48, :], 120, 1)
        there = g_ref[o + 1, 16:48, :]
        t = transmit(here[NV : NV + 1], there[NV : NV + 1])
        step = jnp.where(used, there - here, 0.0)
        steps.append(step)
        flows.append(jnp.where(used, t * step, 0.0))
    tile = jnp.concatenate([tile, pltpu.roll(tile, 64, 1)], 0)
    if steps:
        right = jnp.concatenate([jnp.concatenate(steps, 1), jnp.zeros((96, 128 * len(steps)), jnp.float32)], 0)
        faces = lax.dot_general(
            jnp.concatenate(flows, 1), right, NT, precision=precise, preferred_element_type=jnp.float32
        )
        tile = tile + faces
    diag, inner = lane < NV, lane & 31
    (inverse,) = invert_packed([jnp.where(diag, tile, 0.0) + jnp.where((lane >= NV) & (inner == row), 1.0, 0.0)])
    right_side = jnp.sum(jnp.where(lane == NV, tile, 0.0), 1, keepdims=True)
    right_row = jnp.sum(jnp.where(lane == row, jnp.broadcast_to(right_side, (32, 128)), 0.0), 0, keepdims=True)
    even_diag = jnp.where(row < NV, inverse, 0.0)
    before = pltpu.roll(tile, 96, 1)[:, :32]
    back = jnp.concatenate([jnp.transpose(before), jnp.zeros((32, 96), jnp.float32)], 1)
    back = jnp.where(row == NV, jnp.broadcast_to(right_row, (32, 128)), back)
    even = jnp.where(lane < 32, back, jnp.where(lane < 32 + NV, pltpu.roll(even_diag, 32, 1), 0.0))
    odd = jnp.where(lane < 32, pltpu.roll(tile, 96, 1), jnp.where(lane < 64, pltpu.roll(tile, 32, 1), 0.0))
    both = jnp.where((place_ref[0] & 1) == 0, even, odd)
    top, bottom = both[:16], both[16:]
    half = iota((16, 128), 1)
    packed = jnp.where(
        half < 32,
        top,
        jnp.where(half < 64, pltpu.roll(bottom, 32, 1), jnp.where(half < 96, pltpu.roll(top, 32, 1), pltpu.roll(bottom, 64, 1))),
    )
    share = jnp.where((place_ref[1] & 1) == 0, packed[:8], packed[8:])
    for s in range(out_ref.shape[0]):
        out_ref[s] = share


def total(place, g, copies):
    return pl.pallas_call(
        total_kernel,
        out_shape=f32(copies, 8, 128),
        in_specs=[SMEM, VMEM],
        out_specs=VMEM,
        compiler_params=limit(4),
        name="total",
    )(place, g)


def small_inverse(p):
    a00, a01, a11 = p[0, 0], p[0, 1], p[1, 1]
    b02, b03, b12, b13 = p[0, 2], p[0, 3], p[1, 2], p[1, 3]
    ia = 1.0 / (a00 * a11 - a01 * a01)
    h00, h01, h11 = a11 * ia, a01 * ia, a00 * ia
    w02, w03 = h00 * b02 - h01 * b12, h00 * b03 - h01 * b13
    w12, w13 = h11 * b12 - h01 * b02, h11 * b13 - h01 * b03
    s22 = p[2, 2] - (b02 * w02 + b12 * w12)
    s23 = p[2, 3] - (b02 * w03 + b12 * w13)
    s33 = p[3, 3] - (b03 * w03 + b13 * w13)
    iz = 1.0 / (s22 * s33 - s23 * s23)
    i22, i23, i33 = s33 * iz, -(s23 * iz), s22 * iz
    i02, i03 = -(w02 * i22 + w03 * i23), -(w02 * i23 + w03 * i33)
    i12, i13 = -(w12 * i22 + w13 * i23), -(w12 * i23 + w13 * i33)
    i00 = h00 - (w02 * i02 + w03 * i03)
    i01 = -h01 - (w02 * i12 + w03 * i13)
    i11 = h11 - (w12 * i12 + w13 * i13)
    return [[i00, i01, i02, i03], [i01, i11, i12, i13], [i02, i12, i22, i23], [i03, i13, i23, i33]]


def take(x, index):
    return jnp.take_along_axis(x, index, axis=1)


def spread_row(x, row):
    return jnp.broadcast_to(x[row : row + 1], (8, 128))


def invert_packed(arrays):
    lanes = iota((8, 128), 1)
    rows = iota((8, 128), 0)
    start, inner = lanes & ~31, lanes & 31
    states = []
    for a in arrays:
        tiles = [a[8 * t : 8 * t + 8] for t in range(4)]
        c = [take(tiles[0], start + b) for b in range(4)]
        states.append((tiles, {(i, j): spread_row(c[j], i) for i in range(4) for j in range(i, 4)}))
    for k in range(0, 32, 4):
        index = [start + (k + b) for b in range(4)]
        inside = (inner >= k) & (inner < k + 4)
        tile, q = k // 8, k % 8
        out = []
        for tiles, p in states:
            inv = small_inverse(p)
            cols = [[take(tiles[t], index[b]) for b in range(4)] for t in range(4)]
            pivot = None
            if k < 28:
                t2, q2 = (k + 4) // 8, (k + 4) % 8
                own = [take(tiles[t2], start + (k + 4 + b)) for b in range(4)]
                cross = [[spread_row(cols[t2][b], q2 + i) for b in range(4)] for i in range(4)]
                scaled = [
                    [
                        (inv[b][0] * cross[i][0] + inv[b][1] * cross[i][1])
                        + (inv[b][2] * cross[i][2] + inv[b][3] * cross[i][3])
                        for b in range(4)
                    ]
                    for i in range(4)
                ]
                pivot = {}
                for i in range(4):
                    for j in range(i, 4):
                        change = (cross[i][0] * scaled[j][0] + cross[i][1] * scaled[j][1]) + (
                            cross[i][2] * scaled[j][2] + cross[i][3] * scaled[j][3]
                        )
                        pivot[i, j] = spread_row(own[j], q2 + i) - change
            rhat = [jnp.where(inside, (inner == k + b).astype(jnp.float32), spread_row(tiles[tile], q + b)) for b in range(4)]
            new_rows = [
                (inv[i][0] * rhat[0] + inv[i][1] * rhat[1]) + (inv[i][2] * rhat[2] + inv[i][3] * rhat[3])
                for i in range(4)
            ]
            fresh = []
            for t in range(4):
                c = cols[t]
                v = jnp.where(inside, 0.0, tiles[t])
                v = v - ((c[0] * new_rows[0] + c[1] * new_rows[1]) + (c[2] * new_rows[2] + c[3] * new_rows[3]))
                if t == tile:
                    for b in range(4):
                        v = jnp.where(rows == q + b, new_rows[b], v)
                fresh.append(v)
            out.append((fresh, pivot))
        states = out
    return [jnp.concatenate(tiles, 0) for tiles, _ in states]


def invert_many(arrays):
    lanes = iota((8, 128), 1)
    rows = iota((8, 128), 0)
    start, inner = lanes & ~31, lanes & 31
    for k in range(0, 32, 4):
        index = [start + (k + b) for b in range(4)]
        inside = (inner >= k) & (inner < k + 4)
        tile = k // 8
        out = []
        for a in arrays:
            tiles = [a[8 * t : 8 * t + 8] for t in range(4)]
            r = [jnp.broadcast_to(a[k + b : k + b + 1], (8, 128)) for b in range(4)]
            cols = [[take(tiles[t], index[b]) for b in range(4)] for t in range(4)]
            q = k % 8
            p = {
                (i, j): spread_row(cols[tile][j], q + i) for i in range(4) for j in range(i, 4)
            }
            inv = small_inverse(p)
            rhat = [jnp.where(inside, (inner == k + b).astype(jnp.float32), r[b]) for b in range(4)]
            new_rows = [
                (inv[i][0] * rhat[0] + inv[i][1] * rhat[1]) + (inv[i][2] * rhat[2] + inv[i][3] * rhat[3])
                for i in range(4)
            ]
            fresh = []
            for t in range(4):
                c = cols[t]
                v = jnp.where(inside, 0.0, tiles[t])
                v = v - ((c[0] * new_rows[0] + c[1] * new_rows[1]) + (c[2] * new_rows[2] + c[3] * new_rows[3]))
                if t == tile:
                    for b in range(4):
                        v = jnp.where(rows == (k + b) % 8, new_rows[b], v)
                fresh.append(v)
            out.append(jnp.concatenate(fresh, 0))
        arrays = out
    return arrays


def three(x):
    high = x.astype(jnp.bfloat16).astype(jnp.float32)
    rest = x - high
    middle = rest.astype(jnp.bfloat16).astype(jnp.float32)
    return high, middle, rest - middle


def narrow(*parts):
    return jnp.concatenate([p.astype(jnp.bfloat16) for p in parts], 1)


def six_left(x, lanes):
    h, m, l = three(x)
    return narrow(jnp.where(lanes < 96, h, m), jnp.where(lanes < 32, m, l)[:, :64])


def six_right(x, lanes):
    h, m, l = three(x)
    one = jnp.where(lanes < 32, h, jnp.where(lanes < 64, m, jnp.where(lanes < 96, l, h)))
    return narrow(one, jnp.where(lanes < 32, m, h)[:, :64])


def six_rows(x):
    h, m, l = (p.astype(jnp.bfloat16) for p in three(x))
    return jnp.concatenate([h, m, l, h, m, h], 0)


def six_left_64(x, lanes):
    h, m, l = three(x)
    return narrow(h, jnp.where(lanes < 64, h, m), jnp.where(lanes < 64, m, l))


def six_rows_64(x):
    h, m, l = (p.astype(jnp.bfloat16) for p in three(x))
    return jnp.concatenate([h, m, l, h, m, h], 0)


def solve_kernel(
    count,
    place_ref,
    mine_ref,
    other_ref,
    z_ref,
    k_ref,
    st_ref,
    rs_ref,
    a_ref,
    b_ref,
    g_ref,
    coeff_ref,
    out_ref,
    aug,
    xa,
    xb,
    coupling,
):
    lanes = iota((32, 128), 1)
    rows = iota((32, 128), 0)
    inner = lanes & 31
    blank = jnp.zeros((32, 128), jnp.float32)
    body = rows < NV
    diag_lanes = (lanes >= 64) & (lanes < 64 + NV)
    rhs_lane = lanes == 64 + NV
    kept = diag_lanes | rhs_lane
    below_32, below_64 = lanes < 32, lanes < 64
    flat = (((1,), (0,)), ((), ()))

    def dot(a, b, dims=flat):
        return lax.dot_general(a, b, dims, preferred_element_type=jnp.float32)

    def for_all(total, body_fn, width=32):
        if total <= width:
            for i in range(total):
                body_fn(i)
        else:

            def step(t, _):
                for i in range(width):
                    body_fn(t * width + i)
                return 0

            lax.fori_loop(0, total // width, step, 0)

    half = count // 2
    inner16 = iota((16, 128), 1) & 31

    def pick(t, top, bottom):
        return jnp.concatenate([take(t, top + inner16), take(t, bottom + inner16)], 0)

    second_64 = (lanes & 32) != 0
    back_rows = second_64 & body

    first_core = (place_ref[1] & 1) == 0

    def block(m):
        mine, other = mine_ref[m], other_ref[m]
        return jnp.concatenate([jnp.where(first_core, mine, other), jnp.where(first_core, other, mine)], 0)

    def first_spread(j):
        even, odd = block(2 * j), block(2 * j + 1)
        inverse = pick(even, 64, 96)
        back = pick(even, 0, 32)
        ahead = pick(odd, 0, 32)
        left = six_left(inverse, lanes)
        tb = six_right(back, lanes)
        ta = six_right(jnp.where(rows == NV, jnp.broadcast_to(back[NV : NV + 1], (32, 128)), ahead), lanes)
        zero = jnp.zeros((32, 192), jnp.bfloat16)
        x = dot(left, jnp.concatenate([tb, zero, ta, zero, zero, ta, tb, zero], 0), NT)
        xa[j] = x[:, :128]
        xb[j] = x[:, 128:]
        aug[j] = jnp.concatenate([odd, pltpu.roll(odd, 96, 1)], 0)
        coupling[j] = jnp.where(second_64, 0.0, ahead)
        coupling[count + j] = jnp.where(back_rows, back, 0.0)

    for_all(half, first_spread)
    xb[half] = blank
    coupling[count + half] = blank

    def first_update(j):
        pair = coupling[j] + coupling[count + j + 1]
        x = jnp.concatenate([xa[j], xb[j + 1]], 0)
        aug[j] = jnp.where(kept, aug[j], 0.0) - dot(six_left_64(pair, lanes), six_rows_64(x))

    for_all(half, first_update)

    offsets = [0]
    base = half
    n = half
    unit_pad = ((lanes == rows) & (rows >= NV)).astype(jnp.float32)
    unit_full = (lanes == rows).astype(jnp.float32)

    def packed(blocks):
        total = None
        for g in range(4):
            if blocks[g] is None:
                d = unit_full if g == 0 else pltpu.roll(unit_full, 32 * g, 1)
            else:
                d = jnp.where(diag_lanes, blocks[g], 0.0)
                d = d if g == 2 else pltpu.roll(d, (32 * g + 64) % 128, 1)
                d = d + (unit_pad if g == 0 else pltpu.roll(unit_pad, 32 * g, 1))
            total = d if total is None else total + d
        return total

    def arranged(a):
        r32, r64 = pltpu.roll(a, 32, 1), pltpu.roll(a, 64, 1)
        right = jnp.where(rhs_lane, a, 0.0)
        ba = jnp.where(below_32, a, jnp.where(diag_lanes, r32, right))
        bb = jnp.where(below_64 & ~below_32, a, jnp.where(diag_lanes, r64, right))
        return jnp.concatenate([ba, bb], 1)

    while n > 1:
        half = n // 2
        offsets.append(base)
        packs = (half + 3) // 4
        sets = [[aug[2 * (4 * s + g)] if 4 * s + g < half else None for g in range(4)] for s in range(packs)]
        inverses = (invert_packed if packs < 4 else invert_many)([packed(b) for b in sets])
        for s in range(packs):
            for g in range(min(4, half)):
                left = six_left(take(inverses[s], 32 * g + inner), lanes)
                x = dot(left, six_rows(arranged(sets[s][g])))
                xa[base + 4 * s + g] = x[:, :128]
                xb[base + 4 * s + g] = x[:, 128:]
        xb[base + half] = blank
        for j in range(half):
            a = aug[2 * j + 1]
            pair = jnp.where(below_64, a, pltpu.roll(a, 64, 1))
            x = jnp.concatenate([xa[base + j], xb[base + j + 1]], 0)
            aug[j] = jnp.where(kept, a, 0.0) - dot(six_left_64(pair, lanes), six_rows_64(x))
        base += half
        n = half

    row_id = iota((8, 128), 0)
    lane8 = iota((8, 128), 1)
    unit = (lane8 == 64 + NV).astype(jnp.float32)
    last = aug[0]
    (inverse,) = invert_packed([packed([last, None, None, None])])
    root = jnp.sum(take(last, jnp.full((32, 128), 64 + NV, jnp.int32)) * inverse, 0, keepdims=True)
    root = jnp.where(lane8 < 32, jnp.broadcast_to(root, (8, 128)), 0.0)
    pos = place_ref[0]
    zero = jnp.zeros((8, 128), jnp.float32)
    window = [zero, root, zero]
    for depth in reversed(range(len(offsets))):
        half = count >> (depth + 1)
        here = pos >> depth
        c = here >> 1
        if half > 1:
            start = jnp.minimum(c, half - 2)
            x2 = xa[pl.ds(offsets[depth] + start, 2)].reshape(64, 128)
            va = unit - window[0] - pltpu.roll(window[1], 64, 1)
            vb = unit - window[1] - pltpu.roll(window[2], 64, 1)
            v = jnp.where(row_id == 0, va, vb)
            y = lax.dot_general(v, x2, NT, precision=precise, preferred_element_type=jnp.float32)
            y = jnp.concatenate([y, jnp.zeros((8, 64), jnp.float32)], 1)
            lo = jnp.where(lane8 < 32, y, 0.0)
            hi = jnp.where(lane8 < 32, pltpu.roll(y, 96, 1), 0.0)
            ea = jnp.where(c == start, lo[0:1], hi[0:1])
            eb = jnp.where(c == start, hi[1:2], zero[1:2])
        else:
            va = unit - pltpu.roll(window[1], 64, 1)
            y = lax.dot_general(va, xa[offsets[depth]], NT, precision=precise, preferred_element_type=jnp.float32)
            y = jnp.concatenate([y, jnp.zeros((8, 96), jnp.float32)], 1)
            ea, eb = y[0:1], zero[0:1]
        ea = jnp.broadcast_to(ea, (8, 128))
        eb = jnp.broadcast_to(eb, (8, 128))
        odd = (here & 1) == 1
        window = [
            jnp.where(odd, ea, window[0]),
            jnp.where(odd, window[1], ea),
            jnp.where(odd, eb, window[1]),
        ]
    coeff_ref[...] = window[1][0:1, :NV]
    finish(place_ref, window, z_ref, k_ref, st_ref, rs_ref, a_ref, b_ref, g_ref, out_ref)


def finish(place_ref, window, z_ref, k_ref, st_ref, rs_ref, a_ref, b_ref, g_ref, out_ref):
    vectors, nx, ny = z_ref.shape
    own, owners = place_ref[1], g_ref.shape[0]
    lane8 = iota((8, 128), 1)
    mine = window[1]
    weights = [take(mine, jnp.full((8, 128), v, jnp.int32)) for v in range(vectors)]
    field = None
    for v in range(vectors):
        w = weights[v]
        w = jnp.concatenate([jnp.concatenate([w] * (ny // 128), 1)] * (nx // 8), 0)
        term = w * z_ref[v]
        field = term if field is None else field + term
    k = k_ref[...]

    def in_row(row, block):
        return jnp.dot(row[:, :32], block, precision=precise, preferred_element_type=jnp.float32)

    body = iota((32, ny), 0) < NV
    up, down = neighbours(place_ref, a_ref, b_ref)
    f_up = in_row(window[0], jnp.where(body, up, 0.0))[0:1]
    f_down = in_row(window[2], jnp.where(body, down, 0.0))[0:1]
    k_up, k_down = up[NV : NV + 1], down[NV : NV + 1]

    def beside(o, side, there):
        block = g_ref[o, 16:48, :]
        f_row = in_row(mine, jnp.where(iota((32, 128), 0) < NV, block, 0.0))
        f_row = jnp.where(there, jnp.broadcast_to(f_row[0:1], (8, 128)), 0.0)
        k_row = jnp.where(there, jnp.broadcast_to(block[NV : NV + 1], (8, 128)), 0.0)
        f_col, k_col = [], []
        for g in range(nx // 8):
            at = lane8 == 16 * iota((8, 128), 0) + 8 * side + g
            f_col.append(jnp.sum(jnp.where(at, f_row, 0.0), 1, keepdims=True))
            k_col.append(jnp.sum(jnp.where(at, k_row, 0.0), 1, keepdims=True))
        return jnp.concatenate(f_col, 0), jnp.concatenate(k_col, 0)

    f_left, k_left = beside(jnp.maximum(own - 1, 0), 1, own > 0)
    f_right, k_right = beside(jnp.minimum(own + 1, owners - 1), 0, own < owners - 1)
    row, lane = iota((nx, ny), 0), iota((nx, ny), 1)
    east, west, north, south = row == nx - 1, row == 0, lane == ny - 1, lane == 0

    def flow(shift, axis, edge, f_edge, k_edge):
        f_near = jnp.where(edge, f_edge, pltpu.roll(field, shift, axis))
        k_near = jnp.where(edge, k_edge, pltpu.roll(k, shift, axis))
        return transmit(k, k_near) * (field - f_near)

    applied = st_ref[...] * field
    applied = applied + flow(nx - 1, 0, east, f_down, k_down)
    applied = applied + flow(1, 0, west, f_up, k_up)
    applied = applied + flow(ny - 1, 1, north, f_right, k_right)
    applied = applied + flow(1, 1, south, f_left, k_left)
    out_ref[...] = rs_ref[...] - applied


def solve(place, mine, other, z, k, st, rs, a, b, g):
    count = mine.shape[0]
    nx, ny = k.shape
    return pl.pallas_call(
        functools.partial(solve_kernel, count),
        out_shape=[f32(1, NV), f32(nx, ny)],
        in_specs=[SMEM] + [VMEM] * 9,
        out_specs=[VMEM, VMEM],
        scratch_shapes=[pltpu.VMEM((n, 32, 128), jnp.float32) for n in (count // 2, count, count + 1, 2 * count)],
        compiler_params=limit(16),
        name="solve",
    )(place, mine, other, z, k, st, rs, a, b, g)


def per_device(deflation, permeability_base, design_mask, storage, right_side):
    subs, owners = lax.axis_size("sub"), lax.axis_size("own")
    place = jnp.stack([lax.axis_index("sub"), lax.axis_index("own")]).astype(jnp.int32)
    k = permeability(permeability_base, design_mask)
    edge = edges(deflation, k)
    swaps = [(i, i ^ 1) for i in range(subs) if i ^ 1 < subs]
    others = [(i, i + 1 if i % 2 else i - 1) for i in range(1, subs) if i % 2 == 0 or i + 1 < subs]
    a = lax.ppermute(edge, "sub", swaps)
    b = lax.ppermute(edge, "sub", others)
    p, c = assemble(deflation, k, storage, right_side)
    share = rim(place, edge, a, b, p, c, owners)
    g = lax.all_to_all(share, "own", 0, 0)
    mine = lax.all_to_all(total(place, g, subs), "sub", 0, 0)
    other = lax.ppermute(mine, "own", [(i, i ^ 1) for i in range(owners)])
    return tuple(solve(place, mine, other, deflation, k, storage, right_side, a, b, g))


def solution(mesh):
    fields = P("sub", "own")
    return jax.shard_map(
        per_device,
        mesh=mesh,
        in_specs=(P(None, "sub", "own"), fields, fields, fields, fields),
        out_specs=(P("sub", None), fields),
        check_vma=False,
    )
```
